128 devices in a mesh: rows: 16 (over z_hi, x, core), hash: 8 (over y, z_lo).
Axes of the slice: x: 4, y: 4, z: 4 (z_hi: 2, z_lo: 2; z = z_hi * 2 + z_lo), core: 2. Of those that a mesh axis runs over, the one named last changes fastest.
Arguments:
- tokens: bfloat16 [20480, 768], P('rows'), may hold values from -6 to 6
- item_cuts: int32 [4], replicated, may hold values from 0 to 19968, as said below
- q_codes: int32 [8, 12, 20480], P('hash', None, 'rows'), may hold values from 0 to 255
- k_codes: int32 [8, 12, 20480], P('hash', None, 'rows'), may hold values from 0 to 255
- hyperplanes: float32 [8, 64, 8], P('hash'), may hold values from -1.5 to 1.5
- w_query: bfloat16 [768, 768], replicated, may hold values from -0.21875 to 0.21875
- b_query: float32 [768], replicated, may hold values from -1.5 to 1.5
- w_key: bfloat16 [768, 768], replicated, may hold values from -0.21875 to 0.21875
- b_key: float32 [768], replicated, may hold values from -1.5 to 1.5
- w_value: bfloat16 [768, 768], replicated, may hold values from -0.21875 to 0.21875
- b_value: float32 [768], replicated, may hold values from -1.5 to 1.5
- conv_weight: float32 [12, 65], replicated, may hold values from -0.375 to 0.375
- w_out: bfloat16 [768, 768], replicated, may hold values from -0.4375 to 0.4375
- b_out: float32 [768], replicated, may hold values from -1 to 1
- ln1_gain: float32 [768], replicated, may hold values from 0.5 to 1.5
- ln1_bias: float32 [768], replicated, may hold values from -1 to 1
- w_in: bfloat16 [768, 3072], replicated, may hold values from -0.21875 to 0.21875
- b_in: float32 [3072], replicated, may hold values from -1 to 1
- w_back: bfloat16 [3072, 768], replicated, may hold values from -0.109375 to 0.109375
- b_back: float32 [768], replicated, may hold values from -1 to 1
- ln2_gain: float32 [768], replicated, may hold values from 0.5 to 1.5
- ln2_bias: float32 [768], replicated, may hold values from -1 to 1
- cotangent: float32 [20480, 768], P(('rows', 'hash')), may hold values from -6 to 6
Outputs:
- output: float32 [20480, 768], P(('rows', 'hash'))
- grad_tokens: float32 [20480, 768], P(('rows', 'hash'))
- grad_w_query: float32 [768, 768], replicated
- grad_b_query: float32 [768], replicated
- grad_w_key: float32 [768, 768], replicated
- grad_b_key: float32 [768], replicated
- grad_w_value: float32 [768, 768], replicated
- grad_b_value: float32 [768], replicated
- grad_conv_weight: float32 [12, 65], replicated
- grad_w_out: float32 [768, 768], replicated
- grad_b_out: float32 [768], replicated
- grad_ln1_gain: float32 [768], replicated
- grad_ln1_bias: float32 [768], replicated
- grad_w_in: float32 [768, 3072], replicated
- grad_b_in: float32 [3072], replicated
- grad_w_back: float32 [3072, 768], replicated
- grad_b_back: float32 [768], replicated
- grad_ln2_gain: float32 [768], replicated
- grad_ln2_bias: float32 [768], replicated
The draws below stay inside these ranges and needn't reach their ends.
Inputs may be any that keep to these rules, and one draw needn't show every extreme that they name: item_cuts[0] is 0 and the entries rise; item i holds the positions from item_cuts[i] up to item_cuts[i + 1] (the last item up to 20480); 3 short items hold 512 to 1024 positions each, the last item exactly 512; one long item holds the remaining positions; one or two short items, drawn from the seed, stand before the long one, the first and the last item being short.
All inputs are finite; a program needn't handle non-finite values.
Results may differ from the reference program's by a relative error of at most 0.02.
Values may be sent and summed in bfloat16 or wider, within the bound.
A program may use at most 320 MiB of HBM per device.

```python
import jax
import jax.numpy as jnp
from jax import lax

D = 768
HEADS = 12
FF = 3072
HEAD = 64
TAU = 8
HASHES = 8
CONV_HALF = 32
SHORT_LEN = 512
SHORTS = 3
TOKENS = 20480
ITEMS = 4


def draw_item_cuts(key, part):
    key = jax.random.fold_in(key, 11)
    place_key = jax.random.fold_in(key, 1)
    length_key = jax.random.fold_in(key, 2)
    before = jax.random.randint(place_key, (), 1, SHORTS, dtype=jnp.int32)
    places = jnp.arange(ITEMS, dtype=jnp.int32)
    extra = jax.random.randint(length_key, (ITEMS,), 0, SHORT_LEN + 1, dtype=jnp.int32)
    short_lengths = SHORT_LEN + jnp.where(places == ITEMS - 1, 0, extra).astype(jnp.int32)
    shorts_total = jnp.sum(jnp.where(places == before, 0, short_lengths)).astype(jnp.int32)
    lengths = jnp.where(places == before, TOKENS - shorts_total, short_lengths).astype(jnp.int32)
    ends = jnp.cumsum(lengths).astype(jnp.int32)
    starts = jnp.concatenate([jnp.zeros((1,), jnp.int32), ends[:-1]])
    return starts.astype(jnp.int32)


def plant(result, stream_key, low, top_value):
    longest = result.shape.index(max(result.shape))
    spots = []
    for shift in (0, 1):
        where = [jax.random.randint(jax.random.fold_in(stream_key, axis), (), 0, length) for axis, length in enumerate(result.shape)]
        where[longest] = (where[longest] + shift) % result.shape[longest]
        spots.append(tuple(where))
    return result.at[spots[0]].set(low).at[spots[1]].set(top_value)


def shard_levels(stream_key, extent, shards, least, largest):
    def one(dim, shards_of):
        steps = jax.random.uniform(jax.random.fold_in(jax.random.fold_in(stream_key, 6), dim), (shards_of,), jnp.float32, least / len(shards), largest / len(shards))
        return jnp.repeat(jnp.exp(steps), extent[dim] // shards_of).reshape((-1,) + (1,) * (len(extent) - dim - 1))

    level = one(*shards[0])
    for cut in shards[1:]:
        level = level * one(*cut)
    return level


def noise(stream_key, extent, deviation, most, cuts=(), kind=jnp.bfloat16):
    result = jax.random.normal(stream_key, extent, jnp.float32) * deviation
    if len(cuts) > 0:
        result = shard_levels(stream_key, extent, cuts, -0.22, 0.18) * result
    return jnp.clip(result, min=-most, max=most).astype(kind)


def setup_inputs(seed: int = 0) -> dict:
    key_of = jax.random.split(jax.random.key(seed), 24)
    return {
        "tokens": noise(key_of[0], (TOKENS, D), 1.0, 6.0, ((0, 16),)),
        "item_cuts": draw_item_cuts(jax.random.fold_in(key_of[23], 71), 0),
        "q_codes": plant(jax.random.randint(key_of[2], (HASHES, HEADS, TOKENS), 0, 2 ** TAU), jax.random.fold_in(key_of[2], 1), 0, (2 ** TAU) - 1).astype(jnp.int32),
        "k_codes": plant(jax.random.randint(key_of[3], (HASHES, HEADS, TOKENS), 0, 2 ** TAU), jax.random.fold_in(key_of[3], 1), 0, (2 ** TAU) - 1).astype(jnp.int32),
        "hyperplanes": noise(key_of[4], (HASHES, HEAD, TAU), 0.25, 1.5, ((0, 8),), jnp.float32),
        "w_query": noise(key_of[5], (D, D), D ** -0.5, 0.21875),
        "b_query": noise(key_of[6], (D,), 0.3, 1.5, (), jnp.float32),
        "w_key": noise(key_of[7], (D, D), D ** -0.5, 0.21875),
        "b_key": noise(key_of[8], (D,), 0.3, 1.5, (), jnp.float32),
        "w_value": noise(key_of[9], (D, D), D ** -0.5, 0.21875),
        "b_value": noise(key_of[10], (D,), 0.3, 1.5, (), jnp.float32),
        "conv_weight": noise(key_of[11], (HEADS, 2 * CONV_HALF + 1), (4 * (2 * CONV_HALF + 1)) ** -0.5, 0.375, (), jnp.float32),
        "w_out": noise(key_of[12], (D, D), (D // 4) ** -0.5, 0.4375),
        "b_out": noise(key_of[13], (D,), 0.2, 1.0, (), jnp.float32),
        "ln1_gain": jnp.clip(1.0 + 0.1 * jax.random.normal(key_of[14], (D,), jnp.float32), 0.5, 1.5),
        "ln1_bias": noise(key_of[15], (D,), 0.2, 1.0, (), jnp.float32),
        "w_in": noise(key_of[16], (D, FF), D ** -0.5, 0.21875),
        "b_in": noise(key_of[17], (FF,), 0.2, 1.0, (), jnp.float32),
        "w_back": noise(key_of[18], (FF, D), FF ** -0.5, 0.109375),
        "b_back": noise(key_of[19], (D,), 0.2, 1.0, (), jnp.float32),
        "ln2_gain": jnp.clip(1.0 + 0.1 * jax.random.normal(key_of[20], (D,), jnp.float32), 0.5, 1.5),
        "ln2_bias": noise(key_of[21], (D,), 0.2, 1.0, (), jnp.float32),
        "cotangent": noise(key_of[22], (TOKENS, D), 1.0, 6.0, ((0, 128),), jnp.float32),
    }


@jax.custom_vjp
def low(v):
    return lax.optimization_barrier(v.astype(jnp.bfloat16)).astype(jnp.float32)

@jax.custom_vjp
def low_back(v):
    return v

def low_keep(v):
    return (low(v), None)

def low_pass(kept, grad):
    return (grad,)

def back_keep(v):
    return (v, None)

def back_low(kept, grad):
    return (low(grad),)
low.defvjp(low_keep, low_pass)
low_back.defvjp(back_keep, back_low)
EPS_NORM = 1e-05
EPS_UNIT = 1e-06
HIGHEST = lax.Precision.HIGHEST

def matmul(left, right):
    return jnp.dot(left, right, precision=HIGHEST, preferred_element_type=jnp.float32)

def layer_norm(values, norm_gain, norm_bias):
    row_mean = lax.optimization_barrier(jnp.mean(values, axis=-1, keepdims=True))
    centred = values - row_mean
    spread = lax.optimization_barrier(jnp.mean(centred * centred, axis=-1, keepdims=True))
    return centred * lax.rsqrt(spread + EPS_NORM) * norm_gain + norm_bias

def code_signs(code_ints, code_bits):
    shifts = jnp.arange(code_bits, dtype=jnp.int32)
    picked = jnp.bitwise_and(jnp.right_shift(code_ints[..., None], shifts), 1)
    return (2 * picked - 1).astype(jnp.float32)

def hash_weight(projected_rows, signs, planes):
    shaped = projected_rows.reshape(projected_rows.shape[0], HEADS, HEAD)
    unit_rows = shaped * lax.rsqrt(lax.optimization_barrier(jnp.sum(shaped * shaped, axis=-1, keepdims=True)) + EPS_UNIT)
    lifted = jnp.einsum('rhe,eb->hrb', unit_rows, planes, precision=HIGHEST)
    return jnp.exp(lax.optimization_barrier(jnp.sum(signs * lifted, axis=-1)))

def estimate_all(query_rows, key_rows, value_rows, hyperplanes, q_codes, k_codes, item_of):
    per_item = 2 ** TAU
    n_buckets = ITEMS * per_item
    value_heads = value_rows.reshape(TOKENS, HEADS, HEAD).transpose(1, 0, 2)
    head_base = (jnp.arange(HEADS, dtype=jnp.int32) * n_buckets)[:, None] + item_of[None, :] * per_item

    def one_set(carry, pieces):
        planes, query_ints, key_ints = pieces
        key_w = hash_weight(key_rows, code_signs(key_ints, TAU), planes)
        query_w = hash_weight(query_rows, code_signs(query_ints, TAU), planes)
        key_slot = (head_base + key_ints).reshape(-1)
        query_slot = (head_base + query_ints).reshape(-1)
        weighted = (key_w[..., None] * value_heads).reshape(-1, HEAD)
        bucket_sums = jax.ops.segment_sum(weighted, key_slot, num_segments=HEADS * n_buckets)
        bucket_mass = jax.ops.segment_sum(key_w.reshape(-1), key_slot, num_segments=HEADS * n_buckets)
        numer_add = query_w[..., None] * bucket_sums[query_slot].reshape(HEADS, TOKENS, HEAD)
        denom_add = query_w * bucket_mass[query_slot].reshape(HEADS, TOKENS)
        return ((carry[0] + numer_add, carry[1] + denom_add), None)
    start_carry = (jnp.zeros((HEADS, TOKENS, HEAD), jnp.float32), jnp.zeros((HEADS, TOKENS), jnp.float32))
    (numerator, denominator), _ = lax.scan(jax.checkpoint(one_set), start_carry, (hyperplanes, q_codes, k_codes))
    estimate = numerator / (denominator[..., None] + 1.0)
    return estimate.transpose(1, 0, 2).reshape(TOKENS, D)

def conv_values(value_rows, conv_weight, item_of):
    shaped = value_rows.reshape(TOKENS, HEADS, HEAD)
    padded = jnp.pad(shaped, ((CONV_HALF, CONV_HALF), (0, 0), (0, 0)))
    item_tags = jnp.pad(item_of + 1, (CONV_HALF, CONV_HALF))
    own_tags = item_of + 1
    running = jnp.zeros((TOKENS, HEADS, HEAD), jnp.float32)
    for tap_index in range(2 * CONV_HALF + 1):
        same_item = (item_tags[tap_index:tap_index + TOKENS] == own_tags).astype(jnp.float32)
        running = running + conv_weight[:, tap_index][None, :, None] * same_item[:, None, None] * padded[tap_index:tap_index + TOKENS]
    return running.reshape(TOKENS, D)

def reference(tokens, item_cuts, q_codes, k_codes, hyperplanes, w_query, b_query, w_key, b_key, w_value, b_value, conv_weight, w_out, b_out, ln1_gain, ln1_bias, w_in, b_in, w_back, b_back, ln2_gain, ln2_bias, cotangent):
    positions = jnp.arange(TOKENS, dtype=jnp.int32)
    item_of = lax.optimization_barrier(jnp.sum((positions[:, None] >= item_cuts[None, :]).astype(jnp.int32), axis=1)) - 1

    def forward(inputs, wq, bq, wk, bk, wv, bv, conv_w, wo, bo, gain_one, bias_one, wi, bi, wb, bb, gain_two, bias_two):
        query_rows = low_back(matmul(inputs, wq) + bq)
        key_rows = low_back(matmul(inputs, wk) + bk)
        value_rows = low_back(matmul(inputs, wv) + bv)
        attended = estimate_all(query_rows, key_rows, value_rows, hyperplanes, q_codes, k_codes, item_of)
        attended = attended + conv_values(value_rows, conv_w, item_of)
        attended = low(low_back(attended))
        branch = low_back(matmul(attended, wo) + bo)
        hidden = layer_norm(inputs + branch, gain_one, bias_one)
        inner_pre = low_back(matmul(low(hidden), wi) + bi)
        activated = low(jax.nn.gelu(inner_pre, approximate=False))
        outer_out = low_back(matmul(activated, wb) + bb)
        return layer_norm(hidden + outer_out, gain_two, bias_two)
    weights = (w_query, b_query, w_key, b_key, w_value, b_value, conv_weight, w_out, b_out, ln1_gain, ln1_bias, w_in, b_in, w_back, b_back, ln2_gain, ln2_bias)
    weights = tuple((entry.astype(jnp.float32) for entry in weights))
    output, pullback = jax.vjp(forward, tokens.astype(jnp.float32), *weights)
    grads = pullback(cotangent)
    return (output, grads[0], grads[1], grads[2], grads[3], grads[4], grads[5], grads[6], grads[7], grads[8], grads[9], grads[10], grads[11], grads[12], grads[13], grads[14], grads[15], grads[16], grads[17])
```

```python
import functools

import jax
import jax.numpy as jnp
from jax import lax
from jax.experimental import pallas as pl
from jax.experimental.pallas import tpu as pltpu
from jax.sharding import Mesh, PartitionSpec as P

BF = jnp.bfloat16
F32 = jnp.float32
HIGHEST = lax.Precision.HIGHEST
EPS_NORM = 1e-05
EPS_UNIT = 1e-06

D = 768
HEADS = 12
HEAD = 64
SETS = 8
BITS = 8
SLOTS = 256
FF = 3072
ROWS = 1280
BLOCK = 2560
OWN = 160
MEMBERS = 16
EDGE = 128
TOTAL = 20480
BLOCKS = 8
MESH = pl.DeviceIdType.MESH
CHUNK = 512
CHUNKS = BLOCK // CHUNK
ITEM = 80
CLASSES = 3
VMEM_LIMIT = 56 * 1024 * 1024

BLOCK_AXES = ("zh", "x")
MEMBER_AXES = ("c", "y", "zl")
ALL_AXES = BLOCK_AXES + MEMBER_AXES


def nt(left, right, **kw):
    return lax.dot_general(left, right, (((1,), (1,)), ((), ())), preferred_element_type=F32, **kw)


def nn(left, right, **kw):
    return lax.dot_general(left, right, (((1,), (0,)), ((), ())), preferred_element_type=F32, **kw)


def tn(left, right, **kw):
    return lax.dot_general(left, right, (((0,), (0,)), ((), ())), preferred_element_type=F32, **kw)


def unit_of(proj):
    scale = lax.rsqrt(jnp.sum(proj * proj, axis=0, keepdims=True) + EPS_UNIT)
    return proj * scale, scale


def bits_of(codes):
    return [(jnp.bitwise_and(codes, 1 << b) != 0) for b in range(BITS)]


def hash_weight(proj, codes, planes):
    unit, _ = unit_of(proj)
    lifted = nn(planes, unit, precision=HIGHEST)
    total = None
    for b, bit in enumerate(bits_of(codes)):
        part = lifted[b * SETS : (b + 1) * SETS]
        part = jnp.where(bit, part, -part)
        total = part if total is None else total + part
    return jnp.exp(total)


def hash_back(z_grad, proj, codes, planes):
    unit, scale = unit_of(proj)
    lifted_grad = jnp.concatenate([jnp.where(bit, z_grad, -z_grad) for bit in bits_of(codes)], axis=0)
    unit_grad = tn(planes, lifted_grad, precision=HIGHEST)
    return scale * (unit_grad - unit * jnp.sum(unit * unit_grad, axis=0, keepdims=True))


def one_hot(codes_row, weight_row):
    width = codes_row.shape[1]
    slots = lax.broadcasted_iota(jnp.int32, (SLOTS, width), 0)
    return jnp.where(slots == codes_row, weight_row, 0.0).astype(BF)


def fill_hot(hot_ref, codes, weights):
    for s in range(SETS):
        hot_ref[s * SLOTS : (s + 1) * SLOTS, :] = one_hot(codes[s : s + 1], weights[s : s + 1])


def by_item(sums, mass, masks):
    width = sums.shape[1]
    lead = lax.broadcasted_iota(jnp.int32, (ITEM - HEAD, width), 0) == 0
    tail = jnp.where(lead, mass, 0.0)
    whole = jnp.concatenate([sums, tail], axis=0)
    return jnp.concatenate([whole * masks[w : w + 1] for w in range(CLASSES)], axis=0).astype(BF)


def pick_item(stacked, masks):
    total = None
    for w in range(CLASSES):
        part = stacked[w * ITEM : (w + 1) * ITEM] * masks[w : w + 1]
        total = part if total is None else total + part
    return total


def circulant(base):
    grid = jnp.broadcast_to(base, (256, 256))
    grid = pltpu.roll(grid, 0, 1, stride=1, stride_axis=0)
    row = lax.broadcasted_iota(jnp.int32, (256, 256), 0)
    col = lax.broadcasted_iota(jnp.int32, (256, 256), 1)
    return (
        jnp.where(col < row, grid, 0.0).astype(BF),
        jnp.where(col >= row, grid, 0.0).astype(BF),
    )


def pack(rows, out, *lead):
    half = OWN // 2
    for p in range(MEMBERS):
        upper = rows[p * OWN : p * OWN + half]
        lower = rows[p * OWN + half : (p + 1) * OWN]
        out[(p, *lead)] = jnp.concatenate([upper, lower], axis=1).astype(BF)


def unpack(chunks, rows):
    half = OWN // 2
    for p in range(MEMBERS):
        both = chunks[p].astype(F32)
        rows[p * OWN : p * OWN + half] = both[:, :HEAD]
        rows[p * OWN + half : (p + 1) * OWN] = both[:, HEAD:]


def chunk_of(i, width=CHUNK, offset=0):
    return pl.ds(pl.multiple_of(i * width, 128) + offset, width)


def fill_kernel(tok, w_t, bias, planes, codes, masks, qkv, weights, long_out, short_out, hot, acc):
    acc[...] = jnp.zeros_like(acc)

    def step(i, _):
        cols = chunk_of(i)
        rows = pl.ds(pl.multiple_of(i * CHUNK, CHUNK), CHUNK)
        proj = nt(w_t[...], tok[rows, :]) + bias[...]
        qkv[:, cols] = proj
        q_codes = codes[0, :, cols]
        k_codes = codes[1, :, cols]
        q_w = hash_weight(proj[:HEAD], q_codes, planes[...])
        k_w = hash_weight(proj[HEAD : 2 * HEAD], k_codes, planes[...])
        weights[:, cols] = jnp.concatenate([q_w, k_w], axis=0)
        items = by_item(proj[2 * HEAD :], jnp.ones((1, CHUNK), F32), masks[:, cols])
        fill_hot(hot, k_codes, k_w)
        acc[...] += nt(items, hot[...])
        return 0

    lax.fori_loop(0, CHUNKS, step, 0)
    long_out[...] = acc[:ITEM].astype(BF)
    short_out[...] = acc[ITEM:].astype(BF)


def read_kernel(
    long_tab, short_tab, codes, weights, masks, value, before, after, v_bias, taps,
    attended, estimate, scale, hot, table, ext, rows_ref,
):
    table[:ITEM] = long_tab[...]
    table[ITEM:] = short_tab[...]
    ones = jnp.ones((1, EDGE), F32)
    ext[:, :EDGE] = by_item(before[...].astype(F32) + v_bias[...], ones, masks[:, :EDGE])
    ext[:, EDGE + BLOCK :] = by_item(after[...].astype(F32) + v_bias[...], ones, masks[:, EDGE + BLOCK :])

    def build(i, _):
        cols = chunk_of(i)
        inner = chunk_of(i, offset=EDGE)
        ext[:, inner] = by_item(value[:, cols] + v_bias[...], jnp.ones((1, CHUNK), F32), masks[:, inner])
        return 0

    lax.fori_loop(0, CHUNKS, build, 0)
    lower, upper = circulant(taps[...])

    def step(i, _):
        cols = chunk_of(i)
        inner = chunk_of(i, offset=EDGE)
        own = masks[:, inner]
        fill_hot(hot, codes[0, :, cols], weights[:SETS, cols])
        found = pick_item(nn(table[...], hot[...]), own)
        recip = 1.0 / (found[HEAD : HEAD + 1] + 1.0)
        est = (found[:HEAD] - v_bias[...]) * recip
        estimate[:, cols] = est
        scale[:, cols] = recip
        mixed = []
        for half in range(2):
            at = pl.multiple_of(i * CHUNK, 256) + half * 256
            mixed.append(nn(ext[:, pl.ds(at, 256)], lower) + nn(ext[:, pl.ds(at + 256, 256)], upper))
        conv = pick_item(jnp.concatenate(mixed, axis=1), own)[:HEAD]
        rows = pl.ds(pl.multiple_of(i * CHUNK, CHUNK), CHUNK)
        rows_ref[rows, :] = jnp.transpose(est + v_bias[...] + conv)
        return 0

    lax.fori_loop(0, CHUNKS, step, 0)
    pack(rows_ref, attended)


def read_back_kernel(
    chunks, estimate, scale, codes, weights, masks, long_out, short_out, grad, denom, hot, acc,
    grad_rows,
):
    acc[...] = jnp.zeros_like(acc)
    unpack(chunks, grad_rows)

    def step(i, _):
        cols = chunk_of(i)
        rows = pl.ds(pl.multiple_of(i * CHUNK, CHUNK), CHUNK)
        got = jnp.transpose(grad_rows[rows, :])
        grad[:, cols] = got
        numer = got * scale[:, cols]
        den = -jnp.sum(numer * estimate[:, cols], axis=0, keepdims=True)
        denom[:, cols] = den
        items = by_item(numer, den, masks[:, cols])
        fill_hot(hot, codes[0, :, cols], weights[:SETS, cols])
        acc[...] += nt(items, hot[...])
        return 0

    lax.fori_loop(0, CHUNKS, step, 0)
    long_out[...] = acc[:ITEM].astype(BF)
    short_out[...] = acc[ITEM:].astype(BF)


def query_back_kernel(
    long_tab, short_tab, grad, denom, scale, codes, weights, masks, query, planes, out, table
):
    table[:ITEM] = long_tab[...]
    table[ITEM:] = short_tab[...]

    def step(i, _):
        cols = chunk_of(i)
        own = masks[:, cols]
        q_codes = codes[0, :, cols]
        numer = grad[:, cols] * scale[:, cols]
        den = denom[:, cols]
        parts = []
        for s in range(SETS):
            hot = one_hot(q_codes[s : s + 1], 1.0)
            found = pick_item(nn(table[:, s * SLOTS : (s + 1) * SLOTS], hot), own)
            parts.append(
                jnp.sum(found[:HEAD] * numer, axis=0, keepdims=True) + found[HEAD : HEAD + 1] * den
            )
        z_grad = jnp.concatenate(parts, axis=0) * weights[:SETS, cols]
        out[:, cols] = hash_back(z_grad, query[:, cols], q_codes, planes[...]).astype(BF)
        return 0

    lax.fori_loop(0, CHUNKS, step, 0)


def key_back_kernel(
    long_tab, short_tab, grad, before, after, codes, weights, masks, qkv, v_before, v_after,
    planes, v_bias, taps_back, q_grad, tok,
    grad_out, w_out, b_out, taps_out, table, ext, v_ext, g_all, rows_ref,
):
    table[:ITEM] = long_tab[...]
    table[ITEM:] = short_tab[...]
    none = jnp.zeros((1, EDGE), F32)
    lo, hi = slice(None, EDGE), slice(EDGE + BLOCK, None)
    ext[:, lo] = by_item(before[...].astype(F32), none, masks[:, lo])
    ext[:, hi] = by_item(after[...].astype(F32), none, masks[:, hi])
    v_ext[:, lo] = by_item(v_before[...].astype(F32) + v_bias[...], none, masks[:, lo])
    v_ext[:, hi] = by_item(v_after[...].astype(F32) + v_bias[...], none, masks[:, hi])

    def build(i, _):
        cols = chunk_of(i)
        inner = chunk_of(i, offset=EDGE)
        zero = jnp.zeros((1, CHUNK), F32)
        ext[:, inner] = by_item(grad[:, cols], zero, masks[:, inner])
        v_ext[:, inner] = by_item(qkv[2 * HEAD :, cols] + v_bias[...], zero, masks[:, inner])
        return 0

    lax.fori_loop(0, CHUNKS, build, 0)
    lower, upper = circulant(taps_back[...])

    def step(i, carry):
        cols = chunk_of(i)
        inner = chunk_of(i, offset=EDGE)
        own = masks[:, inner]
        k_codes = codes[1, :, cols]
        k_w = weights[SETS:, cols]
        val = qkv[2 * HEAD :, cols]
        parts = []
        v_grad = jnp.zeros((HEAD, CHUNK), F32)
        for s in range(SETS):
            hot = one_hot(k_codes[s : s + 1], 1.0)
            found = pick_item(nn(table[:, s * SLOTS : (s + 1) * SLOTS], hot), own)
            parts.append(
                jnp.sum(found[:HEAD] * val, axis=0, keepdims=True) + found[HEAD : HEAD + 1]
            )
            v_grad = v_grad + found[:HEAD] * k_w[s : s + 1]
        z_grad = jnp.concatenate(parts, axis=0) * k_w
        k_grad = hash_back(z_grad, qkv[HEAD : 2 * HEAD, cols], k_codes, planes[...])
        mixed = []
        c_low, c_high = carry
        for half in range(2):
            at = pl.multiple_of(i * CHUNK, 256) + half * 256
            mixed.append(nn(ext[:, pl.ds(at, 256)], lower) + nn(ext[:, pl.ds(at + 256, 256)], upper))
            here = ext[:, pl.ds(at + EDGE, 256)]
            c_low = c_low + tn(v_ext[:, pl.ds(at, 256)], here)
            c_high = c_high + tn(v_ext[:, pl.ds(at + 256, 256)], here)
        v_grad = v_grad + pick_item(jnp.concatenate(mixed, axis=1), own)[:HEAD]
        g_all[:HEAD, cols] = q_grad[:, cols]
        g_all[HEAD : 2 * HEAD, cols] = k_grad.astype(BF)
        g_all[2 * HEAD :, cols] = v_grad.astype(BF)
        return c_low, c_high

    zeros = jnp.zeros((256, 256), F32)
    c_low, c_high = lax.fori_loop(0, CHUNKS, step, (zeros, zeros))
    row = lax.broadcasted_iota(jnp.int32, (256, 256), 0)
    col = lax.broadcasted_iota(jnp.int32, (256, 256), 1)
    skew = jnp.where(col < row, c_low, c_high)
    for b in range(8):
        skew = jnp.where(jnp.bitwise_and(row, 1 << b) != 0, pltpu.roll(skew, 256 - (1 << b), 1), skew)
    taps_out[...] = jnp.sum(skew, axis=0, keepdims=True)
    for k in range(3):
        rows_ref[...] = jnp.transpose(g_all[k * HEAD : (k + 1) * HEAD, :].astype(F32))
        pack(rows_ref, grad_out, k)
    w_out[...] = nn(g_all[...], tok[...])
    b_out[...] = jnp.sum(g_all[...].astype(F32), axis=1, keepdims=True)


def member_id(member):
    return {"c": member // 8, "y": (member % 8) // 2, "zl": member % 2}


def block_id(block):
    return {"zh": block // 4, "x": block % 4}


def my_member():
    return lax.axis_index("c") * 8 + lax.axis_index("y") * 2 + lax.axis_index("zl")


def my_block():
    return lax.axis_index("zh") * 4 + lax.axis_index("x")


def greet(ids):
    barrier = pltpu.get_barrier_semaphore()
    for one in ids:
        pl.semaphore_signal(barrier, inc=1, device_id=one, device_id_type=MESH)
    pl.semaphore_wait(barrier, len(ids))


def send(src, dst, send_sem, recv_sem, device):
    return pltpu.make_async_remote_copy(
        src_ref=src, dst_ref=dst, send_sem=send_sem, recv_sem=recv_sem,
        device_id=device, device_id_type=MESH,
    )


def start_kernel(tokens, both, planes, tok_out, codes_out, planes_out, local, send_sem, recv_sem):
    me = my_member()
    core = lax.axis_index("c")
    mine = me % 8
    greet([member_id((me + d) % MEMBERS) for d in range(1, MEMBERS)])
    part = pl.ds(pl.multiple_of(core * ROWS, ROWS), ROWS)
    swap = send(tokens, tok_out.at[part], send_sem.at[32], recv_sem.at[32], member_id((me + 8) % MEMBERS))
    swap.start()
    keep = pltpu.make_async_copy(tokens, tok_out.at[part], local.at[0])
    keep.start()

    def codes_to(d):
        to = (me + d) % MEMBERS
        return to, send(
            both.at[jnp.minimum(to, HEADS - 1)], codes_out.at[me], send_sem.at[d],
            recv_sem.at[me], member_id(to),
        )

    def planes_to(d):
        to = core * 8 + (mine + d) % 8
        return send(planes, planes_out.at[mine], send_sem.at[16 + d], recv_sem.at[16 + mine], member_id(to))

    for d in range(1, MEMBERS):
        to, copy = codes_to(d)
        pl.when(to < HEADS)(copy.start)
    for d in range(1, 8):
        planes_to(d).start()
    own_codes = pltpu.make_async_copy(both.at[jnp.minimum(me, HEADS - 1)], codes_out.at[me], local.at[1])
    own_codes.start()
    own_planes = pltpu.make_async_copy(planes, planes_out.at[mine], local.at[2])
    own_planes.start()
    keep.wait()
    own_codes.wait()
    own_planes.wait()
    for d in range(1, MEMBERS):
        to, copy = codes_to(d)
        pl.when(to < HEADS)(copy.wait_send)
        came = (me + d) % MEMBERS
        got = send(both.at[0], codes_out.at[came], send_sem.at[d], recv_sem.at[came], member_id(came))
        pl.when(me < HEADS)(got.wait_recv)
    for d in range(1, 8):
        planes_to(d).wait_send()
        came = (mine + d) % 8
        send(
            planes, planes_out.at[came], send_sem.at[16 + d], recv_sem.at[16 + came],
            member_id(core * 8 + came),
        ).wait_recv()
    swap.wait_send()
    other = pl.ds(pl.multiple_of((1 - core) * ROWS, ROWS), ROWS)
    send(tokens, tok_out.at[other], send_sem.at[32], recv_sem.at[32], member_id((me + 8) % MEMBERS)).wait_recv()


def scatter_kernel(chunks, out, local, send_sem, recv_sem):
    me = my_member()
    greet([member_id((me + d) % MEMBERS) for d in range(1, MEMBERS)])
    owner = me < HEADS
    mine = jnp.minimum(me, HEADS - 1)

    def to(d):
        dest = (me + d) % MEMBERS
        return send(chunks.at[dest], out.at[mine], send_sem.at[d], recv_sem.at[mine], member_id(dest))

    for d in range(1, MEMBERS):
        pl.when(owner)(to(d).start)
    keep = pltpu.make_async_copy(chunks.at[me], out.at[mine], local)
    pl.when(owner)(keep.start)
    for h in range(HEADS):
        got = send(chunks.at[0], out.at[h], send_sem.at[0], recv_sem.at[h], member_id(h))
        pl.when(me != h)(got.wait_recv)
    for d in range(1, MEMBERS):
        pl.when(owner)(to(d).wait_send)
    pl.when(owner)(keep.wait)


def gather_kernel(chunks, out, local, send_sem, recv_sem):
    me = my_member()
    greet([member_id((me + d) % MEMBERS) for d in range(1, MEMBERS)])
    owner = me < HEADS
    mine = jnp.minimum(me, HEADS - 1)

    def to(d):
        dest = (me + d) % MEMBERS
        copy = send(
            chunks.at[jnp.minimum(dest, HEADS - 1)], out.at[me], send_sem.at[d], recv_sem.at[me],
            member_id(dest),
        )
        return dest < HEADS, copy

    for d in range(1, MEMBERS):
        wanted, copy = to(d)
        pl.when(wanted)(copy.start)
    keep = pltpu.make_async_copy(chunks.at[mine], out.at[me], local)
    keep.start()
    for d in range(1, MEMBERS):
        came = (me + d) % MEMBERS
        got = send(chunks.at[0], out.at[came], send_sem.at[0], recv_sem.at[came], member_id(came))
        pl.when(owner)(got.wait_recv)
    for d in range(1, MEMBERS):
        wanted, copy = to(d)
        pl.when(wanted)(copy.wait_send)
    keep.wait()


def reduce_kernel(part, first, last, out, before, after, got, send_sem, recv_sem, halo_send, halo_recv):
    me = my_block()
    greet([block_id((me + d) % BLOCKS) for d in range(1, BLOCKS)])
    down, up = block_id((me + BLOCKS - 1) % BLOCKS), block_id((me + 1) % BLOCKS)

    def cols(k):
        return pl.ds(pl.multiple_of(k * SLOTS, SLOTS), SLOTS)

    def to_share(d):
        dest = (me + d) % BLOCKS
        return send(
            part.at[:, cols(dest)], got.at[d], send_sem.at[d], recv_sem.at[d], block_id(dest)
        )

    for d in range(1, BLOCKS):
        to_share(d).start()
    to_down = send(first, after, halo_send.at[0], halo_recv.at[0], down)
    to_up = send(last, before, halo_send.at[1], halo_recv.at[1], up)
    to_down.start()
    to_up.start()
    total = part[:, cols(me)].astype(F32)
    for d in range(1, BLOCKS):
        to_share(d).wait_recv()
        total = total + got[d].astype(F32)
    out[:, cols(me)] = total.astype(BF)

    def to_all(d):
        dest = (me + d) % BLOCKS
        return send(
            out.at[:, cols(me)], out.at[:, cols(me)], send_sem.at[BLOCKS + d], recv_sem.at[BLOCKS + d],
            block_id(dest),
        )

    for d in range(1, BLOCKS):
        to_all(d).start()
    for d in range(1, BLOCKS):
        came = (me + BLOCKS - d) % BLOCKS
        send(
            out.at[:, cols(came)], out.at[:, cols(came)], send_sem.at[BLOCKS + d],
            recv_sem.at[BLOCKS + d], block_id(came),
        ).wait_recv()
        to_share(d).wait_send()
        to_all(d).wait_send()
    to_down.wait()
    to_up.wait()


def call(kernel, outs, scratch, *args):
    return pl.pallas_call(
        kernel,
        out_shape=[jax.ShapeDtypeStruct(shape, kind) for shape, kind in outs],
        in_specs=[pl.BlockSpec(memory_space=pltpu.VMEM)] * len(args),
        out_specs=[pl.BlockSpec(memory_space=pltpu.VMEM)] * len(outs),
        scratch_shapes=[pltpu.VMEM(shape, kind) for shape, kind in scratch],
        compiler_params=pltpu.CompilerParams(vmem_limit_bytes=VMEM_LIMIT),
    )(*args)


def talk(kernel, ident, outs, scratch, *args):
    return pl.pallas_call(
        kernel,
        out_shape=[jax.ShapeDtypeStruct(shape, kind) for shape, kind in outs],
        in_specs=[pl.BlockSpec(memory_space=pltpu.VMEM)] * len(args),
        out_specs=[pl.BlockSpec(memory_space=pltpu.VMEM)] * len(outs),
        scratch_shapes=scratch,
        compiler_params=pltpu.CompilerParams(
            collective_id=ident, has_side_effects=True, vmem_limit_bytes=VMEM_LIMIT
        ),
    )(*args)


def dma(count):
    return pltpu.SemaphoreType.DMA((count,))


def all_to_members(array, ident):
    shape = (HEADS,) + array.shape[1:]
    (out,) = talk(scatter_kernel, ident, [(shape, BF)], [pltpu.SemaphoreType.DMA, dma(16), dma(16)], array)
    return out


def all_to_owners(array, ident):
    shape = (MEMBERS,) + array.shape[1:]
    (out,) = talk(gather_kernel, ident, [(shape, BF)], [pltpu.SemaphoreType.DMA, dma(16), dma(16)], array)
    return out


def sum_blocks(part, first, last, ident):
    edge = ((HEAD, EDGE), BF)
    return talk(
        reduce_kernel, ident, [((ITEM, SETS * SLOTS), BF), edge, edge],
        [pltpu.VMEM((BLOCKS, ITEM, SLOTS), BF), dma(2 * BLOCKS), dma(2 * BLOCKS), dma(2), dma(2)],
        part, first, last,
    )


def layer_norm(values, norm_gain, norm_bias):
    row_mean = jnp.mean(values, axis=-1, keepdims=True)
    centred = values - row_mean
    spread = jnp.mean(centred * centred, axis=-1, keepdims=True)
    return centred * lax.rsqrt(spread + EPS_NORM) * norm_gain + norm_bias


def gelu_exact(values):
    return jax.nn.gelu(values, approximate=False)


def to_members(array):
    return lax.all_to_all(array, MEMBER_AXES, 0, 0, tiled=True)


def from_neighbours(first, last):
    up = [(i, (i + 1) % 8) for i in range(8)]
    down = [(j, i) for i, j in up]
    return lax.ppermute(last, BLOCK_AXES, up), lax.ppermute(first, BLOCK_AXES, down)


def item_masks(cuts, block):
    start = block * BLOCK - EDGE
    pos = start + jnp.arange(BLOCK + 2 * EDGE, dtype=jnp.int32)
    item = jnp.sum((pos[None, :] >= cuts[:, None]).astype(jnp.int32), axis=0) - 1
    longest = jnp.where(cuts[2] - cuts[1] > 1024, 1, 2)
    first_half = block < 4
    outer = jnp.where(first_half, 0, 3)
    inner = jnp.where(first_half, 1, 2)
    valid = (pos >= 0) & (pos < TOTAL)
    is_long = valid & (item == longest)
    is_outer = valid & (item == outer)
    is_inner = valid & (item == inner) & (inner != longest)
    none = jnp.zeros_like(is_long)
    return jnp.stack([is_long, is_outer, is_inner] + [none] * 5).astype(F32)


def per_device(
    tokens, item_cuts, q_codes, k_codes, hyperplanes, w_query, b_query, w_key, b_key,
    w_value, b_value, conv_weight, w_out, b_out, ln1_gain, ln1_bias, w_in, b_in, w_back,
    b_back, ln2_gain, ln2_bias, cotangent,
):
    block = lax.axis_index(BLOCK_AXES)
    member = lax.axis_index(MEMBER_AXES)
    hash_at = lax.axis_index(("y", "zl"))
    head = jnp.minimum(member, HEADS - 1)
    both = jnp.concatenate([q_codes, k_codes], axis=0).transpose(1, 0, 2)
    tok, both, planes = talk(
        start_kernel, 0,
        [((BLOCK, D), BF), ((MEMBERS, 2, ROWS), jnp.int32), ((SETS, BITS, HEAD), F32)],
        [dma(3), dma(33), dma(33)],
        tokens, both, hyperplanes[0].T,
    )
    codes = both.reshape(2, SETS, 2, ROWS).transpose(2, 1, 0, 3).reshape(2, SETS, BLOCK)
    planes = planes.transpose(1, 0, 2).reshape(BITS * SETS, HEAD)
    masks = item_masks(item_cuts, block)
    own_masks = masks[:, EDGE : EDGE + BLOCK]

    def head_cols(weight):
        return lax.dynamic_slice_in_dim(weight, head * HEAD, HEAD, 1).T

    def head_bias(bias):
        return lax.dynamic_slice_in_dim(bias, head * HEAD, HEAD, 0)[:, None]

    w_t = jnp.concatenate([head_cols(w) for w in (w_query, w_key, w_value)], axis=0)
    v_bias = head_bias(b_value)
    bias_t = jnp.concatenate([head_bias(b_query), head_bias(b_key), jnp.zeros_like(v_bias)], axis=0)
    taps = lax.dynamic_slice_in_dim(conv_weight, head, 1, 0)
    taps_fwd = jnp.pad(taps[:, ::-1], ((0, 0), (96, 95)))
    taps_bwd = jnp.pad(taps, ((0, 0), (96, 95)))

    hot = ((SETS * SLOTS, CHUNK), BF)
    acc = ((CLASSES * ITEM, SETS * SLOTS), F32)
    table = ((CLASSES * ITEM, SETS * SLOTS), BF)
    ext = ((CLASSES * ITEM, BLOCK + 2 * EDGE), BF)
    rows_f32 = ((BLOCK, HEAD), F32)
    long_shape = ((ITEM, SETS * SLOTS), BF)
    short_shape = (((CLASSES - 1) * ITEM, SETS * SLOTS), BF)

    qkv, weights, long_part, short_tab = call(
        fill_kernel,
        [((3 * HEAD, BLOCK), F32), ((2 * SETS, BLOCK), F32), long_shape, short_shape],
        [hot, acc],
        tok, w_t, bias_t, planes, codes, own_masks,
    )
    value = qkv[2 * HEAD :]
    long_tab, v_before, v_after = sum_blocks(
        long_part, value[:, :EDGE].astype(BF), value[:, -EDGE:].astype(BF), 1
    )
    att_rows, estimate, scale = call(
        read_kernel,
        [((MEMBERS, OWN // 2, 2 * HEAD), BF), ((HEAD, BLOCK), F32), ((1, BLOCK), F32)],
        [hot, table, ext, rows_f32],
        long_tab, short_tab, codes, weights, masks, value, v_before, v_after, v_bias, taps_fwd,
    )
    att = all_to_members(att_rows, 2)
    attended_low = att.reshape(HEADS, OWN // 2, 2, HEAD).transpose(2, 1, 0, 3).reshape(OWN, D)

    own_tokens = lax.dynamic_slice_in_dim(tokens, hash_at * OWN, OWN, 0)
    branch = nn(attended_low, w_out) + b_out
    hidden, norm_one_back = jax.vjp(layer_norm, own_tokens.astype(F32) + branch, ln1_gain, ln1_bias)
    hidden_low = hidden.astype(BF)
    inner_pre = nn(hidden_low, w_in) + b_in
    activated, gelu_back = jax.vjp(gelu_exact, inner_pre)
    activated_low = activated.astype(BF)
    outer_out = nn(activated_low, w_back) + b_back
    output, norm_two_back = jax.vjp(layer_norm, hidden + outer_out, ln2_gain, ln2_bias)
    sum_grad, grad_ln2_gain, grad_ln2_bias = norm_two_back(cotangent)
    outer_grad = sum_grad.astype(BF)
    grad_w_back = tn(activated_low, outer_grad)
    grad_b_back = jnp.sum(outer_grad.astype(F32), axis=0)
    (inner_grad,) = gelu_back(nt(outer_grad, w_back))
    inner_low = inner_grad.astype(BF)
    grad_w_in = tn(hidden_low, inner_low)
    grad_b_in = jnp.sum(inner_low.astype(F32), axis=0)
    hidden_grad = sum_grad + nt(inner_low, w_in)
    resid_grad, grad_ln1_gain, grad_ln1_bias = norm_one_back(hidden_grad)
    branch_grad = resid_grad.astype(BF)
    grad_w_out = tn(attended_low, branch_grad)
    grad_b_out = jnp.sum(branch_grad.astype(F32), axis=0)
    attended_grad = nt(branch_grad, w_out).astype(BF)

    grad_chunks = attended_grad.reshape(2, OWN // 2, HEADS, HEAD).transpose(2, 1, 0, 3)
    grad_rows = all_to_owners(grad_chunks.reshape(HEADS, OWN // 2, 2 * HEAD), 3)
    long_gpart, short_gtab, grad_t, denom = call(
        read_back_kernel,
        [long_shape, short_shape, ((HEAD, BLOCK), F32), ((1, BLOCK), F32)],
        [hot, acc, rows_f32],
        grad_rows, estimate, scale, codes, weights, own_masks,
    )
    long_gtab, g_before, g_after = sum_blocks(
        long_gpart, grad_t[:, :EDGE].astype(BF), grad_t[:, -EDGE:].astype(BF), 1
    )
    (q_grad,) = call(
        query_back_kernel,
        [((HEAD, BLOCK), BF)],
        [table],
        long_tab, short_tab, grad_t, denom, scale, codes, weights, own_masks, qkv[:HEAD], planes,
    )
    grad_qkv, head_w, head_b, head_taps = call(
        key_back_kernel,
        [((MEMBERS, 3, OWN // 2, 2 * HEAD), BF), ((3 * HEAD, D), F32), ((3 * HEAD, 1), F32), ((1, 256), F32)],
        [table, ext, ext, ((3 * HEAD, BLOCK), BF), rows_f32],
        long_gtab, short_gtab, grad_t, g_before, g_after, codes, weights, masks, qkv,
        v_before, v_after, planes, v_bias, taps_bwd, q_grad, tok,
    )

    lows = all_to_members(grad_qkv, 4)
    lows = lows.reshape(HEADS, 3, OWN // 2, 2, HEAD).transpose(1, 3, 2, 0, 4).reshape(3, OWN, D)
    grad_tokens = resid_grad + nt(lows[0], w_query) + nt(lows[1], w_key) + nt(lows[2], w_value)

    def all_heads(array):
        return lax.all_gather(lax.psum(array, BLOCK_AXES), MEMBER_AXES, axis=0)[:HEADS]

    heads_w = all_heads(head_w.astype(BF)).astype(F32).reshape(HEADS, 3, HEAD, D)
    heads_w = heads_w.transpose(1, 3, 0, 2).reshape(3, D, D)
    small = jnp.concatenate([head_b[:, 0], head_taps[0, 96:161][::-1]])
    heads_small = all_heads(small)
    heads_b = heads_small[:, : 3 * HEAD].reshape(HEADS, 3, HEAD).transpose(1, 0, 2).reshape(3, D)
    grad_conv_weight = heads_small[:, 3 * HEAD :]

    grad_w_in, grad_w_back, grad_w_out = [
        part.astype(F32)
        for part in lax.psum(
            (grad_w_in.astype(BF), grad_w_back.astype(BF), grad_w_out.astype(BF)), ALL_AXES
        )
    ]
    vectors = (
        grad_b_out, grad_ln1_gain, grad_ln1_bias, grad_b_back, grad_ln2_gain, grad_ln2_bias, grad_b_in,
    )
    joined = lax.psum(jnp.concatenate(vectors), ALL_AXES)
    (
        grad_b_out, grad_ln1_gain, grad_ln1_bias, grad_b_back, grad_ln2_gain, grad_ln2_bias, grad_b_in,
    ) = jnp.split(joined, [D * (k + 1) for k in range(6)])
    return (
        output, grad_tokens, heads_w[0], heads_b[0], heads_w[1], heads_b[1], heads_w[2], heads_b[2],
        grad_conv_weight, grad_w_out, grad_b_out, grad_ln1_gain, grad_ln1_bias, grad_w_in, grad_b_in,
        grad_w_back, grad_b_back, grad_ln2_gain, grad_ln2_bias,
    )


def solution(mesh):
    grid = Mesh(mesh.devices.reshape(2, 4, 2, 4, 2), ALL_AXES)
    rows = ("zh", "x", "c")
    sets = ("y", "zl")
    placed = (
        P(rows, None), P(), P(sets, None, rows), P(sets, None, rows), P(sets, None, None),
    ) + (P(),) * 17 + (P(ALL_AXES, None),)
    return jax.shard_map(
        per_device,
        mesh=grid,
        in_specs=placed,
        out_specs=(P(ALL_AXES, None), P(ALL_AXES, None)) + (P(),) * 17,
        check_vma=False,
    )
```

```python
import functools

import jax
import jax.numpy as jnp
from jax import lax
from jax.experimental import pallas as pl
from jax.experimental.pallas import tpu as pltpu
from jax.sharding import Mesh, PartitionSpec as P

BF = jnp.bfloat16
F32 = jnp.float32
HIGHEST = lax.Precision.HIGHEST
EPS_NORM = 1e-05
EPS_UNIT = 1e-06

D = 768
HEADS = 12
HEAD = 64
SETS = 8
BITS = 8
SLOTS = 256
FF = 3072
ROWS = 1280
BLOCK = 2560
OWN = 160
MEMBERS = 16
EDGE = 128
TOTAL = 20480
BLOCKS = 8
MESH = pl.DeviceIdType.MESH
CHUNK = 512
CHUNKS = BLOCK // CHUNK
ITEM = 80
CLASSES = 3
VMEM_LIMIT = 56 * 1024 * 1024

BLOCK_AXES = ("zh", "x")
MEMBER_AXES = ("c", "y", "zl")
ALL_AXES = BLOCK_AXES + MEMBER_AXES


def nt(left, right, **kw):
    return lax.dot_general(left, right, (((1,), (1,)), ((), ())), preferred_element_type=F32, **kw)


def nn(left, right, **kw):
    return lax.dot_general(left, right, (((1,), (0,)), ((), ())), preferred_element_type=F32, **kw)


def tn(left, right, **kw):
    return lax.dot_general(left, right, (((0,), (0,)), ((), ())), preferred_element_type=F32, **kw)


def unit_of(proj):
    scale = lax.rsqrt(jnp.sum(proj * proj, axis=0, keepdims=True) + EPS_UNIT)
    return proj * scale, scale


def bits_of(codes):
    return [(jnp.bitwise_and(codes, 1 << b) != 0) for b in range(BITS)]


def hash_weight(proj, codes, planes):
    unit, _ = unit_of(proj)
    lifted = nn(planes, unit, precision=HIGHEST)
    total = None
    for b, bit in enumerate(bits_of(codes)):
        part = lifted[b * SETS : (b + 1) * SETS]
        part = jnp.where(bit, part, -part)
        total = part if total is None else total + part
    return jnp.exp(total)


def hash_back(z_grad, proj, codes, planes):
    unit, scale = unit_of(proj)
    lifted_grad = jnp.concatenate([jnp.where(bit, z_grad, -z_grad) for bit in bits_of(codes)], axis=0)
    unit_grad = tn(planes, lifted_grad, precision=HIGHEST)
    return scale * (unit_grad - unit * jnp.sum(unit * unit_grad, axis=0, keepdims=True))


def one_hot(codes_row, weight_row):
    width = codes_row.shape[1]
    slots = lax.broadcasted_iota(jnp.int32, (SLOTS, width), 0)
    return jnp.where(slots == codes_row, weight_row, 0.0).astype(BF)


def fill_hot(hot_ref, codes, weights):
    for s in range(SETS):
        hot_ref[s * SLOTS : (s + 1) * SLOTS, :] = one_hot(codes[s : s + 1], weights[s : s + 1])


def by_item(sums, mass, masks):
    width = sums.shape[1]
    lead = lax.broadcasted_iota(jnp.int32, (ITEM - HEAD, width), 0) == 0
    tail = jnp.where(lead, mass, 0.0)
    whole = jnp.concatenate([sums, tail], axis=0)
    return jnp.concatenate([whole * masks[w : w + 1] for w in range(CLASSES)], axis=0).astype(BF)


def pick_item(stacked, masks):
    total = None
    for w in range(CLASSES):
        part = stacked[w * ITEM : (w + 1) * ITEM] * masks[w : w + 1]
        total = part if total is None else total + part
    return total


def circulant(base):
    grid = jnp.broadcast_to(base, (256, 256))
    grid = pltpu.roll(grid, 0, 1, stride=1, stride_axis=0)
    row = lax.broadcasted_iota(jnp.int32, (256, 256), 0)
    col = lax.broadcasted_iota(jnp.int32, (256, 256), 1)
    return (
        jnp.where(col < row, grid, 0.0).astype(BF),
        jnp.where(col >= row, grid, 0.0).astype(BF),
    )


def pack(rows, out, *lead):
    half = OWN // 2
    for p in range(MEMBERS):
        upper = rows[p * OWN : p * OWN + half]
        lower = rows[p * OWN + half : (p + 1) * OWN]
        out[(p, *lead)] = jnp.concatenate([upper, lower], axis=1).astype(BF)


def unpack(chunks, rows):
    half = OWN // 2
    for p in range(MEMBERS):
        both = chunks[p].astype(F32)
        rows[p * OWN : p * OWN + half] = both[:, :HEAD]
        rows[p * OWN + half : (p + 1) * OWN] = both[:, HEAD:]


def chunk_of(i, width=CHUNK, offset=0):
    return pl.ds(pl.multiple_of(i * width, 128) + offset, width)


def fill_kernel(tok, w_t, bias, planes, codes, masks, qkv, weights, long_out, short_out, hot, acc):
    acc[...] = jnp.zeros_like(acc)

    def step(i, _):
        cols = chunk_of(i)
        rows = pl.ds(pl.multiple_of(i * CHUNK, CHUNK), CHUNK)
        proj = nt(w_t[...], tok[rows, :]) + bias[...]
        qkv[:, cols] = proj
        q_codes = codes[0, :, cols]
        k_codes = codes[1, :, cols]
        q_w = hash_weight(proj[:HEAD], q_codes, planes[...])
        k_w = hash_weight(proj[HEAD : 2 * HEAD], k_codes, planes[...])
        weights[:, cols] = jnp.concatenate([q_w, k_w], axis=0)
        items = by_item(proj[2 * HEAD :], jnp.ones((1, CHUNK), F32), masks[:, cols])
        fill_hot(hot, k_codes, k_w)
        acc[...] += nt(items, hot[...])
        return 0

    lax.fori_loop(0, CHUNKS, step, 0)
    long_out[...] = acc[:ITEM].astype(BF)
    short_out[...] = acc[ITEM:].astype(BF)


def read_kernel(
    long_tab, short_tab, codes, weights, masks, value, before, after, v_bias, taps,
    attended, estimate, scale, hot, table, ext, rows_ref,
):
    table[:ITEM] = long_tab[...]
    table[ITEM:] = short_tab[...]
    ones = jnp.ones((1, EDGE), F32)
    ext[:, :EDGE] = by_item(before[...].astype(F32) + v_bias[...], ones, masks[:, :EDGE])
    ext[:, EDGE + BLOCK :] = by_item(after[...].astype(F32) + v_bias[...], ones, masks[:, EDGE + BLOCK :])

    def build(i, _):
        cols = chunk_of(i)
        inner = chunk_of(i, offset=EDGE)
        ext[:, inner] = by_item(value[:, cols] + v_bias[...], jnp.ones((1, CHUNK), F32), masks[:, inner])
        return 0

    lax.fori_loop(0, CHUNKS, build, 0)
    lower, upper = circulant(taps[...])

    def step(i, _):
        cols = chunk_of(i)
        inner = chunk_of(i, offset=EDGE)
        own = masks[:, inner]
        fill_hot(hot, codes[0, :, cols], weights[:SETS, cols])
        found = pick_item(nn(table[...], hot[...]), own)
        recip = 1.0 / (found[HEAD : HEAD + 1] + 1.0)
        est = (found[:HEAD] - v_bias[...]) * recip
        estimate[:, cols] = est
        scale[:, cols] = recip
        mixed = []
        for half in range(2):
            at = pl.multiple_of(i * CHUNK, 256) + half * 256
            mixed.append(nn(ext[:, pl.ds(at, 256)], lower) + nn(ext[:, pl.ds(at + 256, 256)], upper))
        conv = pick_item(jnp.concatenate(mixed, axis=1), own)[:HEAD]
        rows = pl.ds(pl.multiple_of(i * CHUNK, CHUNK), CHUNK)
        rows_ref[rows, :] = jnp.transpose(est + v_bias[...] + conv)
        return 0

    lax.fori_loop(0, CHUNKS, step, 0)
    pack(rows_ref, attended)


def read_back_kernel(
    chunks, estimate, scale, codes, weights, masks, long_out, short_out, grad, denom, hot, acc,
    grad_rows,
):
    acc[...] = jnp.zeros_like(acc)
    unpack(chunks, grad_rows)

    def step(i, _):
        cols = chunk_of(i)
        rows = pl.ds(pl.multiple_of(i * CHUNK, CHUNK), CHUNK)
        got = jnp.transpose(grad_rows[rows, :])
        grad[:, cols] = got
        numer = got * scale[:, cols]
        den = -jnp.sum(numer * estimate[:, cols], axis=0, keepdims=True)
        denom[:, cols] = den
        items = by_item(numer, den, masks[:, cols])
        fill_hot(hot, codes[0, :, cols], weights[:SETS, cols])
        acc[...] += nt(items, hot[...])
        return 0

    lax.fori_loop(0, CHUNKS, step, 0)
    long_out[...] = acc[:ITEM].astype(BF)
    short_out[...] = acc[ITEM:].astype(BF)


def query_back_kernel(
    long_tab, short_tab, grad, denom, scale, codes, weights, masks, query, planes, out, table
):
    table[:ITEM] = long_tab[...]
    table[ITEM:] = short_tab[...]

    def step(i, _):
        cols = chunk_of(i)
        own = masks[:, cols]
        q_codes = codes[0, :, cols]
        numer = grad[:, cols] * scale[:, cols]
        den = denom[:, cols]
        parts = []
        for s in range(SETS):
            hot = one_hot(q_codes[s : s + 1], 1.0)
            found = pick_item(nn(table[:, s * SLOTS : (s + 1) * SLOTS], hot), own)
            parts.append(
                jnp.sum(found[:HEAD] * numer, axis=0, keepdims=True) + found[HEAD : HEAD + 1] * den
            )
        z_grad = jnp.concatenate(parts, axis=0) * weights[:SETS, cols]
        out[:, cols] = hash_back(z_grad, query[:, cols], q_codes, planes[...]).astype(BF)
        return 0

    lax.fori_loop(0, CHUNKS, step, 0)


def key_back_kernel(
    long_tab, short_tab, grad, before, after, codes, weights, masks, qkv, v_before, v_after,
    planes, v_bias, taps_back, q_grad, tok,
    grad_out, w_out, b_out, taps_out, table, ext, v_ext, g_all, rows_ref,
):
    table[:ITEM] = long_tab[...]
    table[ITEM:] = short_tab[...]
    none = jnp.zeros((1, EDGE), F32)
    lo, hi = slice(None, EDGE), slice(EDGE + BLOCK, None)
    ext[:, lo] = by_item(before[...].astype(F32), none, masks[:, lo])
    ext[:, hi] = by_item(after[...].astype(F32), none, masks[:, hi])
    v_ext[:, lo] = by_item(v_before[...].astype(F32) + v_bias[...], none, masks[:, lo])
    v_ext[:, hi] = by_item(v_after[...].astype(F32) + v_bias[...], none, masks[:, hi])

    def build(i, _):
        cols = chunk_of(i)
        inner = chunk_of(i, offset=EDGE)
        zero = jnp.zeros((1, CHUNK), F32)
        ext[:, inner] = by_item(grad[:, cols], zero, masks[:, inner])
        v_ext[:, inner] = by_item(qkv[2 * HEAD :, cols] + v_bias[...], zero, masks[:, inner])
        return 0

    lax.fori_loop(0, CHUNKS, build, 0)
    lower, upper = circulant(taps_back[...])

    def step(i, carry):
        cols = chunk_of(i)
        inner = chunk_of(i, offset=EDGE)
        own = masks[:, inner]
        k_codes = codes[1, :, cols]
        k_w = weights[SETS:, cols]
        val = qkv[2 * HEAD :, cols]
        parts = []
        v_grad = jnp.zeros((HEAD, CHUNK), F32)
        for s in range(SETS):
            hot = one_hot(k_codes[s : s + 1], 1.0)
            found = pick_item(nn(table[:, s * SLOTS : (s + 1) * SLOTS], hot), own)
            parts.append(
                jnp.sum(found[:HEAD] * val, axis=0, keepdims=True) + found[HEAD : HEAD + 1]
            )
            v_grad = v_grad + found[:HEAD] * k_w[s : s + 1]
        z_grad = jnp.concatenate(parts, axis=0) * k_w
        k_grad = hash_back(z_grad, qkv[HEAD : 2 * HEAD, cols], k_codes, planes[...])
        mixed = []
        c_low, c_high = carry
        for half in range(2):
            at = pl.multiple_of(i * CHUNK, 256) + half * 256
            mixed.append(nn(ext[:, pl.ds(at, 256)], lower) + nn(ext[:, pl.ds(at + 256, 256)], upper))
            here = ext[:, pl.ds(at + EDGE, 256)]
            c_low = c_low + tn(v_ext[:, pl.ds(at, 256)], here)
            c_high = c_high + tn(v_ext[:, pl.ds(at + 256, 256)], here)
        v_grad = v_grad + pick_item(jnp.concatenate(mixed, axis=1), own)[:HEAD]
        g_all[:HEAD, cols] = q_grad[:, cols]
        g_all[HEAD : 2 * HEAD, cols] = k_grad.astype(BF)
        g_all[2 * HEAD :, cols] = v_grad.astype(BF)
        return c_low, c_high

    zeros = jnp.zeros((256, 256), F32)
    c_low, c_high = lax.fori_loop(0, CHUNKS, step, (zeros, zeros))
    row = lax.broadcasted_iota(jnp.int32, (256, 256), 0)
    col = lax.broadcasted_iota(jnp.int32, (256, 256), 1)
    skew = jnp.where(col < row, c_low, c_high)
    for b in range(8):
        skew = jnp.where(jnp.bitwise_and(row, 1 << b) != 0, pltpu.roll(skew, 256 - (1 << b), 1), skew)
    taps_out[...] = jnp.sum(skew, axis=0, keepdims=True)
    for k in range(3):
        rows_ref[...] = jnp.transpose(g_all[k * HEAD : (k + 1) * HEAD, :].astype(F32))
        pack(rows_ref, grad_out, k)
    w_grad = jnp.transpose(nn(g_all[...], tok[...]))
    w_out[:D] = w_grad[:, : 2 * HEAD].astype(BF)
    w_out[D:] = jnp.concatenate(
        [w_grad[: D // 2, 2 * HEAD :], w_grad[D // 2 :, 2 * HEAD :]], axis=1
    ).astype(BF)
    b_out[...] = jnp.sum(g_all[...].astype(F32), axis=1, keepdims=True)


def member_id(member):
    return {"c": member // 8, "y": (member % 8) // 2, "zl": member % 2}


def block_id(block):
    return {"zh": block // 4, "x": block % 4}


def owns(member):
    return (member < 8) | (member % 2 == ((member % 8) // 2) % 2)


def head_at(member):
    return jnp.where(member < 8, member, 8 + (member % 8) // 2)


def owner_of(head):
    return head if head < 8 else 8 + (head - 8) * 2 + (head - 8) % 2


def my_member():
    return lax.axis_index("c") * 8 + lax.axis_index("y") * 2 + lax.axis_index("zl")


def my_block():
    return lax.axis_index("zh") * 4 + lax.axis_index("x")


def greet(ids):
    barrier = pltpu.get_barrier_semaphore()
    for one in ids:
        pl.semaphore_signal(barrier, inc=1, device_id=one, device_id_type=MESH)
    pl.semaphore_wait(barrier, len(ids))


def send(src, dst, send_sem, recv_sem, device):
    return pltpu.make_async_remote_copy(
        src_ref=src, dst_ref=dst, send_sem=send_sem, recv_sem=recv_sem,
        device_id=device, device_id_type=MESH,
    )


def start_kernel(tokens, both, planes, tok_out, codes_out, planes_out, local, send_sem, recv_sem):
    me = my_member()
    core = lax.axis_index("c")
    mine = me % 8
    greet([member_id((me + d) % MEMBERS) for d in range(1, MEMBERS)])
    part = pl.ds(pl.multiple_of(core * ROWS, ROWS), ROWS)
    swap = send(tokens, tok_out.at[part], send_sem.at[32], recv_sem.at[32], member_id((me + 8) % MEMBERS))
    swap.start()
    keep = pltpu.make_async_copy(tokens, tok_out.at[part], local.at[0])
    keep.start()

    def codes_to(d):
        to = (me + d) % MEMBERS
        return to, send(
            both.at[head_at(to)], codes_out.at[me], send_sem.at[d], recv_sem.at[me], member_id(to)
        )

    def planes_to(d):
        to = core * 8 + (mine + d) % 8
        return send(planes, planes_out.at[mine], send_sem.at[16 + d], recv_sem.at[16 + mine], member_id(to))

    for d in range(1, MEMBERS):
        to, copy = codes_to(d)
        pl.when(owns(to))(copy.start)
    for d in range(1, 8):
        planes_to(d).start()
    own_codes = pltpu.make_async_copy(both.at[head_at(me)], codes_out.at[me], local.at[1])
    own_codes.start()
    own_planes = pltpu.make_async_copy(planes, planes_out.at[mine], local.at[2])
    own_planes.start()
    keep.wait()
    own_codes.wait()
    own_planes.wait()
    for d in range(1, MEMBERS):
        to, copy = codes_to(d)
        pl.when(owns(to))(copy.wait_send)
        came = (me + d) % MEMBERS
        got = send(both.at[0], codes_out.at[came], send_sem.at[d], recv_sem.at[came], member_id(came))
        pl.when(owns(me))(got.wait_recv)
    for d in range(1, 8):
        planes_to(d).wait_send()
        came = (mine + d) % 8
        send(
            planes, planes_out.at[came], send_sem.at[16 + d], recv_sem.at[16 + came],
            member_id(core * 8 + came),
        ).wait_recv()
    swap.wait_send()
    other = pl.ds(pl.multiple_of((1 - core) * ROWS, ROWS), ROWS)
    send(tokens, tok_out.at[other], send_sem.at[32], recv_sem.at[32], member_id((me + 8) % MEMBERS)).wait_recv()


def scatter_kernel(chunks, out, local, send_sem, recv_sem):
    me = my_member()
    greet([member_id((me + d) % MEMBERS) for d in range(1, MEMBERS)])
    owner = owns(me)
    mine = head_at(me)

    def to(d):
        dest = (me + d) % MEMBERS
        return send(chunks.at[dest], out.at[mine], send_sem.at[d], recv_sem.at[mine], member_id(dest))

    for d in range(1, MEMBERS):
        pl.when(owner)(to(d).start)
    keep = pltpu.make_async_copy(chunks.at[me], out.at[mine], local)
    pl.when(owner)(keep.start)
    for h in range(HEADS):
        at = owner_of(h)
        got = send(chunks.at[0], out.at[h], send_sem.at[0], recv_sem.at[h], member_id(at))
        pl.when(me != at)(got.wait_recv)
    for d in range(1, MEMBERS):
        pl.when(owner)(to(d).wait_send)
    pl.when(owner)(keep.wait)


def gather_kernel(chunks, out, local, send_sem, recv_sem):
    me = my_member()
    greet([member_id((me + d) % MEMBERS) for d in range(1, MEMBERS)])
    owner = owns(me)
    mine = head_at(me)

    def to(d):
        dest = (me + d) % MEMBERS
        copy = send(
            chunks.at[head_at(dest)], out.at[me], send_sem.at[d], recv_sem.at[me], member_id(dest)
        )
        return owns(dest), copy

    for d in range(1, MEMBERS):
        wanted, copy = to(d)
        pl.when(wanted)(copy.start)
    keep = pltpu.make_async_copy(chunks.at[mine], out.at[me], local)
    keep.start()
    for d in range(1, MEMBERS):
        came = (me + d) % MEMBERS
        got = send(chunks.at[0], out.at[came], send_sem.at[0], recv_sem.at[came], member_id(came))
        pl.when(owner)(got.wait_recv)
    for d in range(1, MEMBERS):
        wanted, copy = to(d)
        pl.when(wanted)(copy.wait_send)
    keep.wait()


def reduce_kernel(part, first, last, out, before, after, got, send_sem, recv_sem, halo_send, halo_recv):
    me = my_block()
    greet([block_id((me + d) % BLOCKS) for d in range(1, BLOCKS)])
    down, up = block_id((me + BLOCKS - 1) % BLOCKS), block_id((me + 1) % BLOCKS)

    def cols(k):
        return pl.ds(pl.multiple_of(k * SLOTS, SLOTS), SLOTS)

    def to_share(d):
        dest = (me + d) % BLOCKS
        return send(
            part.at[:, cols(dest)], got.at[d], send_sem.at[d], recv_sem.at[d], block_id(dest)
        )

    for d in range(1, BLOCKS):
        to_share(d).start()
    to_down = send(first, after, halo_send.at[0], halo_recv.at[0], down)
    to_up = send(last, before, halo_send.at[1], halo_recv.at[1], up)
    to_down.start()
    to_up.start()
    total = part[:, cols(me)].astype(F32)
    for d in range(1, BLOCKS):
        to_share(d).wait_recv()
        total = total + got[d].astype(F32)
    out[:, cols(me)] = total.astype(BF)

    def to_all(d):
        dest = (me + d) % BLOCKS
        return send(
            out.at[:, cols(me)], out.at[:, cols(me)], send_sem.at[BLOCKS + d], recv_sem.at[BLOCKS + d],
            block_id(dest),
        )

    for d in range(1, BLOCKS):
        to_all(d).start()
    for d in range(1, BLOCKS):
        came = (me + BLOCKS - d) % BLOCKS
        send(
            out.at[:, cols(came)], out.at[:, cols(came)], send_sem.at[BLOCKS + d],
            recv_sem.at[BLOCKS + d], block_id(came),
        ).wait_recv()
        to_share(d).wait_send()
        to_all(d).wait_send()
    to_down.wait()
    to_up.wait()


def norm_forward(values):
    centred = values - jnp.mean(values, axis=-1, keepdims=True)
    recip = lax.rsqrt(jnp.mean(centred * centred, axis=-1, keepdims=True) + EPS_NORM)
    return centred * recip, recip


def norm_backward(grad, hat, recip, gain):
    scaled = grad * gain
    mean = jnp.mean(scaled, axis=-1, keepdims=True)
    along = jnp.mean(scaled * hat, axis=-1, keepdims=True)
    return recip * (scaled - mean - hat * along)


def column_sums(values):
    return jnp.sum(values, axis=0, keepdims=True)


def ffn_kernel(
    att, tok, cot, w_out, w_in, w_back, b_out, ln1_gain, ln1_bias, b_in, b_back, ln2_gain, ln2_bias,
    output, resid, chunks, big, vec,
    w_out_v, w_in_v, w_back_v, act_v, slope_v, sems,
):
    loads = [
        pltpu.make_async_copy(a, b, sems.at[k])
        for k, (a, b) in enumerate([(w_out, w_out_v), (w_in, w_in_v), (w_back, w_back_v)])
    ]
    for load in loads:
        load.start()
    half = OWN // 2
    pairs = []
    for i in range(HEADS // 2):
        a, b = att[2 * i], att[2 * i + 1]
        top = jnp.concatenate([a[:, :HEAD], b[:, :HEAD]], axis=1)
        low = jnp.concatenate([a[:, HEAD:], b[:, HEAD:]], axis=1)
        pairs.append(jnp.concatenate([top, low], axis=0))
    attended = jnp.concatenate(pairs, axis=1)
    loads[0].wait()
    branch = nn(attended, w_out_v[...]) + b_out[...]
    hat1, recip1 = norm_forward(tok[...].astype(F32) + branch)
    hidden = hat1 * ln1_gain[...] + ln1_bias[...]
    hidden_low = hidden.astype(BF)
    loads[1].wait()
    outer = b_back[...]
    for k in range(FF // D):
        cols = slice(k * D, (k + 1) * D)
        inner = nn(hidden_low, w_in_v[:, cols]) + b_in[:, cols]
        phi = 0.5 * (1.0 + lax.erf(inner * (2.0**-0.5)))
        slope_v[:, cols] = phi + inner * (jnp.exp(-0.5 * inner * inner) * 0.3989422804014327)
        act = (inner * phi).astype(BF)
        act_v[:, cols] = act
        if k == 0:
            loads[2].wait()
        outer = outer + nn(act, w_back_v[cols, :])
    hat2, recip2 = norm_forward(hidden + outer)
    output[...] = hat2 * ln2_gain[...] + ln2_bias[...]
    got = cot[...]
    sum_grad = norm_backward(got, hat2, recip2, ln2_gain[...])
    outer_grad = sum_grad.astype(BF)
    hidden_grad = sum_grad
    sums = [column_sums(outer_grad.astype(F32)), column_sums(got * hat2), column_sums(got)]
    hidden_t = jnp.transpose(hidden).astype(BF)
    bias_rows = []
    for k in range(FF // D):
        cols = slice(k * D, (k + 1) * D)
        act_grad = nt(outer_grad, w_back_v[cols, :])
        inner_grad = (act_grad * slope_v[:, cols]).astype(BF)
        bias_rows.append(column_sums(inner_grad.astype(F32)))
        hidden_grad = hidden_grad + nt(inner_grad, w_in_v[:, cols])
        into = nn(hidden_t, inner_grad).astype(BF)
        back = nn(jnp.transpose(act_v[:, cols].astype(F32)).astype(BF), outer_grad).astype(BF)
        for side in range(2):
            lanes = slice(side * D // 2, (side + 1) * D // 2)
            big[2 * k + side] = into[:, lanes]
            big[8 + 2 * k + side] = back[:, lanes]
    grad1 = norm_backward(hidden_grad, hat1, recip1, ln1_gain[...])
    resid[...] = grad1
    branch_grad = grad1.astype(BF)
    att_grad = nt(branch_grad, w_out_v[...])
    for i in range(HEADS // 2):
        pair = att_grad[:, 2 * i * HEAD : 2 * (i + 1) * HEAD]
        for side in range(2):
            lanes = slice(side * HEAD, (side + 1) * HEAD)
            chunks[2 * i + side] = jnp.concatenate([pair[:half, lanes], pair[half:, lanes]], axis=1).astype(BF)
    into = nn(jnp.transpose(attended.astype(F32)).astype(BF), branch_grad).astype(BF)
    for side in range(2):
        big[16 + side] = into[:, side * D // 2 : (side + 1) * D // 2]
    rows = [column_sums(branch_grad.astype(F32)), column_sums(hidden_grad * hat1), column_sums(hidden_grad)]
    vec[...] = jnp.concatenate(rows + sums + bias_rows + [jnp.zeros((6, D), F32)], axis=0)


AXES = ("c", "x", "y", "z")
ORDERS = (("x", "y", "z"), ("y", "z", "x"), ("z", "x", "y"))
PARTS = 3
HALF_ROWS = 6912
PART_ROWS = HALF_ROWS // PARTS
QUARTER = PART_ROWS // 4
SIXTEENTH = QUARTER // 4
SHARE = 144
CUTS = ((0, 80), (80, 64))


def on_axis(axis, k):
    return {"zh": k // 2, "zl": k % 2} if axis == "z" else {axis: k}


def here():
    spot = {a: lax.axis_index(a) for a in ALL_AXES}
    spot["z"] = spot["zh"] * 2 + spot["zl"]
    return spot


class Slots:
    def __init__(self, send_sem, recv_sem):
        self.send_sem, self.recv_sem, self.used = send_sem, recv_sem, 0

    def take(self):
        k = self.used
        self.used += 1
        return self.send_sem.at[k], self.recv_sem.at[k]


class VectorSum:
    def __init__(self, spot, slots, value, buffer):
        self.spot, self.value, self.buffer, self.copies = spot, value, buffer, {}
        for stage, axis in enumerate(AXES):
            size = 2 if axis == "c" else 4
            self.copies[stage] = []
            for d in range(1, size):
                k = spot[axis]
                here_ref = buffer.at[stage, k]
                copy = send(here_ref, here_ref, *slots.take(), on_axis(axis, (k + d) % size))
                self.copies[stage].append(copy)

    def start(self, stage):
        self.buffer[stage, self.spot[AXES[stage]]] = self.value
        for copy in self.copies[stage]:
            copy.start()

    def finish(self, stage):
        for copy in self.copies[stage]:
            copy.wait()
        total = self.buffer[stage, 0] + self.buffer[stage, 1]
        if stage > 0:
            total = total + (self.buffer[stage, 2] + self.buffer[stage, 3])
        self.value = total


def add_rows(count, step, body):
    def one(i, _):
        body(pl.multiple_of(i * step, 16))
        return 0

    lax.fori_loop(0, count // step, one, 0)


class BigSum:
    def __init__(self, spot, slots, source, half, first, first_sum, second, third, result):
        self.spot, self.source, self.half, self.result = spot, source, half, result
        self.first, self.first_sum, self.second, self.third = first, first_sum, second, third
        c = spot["c"]
        self.copies = {}
        for a in range(PARTS):
            one, two, three = ORDERS[a]
            i, j, k = spot[one], spot[two], spot[three]
            away = self.rows((1 - c) * HALF_ROWS + a * PART_ROWS, PART_ROWS)
            inside = pl.ds(a * PART_ROWS, PART_ROWS)
            sibling = on_axis("c", 1 - c)
            self.copies[0, a] = [send(source.at[away], half.at[inside], *slots.take(), sibling)]
            self.copies[1, a] = []
            self.copies[2, a] = []
            self.copies[3, a] = []
            self.copies[4, a] = []
            self.copies[5, a] = []
            at = c * HALF_ROWS + a * PART_ROWS
            quarter = self.rows(at + i * QUARTER, QUARTER)
            own = self.rows(at + i * QUARTER + j * SIXTEENTH, SIXTEENTH)
            for d in range(1, 4):
                to = (i + d) % 4
                piece = half.at[self.rows(a * PART_ROWS + to * QUARTER, QUARTER)]
                self.copies[1, a].append(send(piece, first.at[a, d - 1], *slots.take(), on_axis(one, to)))
                to = (j + d) % 4
                piece = first_sum.at[a, self.rows(to * SIXTEENTH, SIXTEENTH)]
                self.copies[2, a].append(send(piece, second.at[a, d - 1], *slots.take(), on_axis(two, to)))
                to = (k + d) % 4
                piece = third.at[a, k]
                self.copies[3, a].append(send(piece, piece, *slots.take(), on_axis(three, to)))
                to = (j + d) % 4
                self.copies[4, a].append(send(result.at[own], result.at[own], *slots.take(), on_axis(two, to)))
                to = (i + d) % 4
                self.copies[5, a].append(
                    send(result.at[quarter], result.at[quarter], *slots.take(), on_axis(one, to))
                )
            whole = self.rows(at, PART_ROWS)
            self.copies[6, a] = [send(result.at[whole], result.at[whole], *slots.take(), sibling)]

    @staticmethod
    def rows(start, count):
        return pl.ds(pl.multiple_of(start, 16), count)

    def start(self, stage, a):
        for copy in self.copies[stage, a]:
            copy.start()

    def finish(self, stage, a):
        for copy in self.copies[stage, a]:
            copy.wait()
        spot = self.spot
        one, two, three = ORDERS[a]
        i, j, k = spot[one], spot[two], spot[three]
        at = spot["c"] * HALF_ROWS + a * PART_ROWS
        if stage == 0:

            def body(r):
                got = self.half[self.rows(a * PART_ROWS + r, 128)].astype(F32)
                mine = self.source[self.rows(at + r, 128)].astype(F32)
                self.half[self.rows(a * PART_ROWS + r, 128)] = (got + mine).astype(BF)

            add_rows(PART_ROWS, 128, body)
        if stage == 1:

            def body(r):
                total = self.half[self.rows(a * PART_ROWS + i * QUARTER + r, 96)].astype(F32)
                for d in range(3):
                    total = total + self.first[a, d, self.rows(r, 96)].astype(F32)
                self.first_sum[a, self.rows(r, 96)] = total.astype(BF)

            add_rows(QUARTER, 96, body)
        if stage == 2:
            total = self.first_sum[a, self.rows(j * SIXTEENTH, SIXTEENTH)].astype(F32)
            for d in range(3):
                total = total + self.second[a, d].astype(F32)
            self.third[a, k] = total.astype(BF)
        if stage == 3:
            low = self.third[a, 0].astype(F32) + self.third[a, 1].astype(F32)
            high = self.third[a, 2].astype(F32) + self.third[a, 3].astype(F32)
            own = self.rows(at + i * QUARTER + j * SIXTEENTH, SIXTEENTH)
            self.result[own] = (low + high).astype(BF)


class HeadSum:
    def __init__(self, spot, slots, source, got, even, odd):
        self.spot, self.source, self.got, self.even, self.odd = spot, source, got, even, odd
        c, x, y, zh, zl, z = (spot[a] for a in ("c", "x", "y", "zh", "zl", "z"))
        self.block = zh * 4 + x
        self.is_even, self.is_odd = c == 0, c == 1
        self.active = (c == 0) | (zl == y % 2)
        self.pieces = []
        for d in range(1, BLOCKS):
            to = (self.block + d) % BLOCKS
            piece = source.at[pl.ds(pl.multiple_of(to * SHARE, 16), SHARE)]
            self.pieces.append(send(piece, got.at[d - 1], *slots.take(), block_id(to)))
        self.copies = {}
        for side, (ref, count) in enumerate(((even, 0), (odd, 1))):
            def region(zh_, zl_, x_, y_, lo, n, ref=ref, side=side):
                spots = (zh_, zl_, x_, y_) if side == 0 else (zh_, x_, y_)
                return ref.at[(*spots, pl.ds(lo, n))]

            all2, all4 = slice(None), slice(None)
            self.copies[0, side] = [
                send(region(zh, zl, x, y, 0, SHARE), region(zh, zl, x, y, 0, SHARE), *slots.take(),
                     on_axis("z", (z + d) % 4))
                for d in range(1, 4)
            ]
            for part, (lo, n) in enumerate(CUTS):
                axes = ("x", "y") if part == 0 else ("y", "x")
                two = region(all2, all2, x, y, lo, n)
                if axes[1] == "y":
                    three = region(all2, all2, all4, y, lo, n)
                else:
                    three = region(all2, all2, x, all4, lo, n)
                for stage, piece in ((1, two), (2, three)):
                    axis = axes[stage - 1]
                    self.copies[stage, side, part] = [
                        send(piece, piece, *slots.take(), on_axis(axis, (spot[axis] + d) % 4))
                        for d in range(1, 4)
                    ]
                whole = region(all2, all2, all4, all4, lo, n)
                self.copies[3, side, part] = [send(whole, whole, *slots.take(), on_axis("c", 1 - c))]

    def start_sum(self):
        for copy in self.pieces:
            pl.when(self.active)(copy.start)

    def finish_sum(self):
        spot = self.spot

        def body():
            for copy in self.pieces:
                copy.wait()
            total = self.source[pl.ds(pl.multiple_of(self.block * SHARE, 16), SHARE)].astype(F32)
            for d in range(BLOCKS - 1):
                total = total + self.got[d].astype(F32)
            total = total.astype(BF)

            def keep_even():
                self.even[spot["zh"], spot["zl"], spot["x"], spot["y"]] = total

            def keep_odd():
                self.odd[spot["zh"], spot["x"], spot["y"]] = total

            pl.when(self.is_even)(keep_even)
            pl.when(self.is_odd)(keep_odd)

        pl.when(self.active)(body)

    def start_z(self):
        def even():
            for copy in self.copies[0, 0]:
                copy.start()

        def odd():
            for copy in self.copies[0, 1]:
                copy.start()

        pl.when(self.is_even)(even)
        pl.when(self.is_odd & self.active)(odd)

    def finish_z(self):
        def even():
            for copy in self.copies[0, 0]:
                copy.wait()

        def odd_send():
            for copy in self.copies[0, 1]:
                copy.wait_send()

        pl.when(self.is_even)(even)
        pl.when(self.is_odd & self.active)(odd_send)
        for d in range(1, 4):
            came = (self.spot["z"] + 4 - d) % 4
            sent = self.is_odd & (came % 2 == self.spot["y"] % 2)
            pl.when(sent)(self.copies[0, 1][d - 1].wait_recv)

    def start(self, stage, part):
        for side, mine in enumerate((self.is_even, self.is_odd)):

            def go(side=side):
                for copy in self.copies[stage, side, part]:
                    copy.start()

            pl.when(mine)(go)

    def finish(self, stage, part):
        for side, mine in enumerate((self.is_even, self.is_odd)):

            def go(side=side):
                for copy in self.copies[stage, side, part]:
                    copy.wait()

            pl.when(mine)(go)

    def start_core(self, part):
        for side, mine in enumerate((self.is_even, self.is_odd)):
            pl.when(mine)(self.copies[3, side, part][0].start)

    def finish_core(self, part):
        for side, mine in enumerate((self.is_even, self.is_odd)):
            pl.when(mine)(self.copies[3, side, part][0].wait_send)
            pl.when(~mine)(self.copies[3, side, part][0].wait_recv)


def sum_peers(spot):
    ids = [on_axis("c", 1 - spot["c"])]
    for axis in ("x", "y", "z"):
        ids += [on_axis(axis, (spot[axis] + d) % 4) for d in range(1, 4)]
    ids += [{"zh": 1 - spot["zh"], "x": (spot["x"] + d) % 4} for d in range(1, 4)]
    return ids


BIG_SLOTS = PARTS * (1 + 5 * 3 + 1)
HEAD_SLOTS = 7 + 2 * (3 + 2 * (3 + 3 + 1))
VEC_SLOTS = 1 + 3 * 3


def weight_kernel(
    big, vec, head_w, big_out, vec_out, even, odd,
    half, first, first_sum, second, third, got, vec_buf, send_sem, recv_sem,
):
    spot = here()
    greet(sum_peers(spot))
    slots = Slots(send_sem, recv_sem)
    sums = BigSum(spot, slots, big, half, first, first_sum, second, third, big_out)
    heads = HeadSum(spot, slots, head_w, got, even, odd)
    vector = VectorSum(spot, slots, vec[...], vec_buf)
    parts = range(PARTS)
    for a in parts:
        sums.start(0, a)
    heads.start_sum()
    vector.start(0)
    for a in parts:
        sums.finish(0, a)
        sums.start(1, a)
    vector.finish(0)
    vector.start(1)
    heads.finish_sum()
    heads.start_z()
    for a in parts:
        sums.finish(1, a)
        sums.start(2, a)
    vector.finish(1)
    vector.start(2)
    heads.finish_z()
    for part in range(2):
        heads.start(1, part)
    for a in parts:
        sums.finish(2, a)
        sums.start(3, a)
    vector.finish(2)
    vector.start(3)
    for a in parts:
        sums.finish(3, a)
        sums.start(4, a)
    vector.finish(3)
    vec_out[...] = vector.value
    for part in range(2):
        heads.finish(1, part)
        heads.start(2, part)
    for a in parts:
        sums.finish(4, a)
        sums.start(5, a)
    for part in range(2):
        heads.finish(2, part)
        heads.start_core(part)
    for a in parts:
        sums.finish(5, a)
        sums.start(6, a)
    for part in range(2):
        heads.finish_core(part)
    for a in parts:
        sums.finish(6, a)


def call(kernel, outs, scratch, *args):
    return pl.pallas_call(
        kernel,
        out_shape=[jax.ShapeDtypeStruct(shape, kind) for shape, kind in outs],
        in_specs=[pl.BlockSpec(memory_space=pltpu.VMEM)] * len(args),
        out_specs=[pl.BlockSpec(memory_space=pltpu.VMEM)] * len(outs),
        scratch_shapes=[pltpu.VMEM(shape, kind) for shape, kind in scratch],
        compiler_params=pltpu.CompilerParams(vmem_limit_bytes=VMEM_LIMIT),
    )(*args)


def talk(kernel, ident, outs, scratch, *args):
    return pl.pallas_call(
        kernel,
        out_shape=[jax.ShapeDtypeStruct(shape, kind) for shape, kind in outs],
        in_specs=[pl.BlockSpec(memory_space=pltpu.VMEM)] * len(args),
        out_specs=[pl.BlockSpec(memory_space=pltpu.VMEM)] * len(outs),
        scratch_shapes=scratch,
        compiler_params=pltpu.CompilerParams(
            collective_id=ident, has_side_effects=True, vmem_limit_bytes=VMEM_LIMIT
        ),
    )(*args)


def local_call(kernel, outs, scratch, far, *args):
    return pl.pallas_call(
        kernel,
        out_shape=[jax.ShapeDtypeStruct(shape, kind) for shape, kind in outs],
        in_specs=[
            pl.BlockSpec(memory_space=pl.ANY if k in far else pltpu.VMEM) for k in range(len(args))
        ],
        out_specs=[pl.BlockSpec(memory_space=pltpu.VMEM)] * len(outs),
        scratch_shapes=scratch,
        compiler_params=pltpu.CompilerParams(vmem_limit_bytes=VMEM_LIMIT),
    )(*args)


def dma(count):
    return pltpu.SemaphoreType.DMA((count,))


def all_to_members(array, ident):
    shape = (HEADS,) + array.shape[1:]
    (out,) = talk(scatter_kernel, ident, [(shape, BF)], [pltpu.SemaphoreType.DMA, dma(16), dma(16)], array)
    return out


def all_to_owners(array, ident):
    shape = (MEMBERS,) + array.shape[1:]
    (out,) = talk(gather_kernel, ident, [(shape, BF)], [pltpu.SemaphoreType.DMA, dma(16), dma(16)], array)
    return out


def sum_blocks(part, first, last, ident):
    edge = ((HEAD, EDGE), BF)
    return talk(
        reduce_kernel, ident, [((ITEM, SETS * SLOTS), BF), edge, edge],
        [pltpu.VMEM((BLOCKS, ITEM, SLOTS), BF), dma(2 * BLOCKS), dma(2 * BLOCKS), dma(2), dma(2)],
        part, first, last,
    )


def item_masks(cuts, block):
    start = block * BLOCK - EDGE
    pos = start + jnp.arange(BLOCK + 2 * EDGE, dtype=jnp.int32)
    item = jnp.sum((pos[None, :] >= cuts[:, None]).astype(jnp.int32), axis=0) - 1
    longest = jnp.where(cuts[2] - cuts[1] > 1024, 1, 2)
    first_half = block < 4
    outer = jnp.where(first_half, 0, 3)
    inner = jnp.where(first_half, 1, 2)
    valid = (pos >= 0) & (pos < TOTAL)
    is_long = valid & (item == longest)
    is_outer = valid & (item == outer)
    is_inner = valid & (item == inner) & (inner != longest)
    none = jnp.zeros_like(is_long)
    return jnp.stack([is_long, is_outer, is_inner] + [none] * 5).astype(F32)


def per_device(
    tokens, item_cuts, q_codes, k_codes, hyperplanes, w_query, b_query, w_key, b_key,
    w_value, b_value, conv_weight, w_out, b_out, ln1_gain, ln1_bias, w_in, b_in, w_back,
    b_back, ln2_gain, ln2_bias, cotangent,
):
    block = lax.axis_index(BLOCK_AXES)
    member = lax.axis_index(MEMBER_AXES)
    hash_at = lax.axis_index(("y", "zl"))
    head = head_at(member)
    both = jnp.concatenate([q_codes, k_codes], axis=0).transpose(1, 0, 2)
    tok, both, planes = talk(
        start_kernel, 0,
        [((BLOCK, D), BF), ((MEMBERS, 2, ROWS), jnp.int32), ((SETS, BITS, HEAD), F32)],
        [dma(3), dma(33), dma(33)],
        tokens, both, hyperplanes[0].T,
    )
    codes = both.reshape(2, SETS, 2, ROWS).transpose(2, 1, 0, 3).reshape(2, SETS, BLOCK)
    planes = planes.transpose(1, 0, 2).reshape(BITS * SETS, HEAD)
    masks = item_masks(item_cuts, block)
    own_masks = masks[:, EDGE : EDGE + BLOCK]

    def head_cols(weight):
        return lax.dynamic_slice_in_dim(weight, head * HEAD, HEAD, 1).T

    def head_bias(bias):
        return lax.dynamic_slice_in_dim(bias, head * HEAD, HEAD, 0)[:, None]

    w_t = jnp.concatenate([head_cols(w) for w in (w_query, w_key, w_value)], axis=0)
    v_bias = head_bias(b_value)
    bias_t = jnp.concatenate([head_bias(b_query), head_bias(b_key), jnp.zeros_like(v_bias)], axis=0)
    taps = lax.dynamic_slice_in_dim(conv_weight, head, 1, 0)
    taps_fwd = jnp.pad(taps[:, ::-1], ((0, 0), (96, 95)))
    taps_bwd = jnp.pad(taps, ((0, 0), (96, 95)))

    hot = ((SETS * SLOTS, CHUNK), BF)
    acc = ((CLASSES * ITEM, SETS * SLOTS), F32)
    table = ((CLASSES * ITEM, SETS * SLOTS), BF)
    ext = ((CLASSES * ITEM, BLOCK + 2 * EDGE), BF)
    rows_f32 = ((BLOCK, HEAD), F32)
    long_shape = ((ITEM, SETS * SLOTS), BF)
    short_shape = (((CLASSES - 1) * ITEM, SETS * SLOTS), BF)

    qkv, weights, long_part, short_tab = call(
        fill_kernel,
        [((3 * HEAD, BLOCK), F32), ((2 * SETS, BLOCK), F32), long_shape, short_shape],
        [hot, acc],
        tok, w_t, bias_t, planes, codes, own_masks,
    )
    value = qkv[2 * HEAD :]
    long_tab, v_before, v_after = sum_blocks(
        long_part, value[:, :EDGE].astype(BF), value[:, -EDGE:].astype(BF), 1
    )
    att_rows, estimate, scale = call(
        read_kernel,
        [((MEMBERS, OWN // 2, 2 * HEAD), BF), ((HEAD, BLOCK), F32), ((1, BLOCK), F32)],
        [hot, table, ext, rows_f32],
        long_tab, short_tab, codes, weights, masks, value, v_before, v_after, v_bias, taps_fwd,
    )
    att = all_to_members(att_rows, 2)
    own_tokens = lax.dynamic_slice_in_dim(tokens, hash_at * OWN, OWN, 0)
    output, resid_grad, grad_chunks, big, vec = local_call(
        ffn_kernel,
        [
            ((OWN, D), F32), ((OWN, D), F32), ((HEADS, OWN // 2, 2 * HEAD), BF), ((18, D, D // 2), BF),
            ((16, D), F32),
        ],
        [
            pltpu.VMEM((D, D), BF), pltpu.VMEM((D, FF), BF), pltpu.VMEM((FF, D), BF), pltpu.VMEM((OWN, FF), BF),
            pltpu.VMEM((OWN, FF), F32), dma(3),
        ],
        (3, 4, 5),
        att, own_tokens, cotangent, w_out, w_in, w_back, b_out[None], ln1_gain[None], ln1_bias[None],
        b_in[None], b_back[None], ln2_gain[None], ln2_bias[None],
    )
    grad_rows = all_to_owners(grad_chunks, 3)
    long_gpart, short_gtab, grad_t, denom = call(
        read_back_kernel,
        [long_shape, short_shape, ((HEAD, BLOCK), F32), ((1, BLOCK), F32)],
        [hot, acc, rows_f32],
        grad_rows, estimate, scale, codes, weights, own_masks,
    )
    long_gtab, g_before, g_after = sum_blocks(
        long_gpart, grad_t[:, :EDGE].astype(BF), grad_t[:, -EDGE:].astype(BF), 1
    )
    (q_grad,) = call(
        query_back_kernel,
        [((HEAD, BLOCK), BF)],
        [table],
        long_tab, short_tab, grad_t, denom, scale, codes, weights, own_masks, qkv[:HEAD], planes,
    )
    grad_qkv, head_w, head_b, head_taps = call(
        key_back_kernel,
        [((MEMBERS, 3, OWN // 2, 2 * HEAD), BF), ((D + D // 2, 2 * HEAD), BF), ((3 * HEAD, 1), F32), ((1, 256), F32)],
        [table, ext, ext, ((3 * HEAD, BLOCK), BF), rows_f32],
        long_gtab, short_gtab, grad_t, g_before, g_after, codes, weights, masks, qkv,
        v_before, v_after, planes, v_bias, taps_bwd, q_grad, tok,
    )

    lows = all_to_members(grad_qkv, 4)
    lows = lows.reshape(HEADS, 3, OWN // 2, 2, HEAD).transpose(1, 3, 2, 0, 4).reshape(3, OWN, D)
    grad_tokens = resid_grad + nt(lows[0], w_query) + nt(lows[1], w_key) + nt(lows[2], w_value)

    small = jnp.concatenate([head_b[:, 0], head_taps[0, 96:161][::-1]])
    small = jnp.pad(small, (0, D // 2 - small.shape[0]))
    row = lax.broadcasted_iota(jnp.int32, (16, D // 2), 0)
    small = jnp.where((row == head) & owns(member), small[None], 0.0)
    wide = D + D // 2
    big_sum, vec_sum, even, odd = talk(
        weight_kernel, 5,
        [
            ((18 * D, D // 2), BF), ((16, wide), F32), ((2, 2, 4, 4, SHARE, 128), BF),
            ((2, 4, 4, SHARE, 128), BF),
        ],
        [
            pltpu.VMEM((HALF_ROWS, D // 2), BF), pltpu.VMEM((PARTS, 3, QUARTER, D // 2), BF),
            pltpu.VMEM((PARTS, QUARTER, D // 2), BF), pltpu.VMEM((PARTS, 3, SIXTEENTH, D // 2), BF),
            pltpu.VMEM((PARTS, 4, SIXTEENTH, D // 2), BF), pltpu.VMEM((BLOCKS - 1, SHARE, 128), BF),
            pltpu.VMEM((4, 4, 16, wide), F32), dma(BIG_SLOTS + HEAD_SLOTS + VEC_SLOTS),
            dma(BIG_SLOTS + HEAD_SLOTS + VEC_SLOTS),
        ],
        big.reshape(18 * D, D // 2), jnp.concatenate([vec, small], axis=1), head_w,
    )
    by_head = jnp.concatenate(
        [
            even.transpose(3, 1, 0, 2, 4, 5).reshape(8, D + D // 2, 2 * HEAD),
            odd.transpose(2, 0, 1, 3, 4).reshape(4, D + D // 2, 2 * HEAD),
        ]
    )
    two = by_head[:, :D].reshape(HEADS, D, 2, HEAD).transpose(2, 1, 0, 3).reshape(2, D, D)
    last = by_head[:, D:].reshape(HEADS, D // 2, 2, HEAD).transpose(2, 1, 0, 3).reshape(D, D)
    heads_w = (two[0].astype(F32), two[1].astype(F32), last.astype(F32))
    heads_small = vec_sum[:HEADS, D:]
    heads_b = heads_small[:, : 3 * HEAD].reshape(HEADS, 3, HEAD).transpose(1, 0, 2).reshape(3, D)
    grad_conv_weight = heads_small[:, 3 * HEAD : 3 * HEAD + 65]
    big_sum = big_sum.reshape(18, D, D // 2)
    grad_w_in = big_sum[:8].transpose(1, 0, 2).reshape(D, FF).astype(F32)
    grad_w_back = big_sum[8:16].reshape(4, 2, D, D // 2).transpose(0, 2, 1, 3).reshape(FF, D).astype(F32)
    grad_w_out = big_sum[16:].transpose(1, 0, 2).reshape(D, D).astype(F32)
    vectors = vec_sum[:, :D]
    grad_b_out, grad_ln1_gain, grad_ln1_bias, grad_b_back, grad_ln2_gain, grad_ln2_bias = (
        vectors[k] for k in range(6)
    )
    grad_b_in = vectors[6:10].reshape(FF)
    return (
        output, grad_tokens, heads_w[0], heads_b[0], heads_w[1], heads_b[1], heads_w[2], heads_b[2],
        grad_conv_weight, grad_w_out, grad_b_out, grad_ln1_gain, grad_ln1_bias, grad_w_in, grad_b_in,
        grad_w_back, grad_b_back, grad_ln2_gain, grad_ln2_bias,
    )


def solution(mesh):
    grid = Mesh(mesh.devices.reshape(2, 4, 2, 4, 2), ALL_AXES)
    rows = ("zh", "x", "c")
    sets = ("y", "zl")
    placed = (
        P(rows, None), P(), P(sets, None, rows), P(sets, None, rows), P(sets, None, None),
    ) + (P(),) * 17 + (P(ALL_AXES, None),)
    return jax.shard_map(
        per_device,
        mesh=grid,
        in_specs=placed,
        out_specs=(P(ALL_AXES, None), P(ALL_AXES, None)) + (P(),) * 17,
        check_vma=False,
    )
```

```python
import jax
import jax.numpy as jnp
from jax import lax
from jax.experimental import pallas as pl
from jax.experimental.pallas import tpu as pltpu
from jax.sharding import Mesh, PartitionSpec as P

BF = jnp.bfloat16
F32 = jnp.float32
I32 = jnp.int32
HIGHEST = lax.Precision.HIGHEST
MESH = pl.DeviceIdType.MESH
EPS_NORM = 1e-05
EPS_UNIT = 1e-06

D = 768
HEADS = 12
HEAD = 64
SETS = 8
BITS = 8
SLOTS = 256
TABLE = SETS * SLOTS
FF = 3072
ROWS = 1280
BLOCK = 2560
BLOCKS = 8
OWN = 160
SIDE = OWN // 2
MEMBERS = 16
EDGE = 128
EXT = BLOCK + 2 * EDGE
TOTAL = 20480
CHUNK = 640
CHUNKS = BLOCK // CHUNK
PER_CHUNK = CHUNK // OWN
ITEM = 80
CLASSES = 3
STACK = ITEM * CLASSES
SHARE = 144
HEAD_ROWS = D + D // 2
SMALL = 512
WIDE = FF + D
VMEM_LIMIT = 58 * 1024 * 1024

BLOCK_AXES = ("zh", "x")
ALL_AXES = ("zh", "x", "c", "y", "zl")


def nt(left, right, **kw):
    return lax.dot_general(left, right, (((1,), (1,)), ((), ())), preferred_element_type=F32, **kw)


def nn(left, right, **kw):
    return lax.dot_general(left, right, (((1,), (0,)), ((), ())), preferred_element_type=F32, **kw)


def tn(left, right, **kw):
    return lax.dot_general(left, right, (((0,), (0,)), ((), ())), preferred_element_type=F32, **kw)


def unit_of(proj):
    scale = lax.rsqrt(jnp.sum(proj * proj, axis=0, keepdims=True) + EPS_UNIT)
    return proj * scale, scale


def bits_of(codes):
    return [(jnp.bitwise_and(codes, 1 << b) != 0) for b in range(BITS)]


def hash_weight(proj, codes, planes):
    unit, _ = unit_of(proj)
    lifted = nn(planes, unit, precision=HIGHEST)
    total = None
    for b, bit in enumerate(bits_of(codes)):
        part = lifted[b * SETS : (b + 1) * SETS]
        part = jnp.where(bit, part, -part)
        total = part if total is None else total + part
    return jnp.exp(total)


def hash_back(z_grad, proj, codes, planes):
    unit, scale = unit_of(proj)
    lifted_grad = jnp.concatenate([jnp.where(bit, z_grad, -z_grad) for bit in bits_of(codes)], axis=0)
    unit_grad = tn(planes, lifted_grad, precision=HIGHEST)
    return scale * (unit_grad - unit * jnp.sum(unit * unit_grad, axis=0, keepdims=True))


def one_hot(codes_row, weight_row):
    width = codes_row.shape[1]
    slots = lax.broadcasted_iota(jnp.int32, (SLOTS, width), 0)
    return jnp.where(slots == codes_row, weight_row, 0.0).astype(BF)


def by_item(sums, mass, masks):
    width = sums.shape[1]
    lead = lax.broadcasted_iota(jnp.int32, (ITEM - HEAD, width), 0) == 0
    tail = jnp.where(lead, mass, 0.0)
    whole = jnp.concatenate([sums, tail], axis=0)
    return jnp.concatenate([whole * masks[w : w + 1] for w in range(CLASSES)], axis=0).astype(BF)


def pick_item(stacked, masks):
    total = None
    for w in range(CLASSES):
        part = stacked[w * ITEM : (w + 1) * ITEM] * masks[w : w + 1]
        total = part if total is None else total + part
    return total


def circulant(base):
    grid = jnp.broadcast_to(base, (256, 256))
    grid = pltpu.roll(grid, 0, 1, stride=1, stride_axis=0)
    row = lax.broadcasted_iota(jnp.int32, (256, 256), 0)
    col = lax.broadcasted_iota(jnp.int32, (256, 256), 1)
    return (
        jnp.where(col < row, grid, 0.0).astype(BF),
        jnp.where(col >= row, grid, 0.0).astype(BF),
    )


def member_id(member):
    return {"c": member // 8, "y": (member % 8) // 2, "zl": member % 2}


def block_id(block):
    return {"zh": block // 4, "x": block % 4}


def owns(member):
    return (member < 8) | (member % 2 == ((member % 8) // 2) % 2)


def head_at(member):
    return jnp.where(member < 8, member, 8 + (member % 8) // 2)


def owner_of(head):
    return head if head < 8 else 8 + (head - 8) * 2 + (head - 8) % 2


def my_member():
    return lax.axis_index("c") * 8 + lax.axis_index("y") * 2 + lax.axis_index("zl")


def my_block():
    return lax.axis_index("zh") * 4 + lax.axis_index("x")


def send(src, dst, send_sem, recv_sem, device):
    return pltpu.make_async_remote_copy(
        src_ref=src, dst_ref=dst, send_sem=send_sem, recv_sem=recv_sem,
        device_id=device, device_id_type=MESH,
    )


def on_axis(axis, k):
    return {"zh": k // 2, "zl": k % 2} if axis == "z" else {axis: k}


def here():
    spot = {a: lax.axis_index(a) for a in ALL_AXES}
    spot["z"] = spot["zh"] * 2 + spot["zl"]
    return spot


class Slots:
    def __init__(self, send_sem, recv_sem):
        self.send_sem, self.recv_sem, self.used = send_sem, recv_sem, 0

    def take(self):
        k = self.used
        self.used += 1
        return self.send_sem.at[k], self.recv_sem.at[k]


AXES = ("c", "x", "y", "z")
ORDERS = (("x", "y", "z"), ("y", "z", "x"), ("z", "x", "y"))
PARTS = 3
CUTS = ((0, 80), (80, 64))
VEC_SLOTS = 1 + 3 * 3


class VectorSum:
    def __init__(self, spot, slots, value, buffer):
        self.spot, self.value, self.buffer, self.copies = spot, value, buffer, {}
        for stage, axis in enumerate(AXES):
            size = 2 if axis == "c" else 4
            self.copies[stage] = []
            for d in range(1, size):
                k = spot[axis]
                here_ref = buffer.at[stage, k]
                copy = send(here_ref, here_ref, *slots.take(), on_axis(axis, (k + d) % size))
                self.copies[stage].append(copy)

    def start(self, stage):
        self.buffer[stage, self.spot[AXES[stage]]] = self.value
        for copy in self.copies[stage]:
            copy.start()

    def finish(self, stage):
        for copy in self.copies[stage]:
            copy.wait()
        total = self.buffer[stage, 0] + self.buffer[stage, 1]
        if stage > 0:
            total = total + (self.buffer[stage, 2] + self.buffer[stage, 3])
        self.value = total


def hello(ids):
    barrier = pltpu.get_barrier_semaphore()
    for one in ids:
        pl.semaphore_signal(barrier, inc=1, device_id=one, device_id_type=MESH)


def all_here(count):
    pl.semaphore_wait(pltpu.get_barrier_semaphore(), count)


def every(count, step, body):
    def one(i, _):
        body(pl.multiple_of(i * step, 16))
        return 0

    lax.fori_loop(0, count // step, one, 0)


def span(start, size, unit=128):
    return pl.ds(pl.multiple_of(start, unit), size)


class Matrix:
    def __init__(self, shape, row_cut, refs=None):
        self.rows, self.cols = shape
        self.half = self.rows // 2
        self.part = self.cols // PARTS
        self.quarter = self.half // 4
        self.row_cut = row_cut
        self.col_cut = 4 // row_cut
        self.small = (self.quarter // row_cut, self.part // self.col_cut)
        self.step = 32 if self.part > 512 else 128
        self.quarter_step = 16 if self.part > 512 else 96
        if refs is not None:
            (
                self.source, self.result, self.acc, self.other, self.first, self.first_sum, self.second,
                self.third, self.own,
            ) = refs

    def scratch(self):
        big = (self.half, self.cols)
        quarter = (self.quarter, self.part)
        shapes = [
            big, big, (PARTS, 3, *quarter), (PARTS, *quarter), (PARTS, 3, *self.small), (PARTS, 4, *self.small),
            (PARTS, *self.small),
        ]
        return [pltpu.VMEM(shape, BF) for shape in shapes]

    def lanes(self, a):
        return pl.ds(a * self.part, self.part)

    def spot16(self, j):
        return (j // self.col_cut) * self.small[0], (j % self.col_cut) * self.small[1]


MATRICES = (((D, WIDE), 2), ((FF, D), 4))
BIG_SLOTS = 2 * PARTS * (1 + 5 * 3 + 1)


class BigSum:
    def __init__(self, spot, slots, local, mats):
        self.spot, self.mats, self.local = spot, mats, local
        c = spot["c"]
        sibling = on_axis("c", 1 - c)
        self.copies = {(stage, a): [] for stage in range(7) for a in range(PARTS)}
        self.keeps = {}
        self.loads = []
        for t, m in enumerate(mats):
            own_rows = span(c * m.half, m.half, 16)
            away_rows = span((1 - c) * m.half, m.half, 16)
            self.loads.append(pltpu.make_async_copy(m.source.at[own_rows], m.acc, local.at[t]))
            for a in range(PARTS):
                one, two, three = ORDERS[a]
                i, j, k = spot[one], spot[two], spot[three]
                lanes = m.lanes(a)
                self.copies[0, a].append(
                    send(m.source.at[away_rows, lanes], m.other.at[:, lanes], *slots.take(), sibling)
                )
                row, lane = m.spot16(j)
                at = (
                    span(c * m.half + i * m.quarter + row, m.small[0], 16),
                    span(a * m.part + lane, m.small[1]),
                )
                quarter = (span(c * m.half + i * m.quarter, m.quarter, 16), lanes)
                self.keeps[t, a] = pltpu.make_async_copy(m.own.at[a], m.result.at[at], local.at[2 + t * PARTS + a])
                for d in range(1, 4):
                    to = (i + d) % 4
                    piece = m.acc.at[span(to * m.quarter, m.quarter, 16), lanes]
                    self.copies[1, a].append(send(piece, m.first.at[a, d - 1], *slots.take(), on_axis(one, to)))
                    to = (j + d) % 4
                    row, lane = m.spot16(to)
                    piece = m.first_sum.at[a, span(row, m.small[0], 16), span(lane, m.small[1])]
                    self.copies[2, a].append(send(piece, m.second.at[a, d - 1], *slots.take(), on_axis(two, to)))
                    piece = m.third.at[a, k]
                    self.copies[3, a].append(send(piece, piece, *slots.take(), on_axis(three, (k + d) % 4)))
                    self.copies[4, a].append(
                        send(m.own.at[a], m.result.at[at], *slots.take(), on_axis(two, (j + d) % 4))
                    )
                    piece = m.result.at[quarter]
                    self.copies[5, a].append(send(piece, piece, *slots.take(), on_axis(one, (i + d) % 4)))
                whole = m.result.at[own_rows, lanes]
                self.copies[6, a].append(send(whole, whole, *slots.take(), sibling))

    def load(self):
        for copy in self.loads:
            copy.start()

    def loaded(self):
        for copy in self.loads:
            copy.wait()

    def start(self, stage, a):
        for copy in self.copies[stage, a]:
            copy.start()

    def finish(self, stage, a):
        for copy in self.copies[stage, a]:
            copy.wait()
        spot = self.spot
        one, two, three = ORDERS[a]
        i, j, k = spot[one], spot[two], spot[three]
        for t, m in enumerate(self.mats):
            lanes = m.lanes(a)
            if stage == 0:

                def add_half(r, m=m, lanes=lanes):
                    here_ = (pl.ds(r, m.step), lanes)
                    m.acc[here_] = (m.acc[here_].astype(F32) + m.other[here_].astype(F32)).astype(BF)

                every(m.half, m.step, add_half)
            if stage == 1:

                def add_quarter(r, m=m, lanes=lanes):
                    rows = pl.ds(r, m.quarter_step)
                    total = m.acc[span(i * m.quarter + r, m.quarter_step, 16), lanes].astype(F32)
                    for d in range(3):
                        total = total + m.first[a, d, rows].astype(F32)
                    m.first_sum[a, rows] = total.astype(BF)

                every(m.quarter, m.quarter_step, add_quarter)
            if stage == 2:
                row, lane = m.spot16(j)
                total = m.first_sum[a, span(row, m.small[0], 16), span(lane, m.small[1])].astype(F32)
                for d in range(3):
                    total = total + m.second[a, d].astype(F32)
                m.third[a, k] = total.astype(BF)
            if stage == 3:
                low = m.third[a, 0].astype(F32) + m.third[a, 1].astype(F32)
                high = m.third[a, 2].astype(F32) + m.third[a, 3].astype(F32)
                m.own[a] = (low + high).astype(BF)
                self.keeps[t, a].start()
            if stage == 4:
                self.keeps[t, a].wait()


class HeadSum:
    def __init__(self, spot, slots, source, got, even, odd):
        self.spot, self.source, self.got, self.even, self.odd = spot, source, got, even, odd
        c, x, y, zh, zl, z = (spot[a] for a in ("c", "x", "y", "zh", "zl", "z"))
        self.block = zh * 4 + x
        self.is_even, self.is_odd = c == 0, c == 1
        self.active = (c == 0) | (zl == y % 2)
        self.pieces = []
        for d in range(1, BLOCKS):
            to = (self.block + d) % BLOCKS
            piece = source.at[pl.ds(pl.multiple_of(to * SHARE, 16), SHARE)]
            self.pieces.append(send(piece, got.at[d - 1], *slots.take(), block_id(to)))
        self.copies = {}
        for side, (ref, count) in enumerate(((even, 0), (odd, 1))):
            def region(zh_, zl_, x_, y_, lo, n, ref=ref, side=side):
                spots = (zh_, zl_, x_, y_) if side == 0 else (zh_, x_, y_)
                return ref.at[(*spots, pl.ds(lo, n))]

            all2, all4 = slice(None), slice(None)
            self.copies[0, side] = [
                send(region(zh, zl, x, y, 0, SHARE), region(zh, zl, x, y, 0, SHARE), *slots.take(),
                     on_axis("z", (z + d) % 4))
                for d in range(1, 4)
            ]
            for part, (lo, n) in enumerate(CUTS):
                axes = ("x", "y") if part == 0 else ("y", "x")
                two = region(all2, all2, x, y, lo, n)
                if axes[1] == "y":
                    three = region(all2, all2, all4, y, lo, n)
                else:
                    three = region(all2, all2, x, all4, lo, n)
                for stage, piece in ((1, two), (2, three)):
                    axis = axes[stage - 1]
                    self.copies[stage, side, part] = [
                        send(piece, piece, *slots.take(), on_axis(axis, (spot[axis] + d) % 4))
                        for d in range(1, 4)
                    ]
                whole = region(all2, all2, all4, all4, lo, n)
                self.copies[3, side, part] = [send(whole, whole, *slots.take(), on_axis("c", 1 - c))]

    def start_sum(self):
        for copy in self.pieces:
            pl.when(self.active)(copy.start)

    def finish_sum(self):
        spot = self.spot

        def body():
            for copy in self.pieces:
                copy.wait()
            total = self.source[pl.ds(pl.multiple_of(self.block * SHARE, 16), SHARE)].astype(F32)
            for d in range(BLOCKS - 1):
                total = total + self.got[d].astype(F32)
            total = total.astype(BF)

            def keep_even():
                self.even[spot["zh"], spot["zl"], spot["x"], spot["y"]] = total

            def keep_odd():
                self.odd[spot["zh"], spot["x"], spot["y"]] = total

            pl.when(self.is_even)(keep_even)
            pl.when(self.is_odd)(keep_odd)

        pl.when(self.active)(body)

    def start_z(self):
        def even():
            for copy in self.copies[0, 0]:
                copy.start()

        def odd():
            for copy in self.copies[0, 1]:
                copy.start()

        pl.when(self.is_even)(even)
        pl.when(self.is_odd & self.active)(odd)

    def finish_z(self):
        def even():
            for copy in self.copies[0, 0]:
                copy.wait()

        def odd_send():
            for copy in self.copies[0, 1]:
                copy.wait_send()

        pl.when(self.is_even)(even)
        pl.when(self.is_odd & self.active)(odd_send)
        for d in range(1, 4):
            came = (self.spot["z"] + 4 - d) % 4
            sent = self.is_odd & (came % 2 == self.spot["y"] % 2)
            pl.when(sent)(self.copies[0, 1][d - 1].wait_recv)

    def start(self, stage, part):
        for side, mine in enumerate((self.is_even, self.is_odd)):

            def go(side=side):
                for copy in self.copies[stage, side, part]:
                    copy.start()

            pl.when(mine)(go)

    def finish(self, stage, part):
        for side, mine in enumerate((self.is_even, self.is_odd)):

            def go(side=side):
                for copy in self.copies[stage, side, part]:
                    copy.wait()

            pl.when(mine)(go)

    def start_core(self, part):
        for side, mine in enumerate((self.is_even, self.is_odd)):
            pl.when(mine)(self.copies[3, side, part][0].start)

    def finish_core(self, part):
        for side, mine in enumerate((self.is_even, self.is_odd)):
            pl.when(mine)(self.copies[3, side, part][0].wait_send)
            pl.when(~mine)(self.copies[3, side, part][0].wait_recv)


HEAD_SLOTS = 7 + 2 * (3 + 2 * (3 + 3 + 1))


class TableSum:
    def __init__(self, slots, table, parts, got):
        self.me = my_block()
        self.table, self.parts, self.got = table, parts, got
        self.shares, self.spread = [], []
        for d in range(1, BLOCKS):
            to = (self.me + d) % BLOCKS
            self.shares.append(send(parts.at[d - 1], got.at[d - 1], *slots.take(), block_id(to)))
        mine = table.at[pl.ds(0, ITEM), span(self.me * SLOTS, SLOTS)]
        for d in range(1, BLOCKS):
            to = (self.me + d) % BLOCKS
            self.spread.append(send(mine, mine, *slots.take(), block_id(to)))

    def fill(self, items, codes_ref, weights_ref, hot):
        for t in range(1, BLOCKS + 1):
            s = (self.me + t) % BLOCKS
            slot = t % 2
            for i in range(CHUNKS):
                cols = pl.ds(i * CHUNK, CHUNK)
                hot[slot, :, cols] = one_hot(codes_ref[pl.ds(s, 1), cols], weights_ref[pl.ds(s, 1), cols])
            got = nt(items[...], hot[slot])
            self.table[pl.ds(ITEM, STACK - ITEM), span(s * SLOTS, SLOTS)] = got[ITEM:].astype(BF)
            if t < BLOCKS:
                self.parts[t - 1] = got[:ITEM].astype(BF)
                self.shares[t - 1].start()
            else:
                self.own = got[:ITEM]

    def add(self):
        total = self.own
        for d in range(1, BLOCKS):
            self.shares[d - 1].wait()
            total = total + self.got[d - 1].astype(F32)
        self.table[pl.ds(0, ITEM), span(self.me * SLOTS, SLOTS)] = total.astype(BF)
        for copy in self.spread:
            copy.start()

    def finish(self):
        for copy in self.spread:
            copy.wait()


TABLE_SLOTS = 2 * (BLOCKS - 1)


class Halo:
    def __init__(self, slots, edges, came):
        me = my_block()
        down, up = block_id((me + BLOCKS - 1) % BLOCKS), block_id((me + 1) % BLOCKS)
        self.copies = [
            send(edges.at[0], came.at[1], *slots.take(), down),
            send(edges.at[1], came.at[0], *slots.take(), up),
        ]

    def start(self):
        for copy in self.copies:
            copy.start()

    def finish(self):
        for copy in self.copies:
            copy.wait()


HALO_SLOTS = 2


class Scatter:
    def __init__(self, slots_send, slots_recv, local, chunks, out):
        self.me = my_member()
        self.owner, self.head = owns(self.me), head_at(self.me)
        self.send_sem, self.recv_sem, self.local = slots_send, slots_recv, local
        self.chunks, self.out = chunks, out

    def copy(self, p):
        return send(
            self.chunks.at[p], self.out.at[self.head], self.send_sem.at[p], self.recv_sem.at[self.head], member_id(p)
        )

    def keep(self, p):
        return pltpu.make_async_copy(self.chunks.at[p], self.out.at[self.head], self.local)

    def start(self, p):
        pl.when(self.owner & (self.me != p))(lambda: self.copy(p).start())
        pl.when(self.owner & (self.me == p))(lambda: self.keep(p).start())

    def finish(self):
        for h in range(HEADS):
            at = owner_of(h)
            got = send(self.chunks.at[0], self.out.at[h], self.send_sem.at[0], self.recv_sem.at[h], member_id(at))
            pl.when(self.me != at)(got.wait_recv)
        for p in range(MEMBERS):
            pl.when(self.owner & (self.me != p))(self.copy(p).wait_send)
        pl.when(self.owner)(self.keep(self.me).wait)


class Gather:
    def __init__(self, slots_send, slots_recv, local, chunks, out):
        self.me = my_member()
        self.owner, self.head = owns(self.me), head_at(self.me)
        self.chunks, self.out, self.send_sem, self.recv_sem = chunks, out, slots_send, slots_recv
        self.keep = pltpu.make_async_copy(chunks.at[self.head], out.at[self.me], local)
        self.copies = []
        for d in range(1, MEMBERS):
            to = (self.me + d) % MEMBERS
            copy = send(chunks.at[head_at(to)], out.at[self.me], slots_send.at[d], slots_recv.at[self.me], member_id(to))
            self.copies.append((owns(to), copy))

    def start(self):
        for wanted, copy in self.copies:
            pl.when(wanted)(copy.start)
        self.keep.start()

    def finish(self):
        self.keep.wait()
        for d in range(1, MEMBERS):
            came = (self.me + d) % MEMBERS
            got = send(self.chunks.at[0], self.out.at[came], self.send_sem.at[0], self.recv_sem.at[came], member_id(came))
            pl.when(self.owner)(got.wait_recv)
        for wanted, copy in self.copies:
            pl.when(wanted)(copy.wait_send)


def block_peers():
    me = my_block()
    return [block_id((me + d) % BLOCKS) for d in range(1, BLOCKS)]


def member_peers():
    me = my_member()
    return [member_id((me + d) % MEMBERS) for d in range(1, MEMBERS)]


def iota(shape, dim):
    return lax.broadcasted_iota(I32, shape, dim)


def tap_row(conv_w, head, flip):
    mine = jnp.where(iota((HEADS, 65), 0) == head, conv_w[...], 0.0)
    row, col = iota((65, 256), 0), iota((65, 256), 1)
    place = jnp.where(col == (160 - row if flip else row + 96), 1.0, 0.0)
    return jnp.sum(nn(mine, place, precision=HIGHEST), axis=0, keepdims=True)


def head_column(vector, head):
    rows = jnp.broadcast_to(vector[...][None, :], (128, D))
    pick = jnp.where(iota((HEAD, D), 1) == iota((HEAD, D), 0) + head * HEAD, 1.0, 0.0)
    return nt(pick, rows, precision=HIGHEST)[:, 0:1]


def item_masks(cuts, block):
    start = block * BLOCK - EDGE
    pos = start + iota((1, EXT), 1)
    item = jnp.zeros((1, EXT), I32)
    for k in range(1, 4):
        item = item + jnp.where(pos >= cuts[k], 1, 0)
    longest = jnp.where(cuts[2] - cuts[1] > 1024, 1, 2)
    outer = jnp.where(block < 4, 0, 3)
    inner = jnp.where(block < 4, 1, 2)
    valid = jnp.where((pos >= 0) & (pos < TOTAL), 1.0, 0.0)
    is_long = jnp.where(item == longest, valid, 0.0)
    is_outer = jnp.where(item == outer, valid, 0.0)
    is_inner = jnp.where(item == inner, valid, 0.0) - jnp.where(inner == longest, is_long, 0.0)
    return jnp.concatenate([is_long, is_outer, is_inner, jnp.zeros((5, EXT), F32)], axis=0)


def pack(rows):
    return jnp.concatenate([rows[:SIDE], rows[SIDE:]], axis=1).astype(BF)


def unpack_heads(chunk):
    pairs = []
    for i in range(HEADS // 2):
        a, b = chunk(2 * i), chunk(2 * i + 1)
        top = jnp.concatenate([a[:, :HEAD], b[:, :HEAD]], axis=1)
        low = jnp.concatenate([a[:, HEAD:], b[:, HEAD:]], axis=1)
        pairs.append(jnp.concatenate([top, low], axis=0))
    return jnp.concatenate(pairs, axis=1)


START_SLOTS = 16
FRONT_SEMS = START_SLOTS + 8 + 1 + TABLE_SLOTS + HALO_SLOTS + MEMBERS


def front_kernel(
    tokens, q_codes, k_codes, hyper, cuts, w_query, w_key, w_value, b_query, b_key, b_value, conv_w,
    att, qkv, weights, codes, planes, masks, table, estimate, scale, ext,
    other_tok, codes_out, codes_in, planes_in, w_all, w_t, items, hot, big_hot, parts, got, conv, chunks, edges, came,
    local, send_sem, recv_sem,
):
    me, block, core = my_member(), my_block(), lax.axis_index("c")
    head, owner = head_at(me), owns(me)
    hello(member_peers() + block_peers())
    loads = [
        pltpu.make_async_copy(w, w_all.at[k], local.at[k]) for k, w in enumerate((w_query, w_key, w_value))
    ]
    for load in loads:
        load.start()
    for h in range(HEADS):
        codes_out[h, 0:1, :] = q_codes[0, h : h + 1, :]
        codes_out[h, 1:2, :] = k_codes[0, h : h + 1, :]
    mine = me % 8
    eye = jnp.where(iota((HEAD, HEAD), 0) == iota((HEAD, HEAD), 1), 1.0, 0.0)
    planes_in[mine] = tn(hyper[0], eye, precision=HIGHEST)
    masks[...] = item_masks(cuts, block)
    all_here(MEMBERS - 1 + BLOCKS - 1)

    give = Gather(send_sem.at[pl.ds(0, 16)], recv_sem.at[pl.ds(0, 16)], local.at[3], codes_out, codes_in)
    give.start()
    slots = Slots(send_sem, recv_sem)
    slots.used = START_SLOTS
    swap = send(tokens, other_tok, *slots.take(), on_axis("c", 1 - core))
    swap.start()
    spread = []
    for d in range(1, 8):
        piece = planes_in.at[mine]
        spread.append(send(piece, piece, *slots.take(), member_id(core * 8 + (mine + d) % 8)))
    for copy in spread:
        copy.start()
    table_sum = TableSum(slots, table, parts, got)
    halo = Halo(slots, edges, came)
    base = slots.used
    to_rows = Scatter(
        send_sem.at[pl.ds(base, 16)], recv_sem.at[pl.ds(base, 16)], local.at[4], chunks, att
    )

    pick = jnp.where(iota((HEAD, D), 1) == iota((HEAD, D), 0) + head * HEAD, 1.0, 0.0).astype(BF)
    v_bias = head_column(b_value, head)
    bias = jnp.concatenate([head_column(b_query, head), head_column(b_key, head), jnp.zeros((HEAD, 1), F32)], axis=0)
    for k, load in enumerate(loads):
        load.wait()
        w_t[k * HEAD : (k + 1) * HEAD, :] = nt(pick, w_all[k]).astype(BF)

    def project(source, start):
        def step(i, _):
            rows = span(i * CHUNK, CHUNK)
            qkv[:, span(start + i * CHUNK, CHUNK)] = nt(w_t[...], source[rows, :]) + bias
            return 0

        lax.fori_loop(0, ROWS // CHUNK, step, 0)

    project(tokens, core * ROWS)
    swap.wait()
    project(other_tok, (1 - core) * ROWS)
    edges[0] = qkv[2 * HEAD :, :EDGE].astype(BF)
    edges[1] = qkv[2 * HEAD :, BLOCK - EDGE :].astype(BF)
    halo.start()

    give.finish()
    for copy in spread:
        copy.wait()
    for b in range(BITS):
        planes[b * SETS : (b + 1) * SETS, :] = planes_in[:, b, :]
    for side in range(2):
        for s in range(SETS):
            for k in range(2):
                codes[side, s : s + 1, k * ROWS : (k + 1) * ROWS] = codes_in[k * 8 + s, side : side + 1, :]

    def prepare(i, _):
        cols = span(i * CHUNK, CHUNK)
        inner = span(i * CHUNK + EDGE, CHUNK)
        weights[SETS:, cols] = hash_weight(qkv[HEAD : 2 * HEAD, cols], codes[1, :, cols], planes[...])
        items[:, cols] = by_item(qkv[2 * HEAD :, cols], jnp.ones((1, CHUNK), F32), masks[:, inner])
        return 0

    lax.fori_loop(0, CHUNKS, prepare, 0)
    table_sum.fill(items, codes.at[1], weights.at[pl.ds(SETS, SETS)], hot)

    def query_side(i, _):
        cols = span(i * CHUNK, CHUNK)
        inner = span(i * CHUNK + EDGE, CHUNK)
        weights[:SETS, cols] = hash_weight(qkv[:HEAD, cols], codes[0, :, cols], planes[...])
        ext[:, inner] = by_item(qkv[2 * HEAD :, cols] + v_bias, jnp.zeros((1, CHUNK), F32), masks[:, inner])
        return 0

    lax.fori_loop(0, CHUNKS, query_side, 0)
    table_sum.add()
    halo.finish()
    none = jnp.zeros((1, EDGE), F32)
    ext[:, :EDGE] = by_item(came[0].astype(F32) + v_bias, none, masks[:, :EDGE])
    ext[:, EDGE + BLOCK :] = by_item(came[1].astype(F32) + v_bias, none, masks[:, EDGE + BLOCK :])
    lower, upper = circulant(tap_row(conv_w, head, True))

    def convolve(i, _):
        at = i * 256
        mixed = nn(ext[:, span(at, 256)], lower) + nn(ext[:, span(at + 256, 256)], upper)
        conv[:, span(at, 256)] = pick_item(mixed, masks[:, span(at + EDGE, 256)])[:HEAD] + v_bias
        return 0

    lax.fori_loop(0, BLOCK // 256, convolve, 0)
    table_sum.finish()

    def read(i, _):
        cols = span(i * CHUNK, CHUNK)
        own = masks[:, span(i * CHUNK + EDGE, CHUNK)]
        for s in range(SETS):
            big_hot[s * SLOTS : (s + 1) * SLOTS, :] = one_hot(codes[0, s : s + 1, cols], weights[s : s + 1, cols])
        found = pick_item(nn(table[...], big_hot[...]), own)
        recip = 1.0 / (found[HEAD : HEAD + 1] + 1.0)
        est = (found[:HEAD] - v_bias) * recip
        estimate[:, cols] = est
        scale[:, cols] = recip
        rows = jnp.transpose(est + conv[:, cols])
        for u in range(PER_CHUNK):
            p = i * PER_CHUNK + u
            chunks[p] = pack(rows[u * OWN : (u + 1) * OWN])
            to_rows.start(p)
        return 0

    lax.fori_loop(0, CHUNKS, read, 0)
    to_rows.finish()


def norm_forward(values):
    centred = values - jnp.mean(values, axis=-1, keepdims=True)
    recip = lax.rsqrt(jnp.mean(centred * centred, axis=-1, keepdims=True) + EPS_NORM)
    return centred * recip, recip


def norm_backward(grad, hat, recip, gain):
    scaled = grad * gain
    mean = jnp.mean(scaled, axis=-1, keepdims=True)
    along = jnp.mean(scaled * hat, axis=-1, keepdims=True)
    return recip * (scaled - mean - hat * along)


def column_sums(values):
    return jnp.sum(values, axis=0, keepdims=True)


def ffn_kernel(
    att, tokens, cot, w_out, w_in, w_back, b_out, ln1_gain, ln1_bias, b_in, b_back, ln2_gain, ln2_bias,
    output, resid, chunks, big_a, big_b, vec,
    tok, w_out_v, w_in_v, w_back_v, act_v, slope_v, a_v, b_v, sems, out_sems,
):
    at = (lax.axis_index("y") * 2 + lax.axis_index("zl")) * OWN
    loads = [
        pltpu.make_async_copy(a, b, sems.at[k])
        for k, (a, b) in enumerate(
            [(tokens.at[span(at, OWN, 16)], tok), (w_out, w_out_v), (w_in, w_in_v), (w_back, w_back_v)]
        )
    ]
    for load in loads:
        load.start()
    gain1, gain2 = ln1_gain[...][None, :], ln2_gain[...][None, :]
    attended = unpack_heads(lambda h: att[h])
    loads[0].wait()
    loads[1].wait()
    branch = nn(attended, w_out_v[...]) + b_out[...][None, :]
    hat1, recip1 = norm_forward(tok[...].astype(F32) + branch)
    hidden = hat1 * gain1 + ln1_bias[...][None, :]
    hidden_low = hidden.astype(BF)
    loads[2].wait()
    outer = b_back[...][None, :]
    for k in range(FF // D):
        cols = slice(k * D, (k + 1) * D)
        inner = nn(hidden_low, w_in_v[:, cols]) + b_in[pl.ds(k * D, D)][None, :]
        phi = 0.5 * (1.0 + lax.erf(inner * (2.0**-0.5)))
        slope_v[:, cols] = phi + inner * (jnp.exp(-0.5 * inner * inner) * 0.3989422804014327)
        act = (inner * phi).astype(BF)
        act_v[:, cols] = act
        if k == 0:
            loads[3].wait()
        outer = outer + nn(act, w_back_v[cols, :])
    hat2, recip2 = norm_forward(hidden + outer)
    output[...] = hat2 * gain2 + ln2_bias[...][None, :]
    got = cot[...]
    sum_grad = norm_backward(got, hat2, recip2, gain2)
    outer_grad = sum_grad.astype(BF)
    hidden_grad = sum_grad
    sums = [column_sums(outer_grad.astype(F32)), column_sums(got * hat2), column_sums(got)]
    hidden_t = jnp.transpose(hidden).astype(BF)
    bias_rows = []
    writes = []

    def write(source, dest):
        copy = pltpu.make_async_copy(source, dest, out_sems.at[len(writes)])
        copy.start()
        writes.append(copy)

    for k in range(FF // D):
        cols = slice(k * D, (k + 1) * D)
        act_grad = nt(outer_grad, w_back_v[cols, :])
        inner_grad = (act_grad * slope_v[:, cols]).astype(BF)
        bias_rows.append(column_sums(inner_grad.astype(F32)))
        hidden_grad = hidden_grad + nt(inner_grad, w_in_v[:, cols])
        a_v[:, cols] = nn(hidden_t, inner_grad).astype(BF)
        write(a_v.at[:, cols], big_a.at[:, cols])
        b_v[cols, :] = nn(jnp.transpose(act_v[:, cols].astype(F32)).astype(BF), outer_grad).astype(BF)
        write(b_v.at[cols, :], big_b.at[cols, :])
    grad1 = norm_backward(hidden_grad, hat1, recip1, gain1)
    resid[...] = grad1
    branch_grad = grad1.astype(BF)
    att_grad = nt(branch_grad, w_out_v[...])
    for h in range(HEADS):
        chunks[h] = pack(att_grad[:, h * HEAD : (h + 1) * HEAD])
    last = slice(FF, WIDE)
    a_v[:, last] = nn(jnp.transpose(attended.astype(F32)).astype(BF), branch_grad).astype(BF)
    write(a_v.at[:, last], big_a.at[:, last])
    rows = [column_sums(branch_grad.astype(F32)), column_sums(hidden_grad * hat1), column_sums(hidden_grad)]
    vec[...] = jnp.concatenate(rows + sums + bias_rows + [jnp.zeros((6, D), F32)], axis=0)
    for copy in writes:
        copy.wait()


BACK_SEMS = (
    MEMBERS + MEMBERS + 1 + TABLE_SLOTS + HALO_SLOTS + BIG_SLOTS + HEAD_SLOTS + 2 * VEC_SLOTS
)


def back_kernel(
    chunks, tokens, qkv, weights, codes, planes, masks, table, estimate, scale, v_ext, vec, resid, conv_w, b_value,
    big_a, big_b, w_query, w_key, w_value,
    grad_tokens, sum_a, sum_b, vec_out, small_out, even, odd,
    other_tok, w_all, chunks_in, grad, den, items, hot, parts, got, gtable, ext, edges, came, rows_ref, g_all, q_grad,
    mix, g_chunks, g_in, head_w, head_got, vec_buf, small_buf, local, send_sem, recv_sem, *big_refs,
):
    spot = here()
    me, core = my_member(), spot["c"]
    head, owner = head_at(me), owns(me)
    far = {"zh": 1 - spot["zh"], "zl": 1 - spot["zl"]}
    hello(member_peers() + block_peers() + [far])
    slots = Slots(send_sem, recv_sem)
    slots.used = 2 * MEMBERS
    give = Gather(send_sem.at[pl.ds(0, 16)], recv_sem.at[pl.ds(0, 16)], local.at[0], chunks, chunks_in)
    to_rows = Scatter(send_sem.at[pl.ds(16, 16)], recv_sem.at[pl.ds(16, 16)], local.at[1], g_chunks, g_in)
    swap = send(tokens, other_tok, *slots.take(), on_axis("c", 1 - core))
    table_sum = TableSum(slots, gtable, parts, got)
    halo = Halo(slots, edges, came)
    per = len(big_refs) // 2
    mats = [
        Matrix(*MATRICES[t], refs=(source, result, *big_refs[t * per : (t + 1) * per]))
        for t, (source, result) in enumerate(((big_a, sum_a), (big_b, sum_b)))
    ]
    sums = BigSum(spot, slots, local.at[pl.ds(2, 8)], mats)
    heads = HeadSum(spot, slots, head_w, head_got, even, odd)
    vector = VectorSum(spot, slots, vec[...], vec_buf)
    small = VectorSum(spot, slots, None, small_buf)
    loads = [
        pltpu.make_async_copy(w, w_all.at[k], local.at[10 + k]) for k, w in enumerate((w_query, w_key, w_value))
    ]
    sums.load()
    for load in loads:
        load.start()
    v_bias = head_column(b_value, head)
    every_part = range(PARTS)
    all_here(MEMBERS - 1 + BLOCKS - 1 + 1)

    give.start()
    vector.start(0)
    for a in every_part:
        sums.start(0, a)
    swap.start()
    give.finish()

    for p in range(MEMBERS):
        both = chunks_in[p].astype(F32)
        rows_ref[p * OWN : p * OWN + SIDE] = both[:, :HEAD]
        rows_ref[p * OWN + SIDE : (p + 1) * OWN] = both[:, HEAD:]

    def prepare(i, _):
        cols = span(i * CHUNK, CHUNK)
        own = masks[:, span(i * CHUNK + EDGE, CHUNK)]
        this = jnp.transpose(rows_ref[span(i * CHUNK, CHUNK), :])
        grad[:, cols] = this
        numer = this * scale[:, cols]
        mass = -jnp.sum(numer * estimate[:, cols], axis=0, keepdims=True)
        den[:, cols] = mass
        items[:, cols] = by_item(numer, mass, own)
        ext[:, span(i * CHUNK + EDGE, CHUNK)] = by_item(this, jnp.zeros((1, CHUNK), F32), own)
        return 0

    lax.fori_loop(0, CHUNKS, prepare, 0)
    edges[0] = grad[:, :EDGE].astype(BF)
    edges[1] = grad[:, BLOCK - EDGE :].astype(BF)
    halo.start()
    table_sum.fill(items, codes.at[0], weights.at[pl.ds(0, SETS)], hot)

    def query_back(i, _):
        cols = span(i * CHUNK, CHUNK)
        own = masks[:, span(i * CHUNK + EDGE, CHUNK)]
        q_codes = codes[0, :, cols]
        numer = grad[:, cols] * scale[:, cols]
        mass = den[:, cols]
        found_all = []
        for s in range(SETS):
            one = one_hot(q_codes[s : s + 1], 1.0)
            found = pick_item(nn(table[:, s * SLOTS : (s + 1) * SLOTS], one), own)
            found_all.append(
                jnp.sum(found[:HEAD] * numer, axis=0, keepdims=True) + found[HEAD : HEAD + 1] * mass
            )
        z_grad = jnp.concatenate(found_all, axis=0) * weights[:SETS, cols]
        g_all[:HEAD, cols] = hash_back(z_grad, qkv[:HEAD, cols], q_codes, planes[...]).astype(BF)
        return 0

    lax.fori_loop(0, 1, query_back, 0)
    table_sum.add()
    sums.loaded()
    for a in every_part:
        sums.finish(0, a)
        sums.start(1, a)
    vector.finish(0)
    vector.start(1)
    lax.fori_loop(1, CHUNKS, query_back, 0)

    halo.finish()
    none = jnp.zeros((1, EDGE), F32)
    ext[:, :EDGE] = by_item(came[0].astype(F32), none, masks[:, :EDGE])
    ext[:, EDGE + BLOCK :] = by_item(came[1].astype(F32), none, masks[:, EDGE + BLOCK :])
    lower, upper = circulant(tap_row(conv_w, head, False))

    def conv_back(i, carry):
        at = i * 256
        mixed = nn(ext[:, span(at, 256)], lower) + nn(ext[:, span(at + 256, 256)], upper)
        mix[:, span(at, 256)] = pick_item(mixed, masks[:, span(at + EDGE, 256)])[:HEAD]
        this = ext[:, span(at + EDGE, 256)]
        return carry[0] + tn(v_ext[:, span(at, 256)], this), carry[1] + tn(v_ext[:, span(at + 256, 256)], this)

    zeros = jnp.zeros((256, 256), F32)
    c_low, c_high = lax.fori_loop(0, BLOCK // 256, conv_back, (zeros, zeros))
    row, col = iota((256, 256), 0), iota((256, 256), 1)
    skew = jnp.where(col < row, c_low, c_high)
    for b in range(8):
        skew = jnp.where(jnp.bitwise_and(row, 1 << b) != 0, pltpu.roll(skew, 256 - (1 << b), 1), skew)
    taps_grad = jnp.sum(skew, axis=0, keepdims=True)
    vector.finish(1)
    vector.start(2)
    for a in every_part:
        sums.finish(1, a)
        sums.start(2, a)
    table_sum.finish()

    def key_back(i, _):
        cols = span(i * CHUNK, CHUNK)
        own = masks[:, span(i * CHUNK + EDGE, CHUNK)]
        k_codes = codes[1, :, cols]
        k_w = weights[SETS:, cols]
        val = qkv[2 * HEAD :, cols]
        found_all = []
        v_grad = mix[:, cols]
        for s in range(SETS):
            one = one_hot(k_codes[s : s + 1], 1.0)
            found = pick_item(nn(gtable[:, s * SLOTS : (s + 1) * SLOTS], one), own)
            found_all.append(
                jnp.sum(found[:HEAD] * val, axis=0, keepdims=True) + found[HEAD : HEAD + 1]
            )
            v_grad = v_grad + found[:HEAD] * k_w[s : s + 1]
        z_grad = jnp.concatenate(found_all, axis=0) * k_w
        k_grad = hash_back(z_grad, qkv[HEAD : 2 * HEAD, cols], k_codes, planes[...])
        g_all[HEAD : 2 * HEAD, cols] = k_grad.astype(BF)
        g_all[2 * HEAD : 3 * HEAD, cols] = v_grad.astype(BF)
        for k in range(3):
            rows = jnp.transpose(g_all[k * HEAD : (k + 1) * HEAD, cols].astype(F32))
            for u in range(PER_CHUNK):
                g_chunks[i * PER_CHUNK + u, k] = pack(rows[u * OWN : (u + 1) * OWN])
        for u in range(PER_CHUNK):
            to_rows.start(i * PER_CHUNK + u)
        return 0

    lax.fori_loop(0, 2, key_back, 0)
    vector.finish(2)
    vector.start(3)
    for a in every_part:
        sums.finish(2, a)
        sums.start(3, a)
    lax.fori_loop(2, CHUNKS, key_back, 0)

    g_all[3 * HEAD :, :] = jnp.zeros((HEAD, BLOCK), BF)
    own_part = g_all[: 3 * HEAD, span(core * ROWS, ROWS)]
    away = g_all[: 3 * HEAD, span((1 - core) * ROWS, ROWS)]
    swap.wait()
    w_grad = jnp.transpose(nn(own_part, tokens[...]) + nn(away, other_tok[...]))
    head_w[:D] = w_grad[:, : 2 * HEAD].astype(BF)
    head_w[D:] = jnp.concatenate([w_grad[: D // 2, 2 * HEAD :], w_grad[D // 2 :, 2 * HEAD :]], axis=1).astype(BF)
    heads.start_sum()
    for a in every_part:
        sums.finish(3, a)
        sums.start(4, a)
    biases = nt(jnp.ones((8, BLOCK), BF), g_all[...])[0:1]
    mine = (iota((16, SMALL), 0) == head) & owner
    small.value = jnp.where(mine, jnp.concatenate([biases, taps_grad], axis=1), 0.0)
    small.start(0)
    vector.finish(3)
    vec_out[...] = vector.value
    heads.finish_sum()
    heads.start_z()
    for a in every_part:
        sums.finish(4, a)
        sums.start(5, a)
    small.finish(0)
    small.start(1)
    to_rows.finish()
    total = resid[...]
    for k in range(3):
        loads[k].wait()
        total = total + nt(unpack_heads(lambda h, k=k: g_in[h, k]), w_all[k])
    grad_tokens[...] = total
    heads.finish_z()
    for part in range(2):
        heads.start(1, part)
    small.finish(1)
    small.start(2)
    for part in range(2):
        heads.finish(1, part)
        heads.start(2, part)
    small.finish(2)
    small.start(3)
    for a in every_part:
        sums.finish(5, a)
        sums.start(6, a)
    for part in range(2):
        heads.finish(2, part)
        heads.start_core(part)
    small.finish(3)
    small_out[...] = small.value
    for part in range(2):
        heads.finish_core(part)
    for a in every_part:
        sums.finish(6, a)


PIECES = 8


def last_kernel(
    sum_a, sum_b, even, odd, vec, small, tok_grad,
    grad_tokens, g_wq, g_bq, g_wk, g_bk, g_wv, g_bv, g_conv, g_wo, g_bo, g_l1g, g_l1b, g_wi, g_bi, g_wb, g_bb, g_l2g,
    g_l2b,
    a_in, b_in, a_out, b_out, qkv_out, in_sems, out_sems,
):
    a_rows, b_rows = D // PIECES, FF // PIECES
    loads = []
    for k in range(PIECES):
        rows = pl.ds(k * a_rows, a_rows)
        loads.append(pltpu.make_async_copy(sum_a.at[rows], a_in.at[rows], in_sems.at[2 * k]))
        rows = pl.ds(k * b_rows, b_rows)
        loads.append(pltpu.make_async_copy(sum_b.at[rows], b_in.at[rows], in_sems.at[2 * k + 1]))
    for load in loads:
        load.start()
    writes = []

    def write(source, dest):
        copy = pltpu.make_async_copy(source, dest, out_sems.at[len(writes)])
        copy.start()
        writes.append(copy)

    left = iota((SHARE, 128), 1) < HEAD

    def pieces(pair, j):
        zh, x = j // 4, j % 4
        if pair < 4:
            return even[zh, 0, x, pair].astype(F32), even[zh, 1, x, pair].astype(F32)
        return odd[zh, x, 2 * (pair - 4)].astype(F32), odd[zh, x, 2 * (pair - 4) + 1].astype(F32)

    for pair in range(HEADS // 2):
        lanes = pl.ds(pair * 128, 128)
        for j in range(BLOCKS):
            a, b = pieces(pair, j)
            first = jnp.where(left, a, pltpu.roll(b, HEAD, 1))
            second = jnp.where(left, pltpu.roll(a, HEAD, 1), b)
            low, high = j * SHARE, (j + 1) * SHARE
            cut = min(max(D - low, 0), SHARE)
            if cut > 0:
                qkv_out[0, low : low + cut, lanes] = first[:cut]
                qkv_out[1, low : low + cut, lanes] = second[:cut]
            if cut < SHARE:
                start, stop = low + cut - D, high - D
                qkv_out[2, start:stop, lanes] = first[cut:]
                qkv_out[2, D // 2 + start : D // 2 + stop, lanes] = second[cut:]
    for k, dest in enumerate((g_wq, g_wk, g_wv)):
        write(qkv_out.at[k], dest)
    for k in range(PIECES):
        rows = pl.ds(k * a_rows, a_rows)
        loads[2 * k].wait()
        a_out[rows, :] = a_in[rows, :].astype(F32)
        write(a_out.at[rows, pl.ds(0, FF)], g_wi.at[rows])
        write(a_out.at[rows, pl.ds(FF, D)], g_wo.at[rows])
        rows = pl.ds(k * b_rows, b_rows)
        loads[2 * k + 1].wait()
        b_out[rows, :] = b_in[rows, :].astype(F32)
        write(b_out.at[rows], g_wb.at[rows])
    grad_tokens[...] = tok_grad[...]
    for k, dest in enumerate((g_bo, g_l1g, g_l1b, g_bb, g_l2g, g_l2b)):
        dest[...] = vec[k, :]
    for k in range(FF // D):
        g_bi[pl.ds(k * D, D)] = vec[6 + k, :]
    for k, dest in enumerate((g_bq, g_bk, g_bv)):
        for pair in range(HEADS // 2):
            lanes = slice(k * HEAD, (k + 1) * HEAD)
            dest[pl.ds(pair * 128, 128)] = jnp.concatenate(
                [small[2 * pair : 2 * pair + 1, lanes], small[2 * pair + 1 : 2 * pair + 2, lanes]], axis=1
            )[0]
    row, col = iota((256, 128), 0), iota((256, 128), 1)
    flip = jnp.where(row == 160 - col, 1.0, 0.0)
    g_conv[...] = nn(small[:, 256:], flip, precision=HIGHEST)[:HEADS, :65]
    for copy in writes:
        copy.wait()


VMEM_SPEC = pl.BlockSpec(memory_space=pltpu.VMEM)
ANY_SPEC = pl.BlockSpec(memory_space=pl.ANY)
SMEM_SPEC = pl.BlockSpec(memory_space=pltpu.SMEM)


def call(kernel, outs, scratch, *args, ident=None, far=(), far_outs=(), scalars=()):
    params = {} if ident is None else {"collective_id": ident, "has_side_effects": True}
    specs = [ANY_SPEC if k in far else SMEM_SPEC if k in scalars else VMEM_SPEC for k in range(len(args))]
    return pl.pallas_call(
        kernel,
        out_shape=[jax.ShapeDtypeStruct(shape, kind) for shape, kind in outs],
        in_specs=specs,
        out_specs=[ANY_SPEC if k in far_outs else VMEM_SPEC for k in range(len(outs))],
        scratch_shapes=scratch,
        compiler_params=pltpu.CompilerParams(vmem_limit_bytes=VMEM_LIMIT, **params),
    )(*args)


def dma(count):
    return pltpu.SemaphoreType.DMA((count,))


def vmem(*shape, kind=BF):
    return pltpu.VMEM(shape, kind)


def per_device(
    tokens, item_cuts, q_codes, k_codes, hyperplanes, w_query, b_query, w_key, b_key,
    w_value, b_value, conv_weight, w_out, b_out, ln1_gain, ln1_bias, w_in, b_in, w_back,
    b_back, ln2_gain, ln2_bias, cotangent,
):
    att, qkv, weights, codes, planes, masks, table, estimate, scale, v_ext = call(
        front_kernel,
        [
            ((HEADS, SIDE, 128), BF), ((3 * HEAD, BLOCK), F32), ((2 * SETS, BLOCK), F32), ((2, SETS, BLOCK), I32),
            ((BITS * SETS, HEAD), F32), ((8, EXT), F32), ((STACK, TABLE), BF), ((HEAD, BLOCK), F32),
            ((1, BLOCK), F32), ((STACK, EXT), BF),
        ],
        [
            vmem(ROWS, D), vmem(HEADS, 2, ROWS, kind=I32), vmem(MEMBERS, 2, ROWS, kind=I32),
            vmem(SETS, BITS, HEAD, kind=F32), vmem(3, D, D), vmem(3 * HEAD, D), vmem(STACK, BLOCK),
            vmem(2, SLOTS, BLOCK), vmem(TABLE, CHUNK), vmem(BLOCKS - 1, ITEM, SLOTS), vmem(BLOCKS - 1, ITEM, SLOTS),
            vmem(HEAD, BLOCK, kind=F32), vmem(MEMBERS, SIDE, 128), vmem(2, HEAD, EDGE), vmem(2, HEAD, EDGE),
            dma(5), dma(FRONT_SEMS), dma(FRONT_SEMS),
        ],
        tokens, q_codes, k_codes, hyperplanes, item_cuts, w_query, w_key, w_value, b_query, b_key, b_value,
        conv_weight,
        ident=0, far=(5, 6, 7), scalars=(4,),
    )
    output, resid, chunks, big_a, big_b, vec = call(
        ffn_kernel,
        [
            ((OWN, D), F32), ((OWN, D), F32), ((HEADS, SIDE, 128), BF), ((D, WIDE), BF), ((FF, D), BF),
            ((16, D), F32),
        ],
        [
            vmem(OWN, D), vmem(D, D), vmem(D, FF), vmem(FF, D), vmem(OWN, FF), vmem(OWN, FF, kind=F32),
            vmem(D, WIDE), vmem(FF, D), dma(4), dma(9),
        ],
        att, tokens, cotangent, w_out, w_in, w_back, b_out, ln1_gain, ln1_bias, b_in, b_back, ln2_gain, ln2_bias,
        far=(1, 3, 4, 5), far_outs=(3, 4),
    )
    tok_grad, sum_a, sum_b, vec_sum, small_sum, even, odd = call(
        back_kernel,
        [
            ((OWN, D), F32), ((D, WIDE), BF), ((FF, D), BF), ((16, D), F32), ((16, SMALL), F32),
            ((2, 2, 4, 4, SHARE, 128), BF), ((2, 4, 4, SHARE, 128), BF),
        ],
        [
            vmem(ROWS, D), vmem(3, D, D), vmem(MEMBERS, SIDE, 128), vmem(HEAD, BLOCK, kind=F32),
            vmem(1, BLOCK, kind=F32), vmem(STACK, BLOCK), vmem(2, SLOTS, BLOCK), vmem(BLOCKS - 1, ITEM, SLOTS),
            vmem(BLOCKS - 1, ITEM, SLOTS), vmem(STACK, TABLE), vmem(STACK, EXT), vmem(2, HEAD, EDGE),
            vmem(2, HEAD, EDGE), vmem(BLOCK, HEAD, kind=F32), vmem(4 * HEAD, BLOCK), vmem(16, 128),
            vmem(HEAD, BLOCK, kind=F32), vmem(MEMBERS, 3, SIDE, 128), vmem(HEADS, 3, SIDE, 128),
            vmem(HEAD_ROWS, 128), vmem(BLOCKS - 1, SHARE, 128), vmem(4, 4, 16, D, kind=F32),
            vmem(4, 4, 16, SMALL, kind=F32), dma(13), dma(BACK_SEMS), dma(BACK_SEMS),
        ]
        + Matrix(*MATRICES[0]).scratch()
        + Matrix(*MATRICES[1]).scratch(),
        chunks, tokens, qkv, weights, codes, planes, masks, table, estimate, scale, v_ext, vec, resid, conv_weight,
        b_value, big_a, big_b, w_query, w_key, w_value,
        ident=1, far=(15, 16, 17, 18, 19), far_outs=(1, 2),
    )
    square, line = ((D, D), F32), ((D,), F32)
    rest = call(
        last_kernel,
        [
            ((OWN, D), F32), square, line, square, line, square, line, ((HEADS, 65), F32), square, line, line, line,
            ((D, FF), F32), ((FF,), F32), ((FF, D), F32), line, line, line,
        ],
        [
            vmem(D, WIDE), vmem(FF, D), vmem(D, WIDE, kind=F32), vmem(FF, D, kind=F32), vmem(3, D, D, kind=F32),
            dma(2 * PIECES), dma(3 + 3 * PIECES),
        ],
        sum_a, sum_b, even, odd, vec_sum, small_sum, tok_grad,
        far=(0, 1), far_outs=(1, 3, 5, 8, 12, 14),
    )
    return (output, *rest)


def solution(mesh):
    grid = Mesh(mesh.devices.reshape(2, 4, 2, 4, 2), ALL_AXES)
    rows = ("zh", "x", "c")
    sets = ("y", "zl")
    placed = (
        P(rows, None), P(), P(sets, None, rows), P(sets, None, rows), P(sets, None, None),
    ) + (P(),) * 17 + (P(ALL_AXES, None),)
    return jax.shard_map(
        per_device,
        mesh=grid,
        in_specs=placed,
        out_specs=(P(ALL_AXES, None), P(ALL_AXES, None)) + (P(),) * 17,
        check_vma=False,
    )
```

```python
import jax
import jax.numpy as jnp
from jax import lax
from jax.experimental import pallas as pl
from jax.experimental.pallas import tpu as pltpu
from jax.sharding import Mesh, PartitionSpec as P

BF = jnp.bfloat16
F32 = jnp.float32
I32 = jnp.int32
HIGHEST = lax.Precision.HIGHEST
MESH = pl.DeviceIdType.MESH
EPS_NORM = 1e-05
EPS_UNIT = 1e-06

D = 768
HEADS = 12
HEAD = 64
SETS = 8
BITS = 8
SLOTS = 256
TABLE = SETS * SLOTS
FF = 3072
ROWS = 1280
BLOCK = 2560
BLOCKS = 8
OWN = 160
SIDE = OWN // 2
MEMBERS = 16
EDGE = 128
EXT = BLOCK + 2 * EDGE
TOTAL = 20480
CHUNK = 640
CHUNKS = BLOCK // CHUNK
PER_CHUNK = CHUNK // OWN
ITEM = 80
CLASSES = 3
STACK = ITEM * CLASSES
SHARE = 144
HEAD_ROWS = D + D // 2
SMALL = 512
WIDE = FF + D
VMEM_LIMIT = 61 * 1024 * 1024

BLOCK_AXES = ("zh", "x")
ALL_AXES = ("zh", "x", "c", "y", "zl")


def nt(left, right, **kw):
    return lax.dot_general(left, right, (((1,), (1,)), ((), ())), preferred_element_type=F32, **kw)


def nn(left, right, **kw):
    return lax.dot_general(left, right, (((1,), (0,)), ((), ())), preferred_element_type=F32, **kw)


def tn(left, right, **kw):
    return lax.dot_general(left, right, (((0,), (0,)), ((), ())), preferred_element_type=F32, **kw)


def unit_of(proj):
    scale = lax.rsqrt(jnp.sum(proj * proj, axis=0, keepdims=True) + EPS_UNIT)
    return proj * scale, scale


def bits_of(codes):
    return [(jnp.bitwise_and(codes, 1 << b) != 0) for b in range(BITS)]


def hash_weight(proj, codes, planes):
    unit, _ = unit_of(proj)
    lifted = nn(planes, unit, precision=HIGHEST)
    total = None
    for b, bit in enumerate(bits_of(codes)):
        part = lifted[b * SETS : (b + 1) * SETS]
        part = jnp.where(bit, part, -part)
        total = part if total is None else total + part
    return jnp.exp(total)


def hash_back(z_grad, proj, codes, planes):
    unit, scale = unit_of(proj)
    lifted_grad = jnp.concatenate([jnp.where(bit, z_grad, -z_grad) for bit in bits_of(codes)], axis=0)
    unit_grad = tn(planes, lifted_grad, precision=HIGHEST)
    return scale * (unit_grad - unit * jnp.sum(unit * unit_grad, axis=0, keepdims=True))


def one_hot(codes_row, weight_row):
    width = codes_row.shape[1]
    slots = lax.broadcasted_iota(jnp.int32, (SLOTS, width), 0)
    return jnp.where(slots == codes_row, weight_row, 0.0).astype(BF)


def by_item(sums, mass, masks):
    width = sums.shape[1]
    lead = lax.broadcasted_iota(jnp.int32, (ITEM - HEAD, width), 0) == 0
    tail = jnp.where(lead, mass, 0.0)
    whole = jnp.concatenate([sums, tail], axis=0)
    return jnp.concatenate([whole * masks[w : w + 1] for w in range(CLASSES)], axis=0).astype(BF)


def pick_item(stacked, masks):
    total = None
    for w in range(CLASSES):
        part = stacked[w * ITEM : (w + 1) * ITEM] * masks[w : w + 1]
        total = part if total is None else total + part
    return total


def circulant(base):
    grid = jnp.broadcast_to(base, (256, 256))
    grid = pltpu.roll(grid, 0, 1, stride=1, stride_axis=0)
    row = lax.broadcasted_iota(jnp.int32, (256, 256), 0)
    col = lax.broadcasted_iota(jnp.int32, (256, 256), 1)
    return (
        jnp.where(col < row, grid, 0.0).astype(BF),
        jnp.where(col >= row, grid, 0.0).astype(BF),
    )


def member_id(member):
    return {"c": member // 8, "y": (member % 8) // 2, "zl": member % 2}


def block_id(block):
    return {"zh": block // 4, "x": block % 4}


def owns(member):
    return (member < 8) | (member % 2 == ((member % 8) // 2) % 2)


def head_at(member):
    return jnp.where(member < 8, member, 8 + (member % 8) // 2)


def owner_of(head):
    return head if head < 8 else 8 + (head - 8) * 2 + (head - 8) % 2


def my_member():
    return lax.axis_index("c") * 8 + lax.axis_index("y") * 2 + lax.axis_index("zl")


def my_block():
    return lax.axis_index("zh") * 4 + lax.axis_index("x")


def send(src, dst, send_sem, recv_sem, device):
    return pltpu.make_async_remote_copy(
        src_ref=src, dst_ref=dst, send_sem=send_sem, recv_sem=recv_sem,
        device_id=device, device_id_type=MESH,
    )


def on_axis(axis, k):
    return {"zh": k // 2, "zl": k % 2} if axis == "z" else {axis: k}


def here():
    spot = {a: lax.axis_index(a) for a in ALL_AXES}
    spot["z"] = spot["zh"] * 2 + spot["zl"]
    return spot


class Slots:
    def __init__(self, send_sem, recv_sem):
        self.send_sem, self.recv_sem, self.used = send_sem, recv_sem, 0

    def take(self):
        k = self.used
        self.used += 1
        return self.send_sem.at[k], self.recv_sem.at[k]


AXES = ("c", "x", "y", "z")
ORDERS = (("x", "y", "z"), ("y", "z", "x"), ("z", "x", "y"))
PARTS = 3
VEC_SLOTS = 1 + 3 * 3


class VectorSum:
    def __init__(self, spot, slots, value, buffer):
        self.spot, self.value, self.buffer, self.copies = spot, value, buffer, {}
        for stage, axis in enumerate(AXES):
            size = 2 if axis == "c" else 4
            self.copies[stage] = []
            for d in range(1, size):
                k = spot[axis]
                here_ref = buffer.at[stage, k]
                copy = send(here_ref, here_ref, *slots.take(), on_axis(axis, (k + d) % size))
                self.copies[stage].append(copy)

    def start(self, stage):
        self.buffer[stage, self.spot[AXES[stage]]] = self.value
        for copy in self.copies[stage]:
            copy.start()

    def finish(self, stage):
        for copy in self.copies[stage]:
            copy.wait()
        total = self.buffer[stage, 0] + self.buffer[stage, 1]
        if stage > 0:
            total = total + (self.buffer[stage, 2] + self.buffer[stage, 3])
        self.value = total


def dma(count):
    return pltpu.SemaphoreType.DMA((count,))


def vmem(*shape, kind=BF):
    return pltpu.VMEM(shape, kind)


def hello(ids):
    barrier = pltpu.get_barrier_semaphore()
    for one in ids:
        pl.semaphore_signal(barrier, inc=1, device_id=one, device_id_type=MESH)


def all_here(count):
    pl.semaphore_wait(pltpu.get_barrier_semaphore(), count)


def every(count, step, body):
    def one(i, _):
        body(pl.multiple_of(i * step, 16))
        return 0

    lax.fori_loop(0, count // step, one, 0)


def span(start, size, unit=128):
    return pl.ds(pl.multiple_of(start, unit), size)


class Matrix:
    def __init__(self, shape, row_cut, refs=None):
        self.rows, self.cols = shape
        self.half = self.rows // 2
        self.part = self.cols // PARTS
        self.quarter = self.half // 4
        self.eighth = self.quarter // 2
        self.row_cut = row_cut
        self.col_cut = 4 // row_cut
        self.small = (self.quarter // row_cut, self.part // self.col_cut)
        self.step = 16 if self.part > 512 else 96
        if refs is not None:
            (
                self.result, self.acc, self.relay, self.mixed, self.first, self.first_sum, self.second, self.third,
                self.own,
            ) = refs

    def whole(self):
        return pltpu.VMEM((self.half, self.cols), BF)

    def scratch(self):
        quarter, eighth = (self.quarter, self.part), (self.eighth, self.part)
        shapes = [
            (PARTS, 2, *eighth), (PARTS, 2, *eighth), (PARTS, 2, *quarter), (PARTS, *quarter),
            (PARTS, 3, *self.small), (PARTS, 4, *self.small), (PARTS, *self.small),
        ]
        return [pltpu.VMEM(shape, BF) for shape in shapes]

    def lanes(self, a):
        return pl.ds(a * self.part, self.part)

    def spot16(self, j):
        return (j // self.col_cut) * self.small[0], (j % self.col_cut) * self.small[1]

    def part_of(self, q, a, side=None, base=0):
        start = base + q * self.quarter
        if side is None:
            return span(start, self.quarter, 16), self.lanes(a)
        return span(start + side * self.eighth, self.eighth, 16), self.lanes(a)


MATRICES = (((D, WIDE), 2), ((FF, D), 4))
BIG_SLOTS = 2 * PARTS * (6 + 3 * 3 + 4 + 4)


class BigSum:
    def __init__(self, spot, slots, local, mats):
        self.spot, self.mats, self.local = spot, mats, local
        c = spot["c"]
        sibling = on_axis("c", 1 - c)
        self.copies = {}
        self.keeps = {}
        for t, m in enumerate(mats):
            base = c * m.half
            for a in range(PARTS):
                one, two, three = ORDERS[a]
                i, j, k = spot[one], spot[two], spot[three]
                up, down, across = (i + 1) % 4, (i + 3) % 4, (i + 2) % 4
                to_up, to_down = on_axis(one, up), on_axis(one, down)

                def put(name, src, dst, device):
                    self.copies.setdefault((name, a), []).append(send(src, dst, *slots.take(), device))

                put("far", m.acc.at[m.part_of(across, a, 0)], m.relay.at[a, 0], to_up)
                put("far", m.acc.at[m.part_of(across, a, 1)], m.relay.at[a, 1], to_down)
                upper, lower = pl.ds(0, m.eighth), pl.ds(m.eighth, m.eighth)
                put("near", m.acc.at[m.part_of(up, a, 1)], m.first.at[a, 0, lower], to_up)
                put("near", m.acc.at[m.part_of(down, a, 0)], m.first.at[a, 1, upper], to_down)
                put("mixed", m.mixed.at[a, 0], m.first.at[a, 0, upper], to_up)
                put("mixed", m.mixed.at[a, 1], m.first.at[a, 1, lower], to_down)
                row, lane = m.spot16(j)
                at = (
                    span(base + i * m.quarter + row, m.small[0], 16),
                    span(a * m.part + lane, m.small[1]),
                )
                self.keeps[t, a] = pltpu.make_async_copy(m.own.at[a], m.result.at[at], local.at[t * PARTS + a])
                for d in range(1, 4):
                    to = (j + d) % 4
                    row, lane = m.spot16(to)
                    piece = m.first_sum.at[a, span(row, m.small[0], 16), span(lane, m.small[1])]
                    put("second", piece, m.second.at[a, d - 1], on_axis(two, to))
                    piece = m.third.at[a, k]
                    put("third", piece, piece, on_axis(three, (k + d) % 4))
                    put("back", m.own.at[a], m.result.at[at], on_axis(two, (j + d) % 4))
                mine = m.result.at[m.part_of(i, a, None, base)]
                put("ring", mine, mine, to_up)
                put("ring", mine, mine, to_down)
                piece = m.result.at[m.part_of(down, a, 0, base)]
                put("pass", piece, piece, to_up)
                piece = m.result.at[m.part_of(up, a, 1, base)]
                put("pass", piece, piece, to_down)
                for q in (i, up, down, across):
                    piece = m.result.at[m.part_of(q, a, None, base)]
                    put("core", piece, piece, sibling)

    def start(self, name, a):
        for copy in self.copies[name, a]:
            copy.start()

    def wait(self, name, a):
        for copy in self.copies[name, a]:
            copy.wait()

    def start_core(self, a, which):
        for t in range(len(self.mats)):
            for q in which:
                self.copies["core", a][4 * t + q].start()

    def begin(self, a):
        self.start("far", a)
        self.start("near", a)

    def relay(self, a):
        self.wait("far", a)
        i = self.spot[ORDERS[a][0]]
        for m in self.mats:
            for side, q in ((0, (i + 1) % 4), (1, (i + 3) % 4)):

                def add(r, m=m, side=side, q=q):
                    rows = pl.ds(r, m.step)
                    start = q * m.quarter + side * m.eighth
                    mine = m.acc[span(start + r, m.step, 16), m.lanes(a)].astype(F32)
                    m.mixed[a, side, rows] = (mine + m.relay[a, side, rows].astype(F32)).astype(BF)

                every(m.eighth, m.step, add)
        self.start("mixed", a)

    def second(self, a):
        self.wait("near", a)
        self.wait("mixed", a)
        i = self.spot[ORDERS[a][0]]
        for m in self.mats:

            def add(r, m=m):
                rows = pl.ds(r, m.step)
                total = m.acc[span(i * m.quarter + r, m.step, 16), m.lanes(a)].astype(F32)
                total = total + m.first[a, 0, rows].astype(F32) + m.first[a, 1, rows].astype(F32)
                m.first_sum[a, rows] = total.astype(BF)

            every(m.quarter, m.step, add)
        self.start("second", a)

    def third(self, a):
        self.wait("second", a)
        _, two, three = ORDERS[a]
        j, k = self.spot[two], self.spot[three]
        for m in self.mats:
            row, lane = m.spot16(j)
            total = m.first_sum[a, span(row, m.small[0], 16), span(lane, m.small[1])].astype(F32)
            for d in range(3):
                total = total + m.second[a, d].astype(F32)
            m.third[a, k] = total.astype(BF)
        self.start("third", a)

    def back(self, a):
        self.wait("third", a)
        for t, m in enumerate(self.mats):
            low = m.third[a, 0].astype(F32) + m.third[a, 1].astype(F32)
            high = m.third[a, 2].astype(F32) + m.third[a, 3].astype(F32)
            m.own[a] = (low + high).astype(BF)
            self.keeps[t, a].start()
        self.start("back", a)

    def ring(self, a):
        self.wait("back", a)
        for t in range(len(self.mats)):
            self.keeps[t, a].wait()
        self.start("ring", a)
        self.start_core(a, (0,))

    def pass_on(self, a):
        self.wait("ring", a)
        self.start("pass", a)
        self.start_core(a, (1, 2))

    def core(self, a):
        self.wait("pass", a)
        self.start_core(a, (3,))

    def finish(self, a):
        self.wait("core", a)


class HeadSum:
    def __init__(self, spot, slots, source, got, even, odd):
        self.spot, self.source, self.got, self.even, self.odd = spot, source, got, even, odd
        c, x, y, zh, zl = (spot[a] for a in ("c", "x", "y", "zh", "zl"))
        self.block = zh * 4 + x
        self.is_even, self.is_odd = c == 0, c == 1
        self.active = (c == 0) | (zl == y % 2)
        self.pieces = []
        for d in range(1, BLOCKS):
            to = (self.block + d) % BLOCKS
            piece = source.at[pl.ds(pl.multiple_of(to * SHARE, 16), SHARE)]
            self.pieces.append(send(piece, got.at[d - 1], *slots.take(), block_id(to)))
        self.copies = {}
        whole = slice(None)
        for p in range(PARTS):
            rows = pl.ds(p * SHARE // PARTS, SHARE // PARTS)
            for stage in range(4):
                done = ORDERS[p][:stage]
                in_x = whole if "x" in done else x
                in_zh = whole if "z" in done else zh
                even_at = (in_zh, whole if "z" in done else zl, in_x, whole if "y" in done else y, rows)
                if "y" not in done:
                    in_y = (y % 2, y // 2)
                else:
                    in_y = (whole if "z" in done else zl, whole)
                odd_at = (in_zh, in_x, *in_y, rows)
                for side, piece in enumerate((even.at[even_at], odd.at[odd_at])):
                    if stage == 3:
                        self.copies[p, stage, side] = [send(piece, piece, *slots.take(), on_axis("c", 1 - c))]
                        continue
                    axis = ORDERS[p][stage]
                    self.copies[p, stage, side] = [
                        send(piece, piece, *slots.take(), on_axis(axis, (spot[axis] + d) % 4)) for d in range(1, 4)
                    ]

    def start_sum(self):
        for copy in self.pieces:
            pl.when(self.active)(copy.start)

    def finish_sum(self):
        spot = self.spot

        def body():
            for copy in self.pieces:
                copy.wait()
            total = self.source[pl.ds(pl.multiple_of(self.block * SHARE, 16), SHARE)].astype(F32)
            for d in range(BLOCKS - 1):
                total = total + self.got[d].astype(F32)
            total = total.astype(BF)

            def keep_even():
                self.even[spot["zh"], spot["zl"], spot["x"], spot["y"]] = total

            def keep_odd():
                self.odd[spot["zh"], spot["x"], spot["y"] % 2, spot["y"] // 2] = total

            pl.when(self.is_even)(keep_even)
            pl.when(self.is_odd)(keep_odd)

        pl.when(self.active)(body)

    def sends(self, p, stage):
        return self.is_odd if stage > 0 and ORDERS[p][:stage] != ("x",) else self.is_odd & self.active

    def start(self, p, stage):
        def go(side):
            for copy in self.copies[p, stage, side]:
                copy.start()

        pl.when(self.is_even)(lambda: go(0))
        pl.when(self.sends(p, stage) if stage < 3 else self.is_odd)(lambda: go(1))

    def finish(self, p, stage):
        if stage == 3:
            for side, mine in enumerate((self.is_even, self.is_odd)):
                copy = self.copies[p, stage, side][0]
                pl.when(mine)(copy.wait_send)
                pl.when(jnp.logical_not(mine))(copy.wait_recv)
            return

        def even():
            for copy in self.copies[p, stage, 0]:
                copy.wait()

        def odd_sent():
            for copy in self.copies[p, stage, 1]:
                copy.wait_send()

        pl.when(self.is_even)(even)
        pl.when(self.sends(p, stage))(odd_sent)
        axis = ORDERS[p][stage]
        early = stage == 0 or ORDERS[p][:stage] == ("x",)
        for d in range(1, 4):
            came = (self.spot[axis] + 4 - d) % 4
            sent = self.is_odd
            if early and axis == "x":
                sent = sent & self.active
            if early and axis == "y":
                sent = sent & (self.spot["zl"] == came % 2)
            if early and axis == "z":
                sent = sent & (came % 2 == self.spot["y"] % 2)
            pl.when(sent)(self.copies[p, stage, 1][d - 1].wait_recv)


HEAD_SLOTS = 7 + 2 * PARTS * (3 * 3 + 1)


class TableSum:
    def __init__(self, slots, table, parts, got):
        self.me = my_block()
        self.table, self.parts, self.got = table, parts, got
        self.shares, self.spread = [], []
        for d in range(1, BLOCKS):
            to = (self.me + d) % BLOCKS
            self.shares.append(send(parts.at[d - 1], got.at[d - 1], *slots.take(), block_id(to)))
        mine = table.at[pl.ds(0, ITEM), span(self.me * SLOTS, SLOTS)]
        for d in range(1, BLOCKS):
            to = (self.me + d) % BLOCKS
            self.spread.append(send(mine, mine, *slots.take(), block_id(to)))

    def fill(self, items, codes_ref, weights_ref, hot):
        for t in range(1, BLOCKS + 1):
            s = (self.me + t) % BLOCKS
            slot = t % 2
            for i in range(CHUNKS):
                cols = pl.ds(i * CHUNK, CHUNK)
                hot[slot, :, cols] = one_hot(codes_ref[pl.ds(s, 1), cols], weights_ref[pl.ds(s, 1), cols])
            got = nt(items[...], hot[slot])
            self.table[pl.ds(ITEM, STACK - ITEM), span(s * SLOTS, SLOTS)] = got[ITEM:].astype(BF)
            if t < BLOCKS:
                self.parts[t - 1] = got[:ITEM].astype(BF)
                self.shares[t - 1].start()
            else:
                self.own = got[:ITEM]

    def add(self):
        total = self.own
        for d in range(1, BLOCKS):
            self.shares[d - 1].wait()
            total = total + self.got[d - 1].astype(F32)
        self.table[pl.ds(0, ITEM), span(self.me * SLOTS, SLOTS)] = total.astype(BF)
        for copy in self.spread:
            copy.start()

    def finish(self):
        for copy in self.spread:
            copy.wait()


TABLE_SLOTS = 2 * (BLOCKS - 1)


class Halo:
    def __init__(self, slots, edges, came):
        me = my_block()
        down, up = block_id((me + BLOCKS - 1) % BLOCKS), block_id((me + 1) % BLOCKS)
        self.copies = [
            send(edges.at[0], came.at[1], *slots.take(), down),
            send(edges.at[1], came.at[0], *slots.take(), up),
        ]

    def start(self):
        for copy in self.copies:
            copy.start()

    def finish(self):
        for copy in self.copies:
            copy.wait()


HALO_SLOTS = 2


class Scatter:
    def __init__(self, slots_send, slots_recv, local, chunks, out):
        self.me = my_member()
        self.owner, self.head = owns(self.me), head_at(self.me)
        self.send_sem, self.recv_sem, self.local = slots_send, slots_recv, local
        self.chunks, self.out = chunks, out

    def copy(self, p):
        return send(
            self.chunks.at[p], self.out.at[self.head], self.send_sem.at[p], self.recv_sem.at[self.head], member_id(p)
        )

    def keep(self, p):
        return pltpu.make_async_copy(self.chunks.at[p], self.out.at[self.head], self.local)

    def start(self, p):
        pl.when(self.owner & (self.me != p))(lambda: self.copy(p).start())
        pl.when(self.owner & (self.me == p))(lambda: self.keep(p).start())

    def finish(self):
        for h in range(HEADS):
            at = owner_of(h)
            got = send(self.chunks.at[0], self.out.at[h], self.send_sem.at[0], self.recv_sem.at[h], member_id(at))
            pl.when(self.me != at)(got.wait_recv)
        for p in range(MEMBERS):
            pl.when(self.owner & (self.me != p))(self.copy(p).wait_send)
        pl.when(self.owner)(self.keep(self.me).wait)


class Gather:
    def __init__(self, slots_send, slots_recv, local, chunks, out):
        self.me = my_member()
        self.owner, self.head = owns(self.me), head_at(self.me)
        self.chunks, self.out, self.send_sem, self.recv_sem = chunks, out, slots_send, slots_recv
        self.keep = pltpu.make_async_copy(chunks.at[self.head], out.at[self.me], local)
        self.copies = []
        for d in range(1, MEMBERS):
            to = (self.me + d) % MEMBERS
            copy = send(chunks.at[head_at(to)], out.at[self.me], slots_send.at[d], slots_recv.at[self.me], member_id(to))
            self.copies.append((owns(to), copy))

    def start(self):
        for wanted, copy in self.copies:
            pl.when(wanted)(copy.start)
        self.keep.start()

    def finish(self):
        self.keep.wait()
        for d in range(1, MEMBERS):
            came = (self.me + d) % MEMBERS
            got = send(self.chunks.at[0], self.out.at[came], self.send_sem.at[0], self.recv_sem.at[came], member_id(came))
            pl.when(self.owner)(got.wait_recv)
        for wanted, copy in self.copies:
            pl.when(wanted)(copy.wait_send)


def block_peers():
    me = my_block()
    return [block_id((me + d) % BLOCKS) for d in range(1, BLOCKS)]


def member_peers():
    me = my_member()
    return [member_id((me + d) % MEMBERS) for d in range(1, MEMBERS)]


def iota(shape, dim):
    return lax.broadcasted_iota(I32, shape, dim)


def tap_row(conv_w, head, flip):
    mine = jnp.where(iota((HEADS, 65), 0) == head, conv_w[...], 0.0)
    row, col = iota((65, 256), 0), iota((65, 256), 1)
    place = jnp.where(col == (160 - row if flip else row + 96), 1.0, 0.0)
    return jnp.sum(nn(mine, place, precision=HIGHEST), axis=0, keepdims=True)


def head_column(vector, head):
    rows = jnp.broadcast_to(vector[...][None, :], (128, D))
    pick = jnp.where(iota((HEAD, D), 1) == iota((HEAD, D), 0) + head * HEAD, 1.0, 0.0)
    return nt(pick, rows, precision=HIGHEST)[:, 0:1]


def item_masks(cuts, block):
    start = block * BLOCK - EDGE
    pos = start + iota((1, EXT), 1)
    item = jnp.zeros((1, EXT), I32)
    for k in range(1, 4):
        item = item + jnp.where(pos >= cuts[k], 1, 0)
    longest = jnp.where(cuts[2] - cuts[1] > 1024, 1, 2)
    outer = jnp.where(block < 4, 0, 3)
    inner = jnp.where(block < 4, 1, 2)
    valid = jnp.where((pos >= 0) & (pos < TOTAL), 1.0, 0.0)
    is_long = jnp.where(item == longest, valid, 0.0)
    is_outer = jnp.where(item == outer, valid, 0.0)
    is_inner = jnp.where(item == inner, valid, 0.0) - jnp.where(inner == longest, is_long, 0.0)
    return jnp.concatenate([is_long, is_outer, is_inner, jnp.zeros((5, EXT), F32)], axis=0)


def pack(rows):
    return jnp.concatenate([rows[:SIDE], rows[SIDE:]], axis=1).astype(BF)


def unpack_heads(chunk):
    pairs = []
    for i in range(HEADS // 2):
        a, b = chunk(2 * i), chunk(2 * i + 1)
        top = jnp.concatenate([a[:, :HEAD], b[:, :HEAD]], axis=1)
        low = jnp.concatenate([a[:, HEAD:], b[:, HEAD:]], axis=1)
        pairs.append(jnp.concatenate([top, low], axis=0))
    return jnp.concatenate(pairs, axis=1)


def norm_forward(values):
    centred = values - jnp.mean(values, axis=-1, keepdims=True)
    recip = lax.rsqrt(jnp.mean(centred * centred, axis=-1, keepdims=True) + EPS_NORM)
    return centred * recip, recip


def norm_backward(grad, hat, recip, gain):
    scaled = grad * gain
    mean = jnp.mean(scaled, axis=-1, keepdims=True)
    along = jnp.mean(scaled * hat, axis=-1, keepdims=True)
    return recip * (scaled - mean - hat * along)


def column_sums(values):
    return jnp.sum(values, axis=0, keepdims=True)


LAYER_SEMS = (
    4 * MEMBERS + 1 + 7 + 6 + 2 * TABLE_SLOTS + 2 * HALO_SLOTS + BIG_SLOTS + HEAD_SLOTS + 2 * VEC_SLOTS
)


def flip_in(values, dest, start):
    dest[start : start + values.shape[1], :] = jnp.transpose(values.astype(F32)).astype(BF)


def layer_kernel(
    tokens, q_codes, k_codes, hyper, cuts, b_query, b_key, b_value, conv_w, b_out, ln1_gain, ln1_bias, b_in, b_back,
    ln2_gain, ln2_bias, cot, w_query, w_key, w_value, w_out, w_in, w_back,
    output, grad_tokens, sum_a, sum_b, vec_out, small_out, even, odd,
    other_tok, qkv, weights, codes, planes, masks, table, estimate, scale, v_ext,
    codes_in, planes_in, parts, got, v_edges, v_came, att_out, att,
    grad_out, chunks_in, g_edges, g_came, g_parts, g_got, gtable, g_chunks, g_in, head_w, head_got, vec_buf, small_buf,
    resid, att_t, hidden_t, act_t, inner_g, outer_g, branch_g, att_s, hidden_s, act_s, inner_s, outer_s, branch_s,
    local, send_sem, recv_sem, *big_refs,
):
    spot = here()
    me, block, core = my_member(), my_block(), spot["c"]
    head, owner, mine = head_at(me), owns(me), me % 8
    far = {"zh": 1 - spot["zh"], "zl": 1 - spot["zl"]}
    hello(member_peers() + block_peers() + [far])

    def sixteen(k):
        at = pl.ds(k * MEMBERS, MEMBERS)
        return send_sem.at[at], recv_sem.at[at]

    slots = Slots(send_sem, recv_sem)
    slots.used = 4 * MEMBERS
    sibling = on_axis("c", 1 - core)
    swap = send(tokens, other_tok, *slots.take(), sibling)
    spread = []
    for d in range(1, 8):
        piece = planes_in.at[mine]
        spread.append(send(piece, piece, *slots.take(), member_id(core * 8 + (mine + d) % 8)))
    acts = []
    for source, dest in ((hidden_t, hidden_s), (act_t, act_s), (att_t, att_s)):
        half = source.shape[0] // 2
        acts.append(send(source.at[span((1 - core) * half, half, 16)], dest, *slots.take(), sibling))
    for source, dest in ((inner_g, inner_s), (outer_g, outer_s), (branch_g, branch_s)):
        acts.append(send(source, dest, *slots.take(), sibling))
    sum_table = TableSum(slots, table, parts, got)
    sum_grads = TableSum(slots, gtable, g_parts, g_got)
    v_halo = Halo(slots, v_edges, v_came)
    g_halo = Halo(slots, g_edges, g_came)
    att_rows = Scatter(*sixteen(1), local.at[4], att_out, att)
    give_grad = Gather(*sixteen(2), local.at[8], grad_out, chunks_in)
    grad_rows = Scatter(*sixteen(3), local.at[9], g_chunks, g_in)
    heads = HeadSum(spot, slots, head_w, head_got, even, odd)
    vector = VectorSum(spot, slots, None, vec_buf)
    small = VectorSum(spot, slots, None, small_buf)
    v_bias = head_column(b_value, head)

    def front(w_all, w_t, items, hot, big_hot, conv, codes_out):
        loads = [
            pltpu.make_async_copy(w, w_all.at[k], local.at[k]) for k, w in enumerate((w_query, w_key, w_value))
        ]
        for load in loads:
            load.start()
        for h in range(HEADS):
            codes_out[h, 0:1, :] = q_codes[h]
            codes_out[h, 1:2, :] = k_codes[h]
        planes_in[mine] = hyper[0]
        masks[...] = item_masks(cuts, block)
        give = Gather(*sixteen(0), local.at[3], codes_out, codes_in)
        all_here(MEMBERS - 1 + BLOCKS - 1 + 1)

        give.start()
        swap.start()
        for copy in spread:
            copy.start()

        pick = jnp.where(iota((HEAD, D), 1) == iota((HEAD, D), 0) + head * HEAD, 1.0, 0.0).astype(BF)
        bias = jnp.concatenate([head_column(b_query, head), head_column(b_key, head), jnp.zeros((HEAD, 1), F32)], axis=0)
        for k, load in enumerate(loads):
            load.wait()
            w_t[k * HEAD : (k + 1) * HEAD, :] = nt(pick, w_all[k]).astype(BF)

        def project(source, start):
            def step(i, _):
                rows = span(i * CHUNK, CHUNK)
                qkv[:, span(start + i * CHUNK, CHUNK)] = nt(w_t[...], source[rows, :]) + bias
                return 0

            lax.fori_loop(0, ROWS // CHUNK, step, 0)

        project(tokens, core * ROWS)
        swap.wait()
        project(other_tok, (1 - core) * ROWS)
        v_edges[0] = qkv[2 * HEAD :, :EDGE].astype(BF)
        v_edges[1] = qkv[2 * HEAD :, BLOCK - EDGE :].astype(BF)
        v_halo.start()

        give.finish()
        for copy in spread:
            copy.wait()
        for b in range(BITS):
            planes[b * SETS : (b + 1) * SETS, :] = planes_in[:, b, :]
        for side in range(2):
            for s in range(SETS):
                for k in range(2):
                    codes[side, s : s + 1, k * ROWS : (k + 1) * ROWS] = codes_in[k * 8 + s, side : side + 1, :]

        def prepare(i, _):
            cols = span(i * CHUNK, CHUNK)
            inner = span(i * CHUNK + EDGE, CHUNK)
            weights[SETS:, cols] = hash_weight(qkv[HEAD : 2 * HEAD, cols], codes[1, :, cols], planes[...])
            items[:, cols] = by_item(qkv[2 * HEAD :, cols], jnp.ones((1, CHUNK), F32), masks[:, inner])
            return 0

        lax.fori_loop(0, CHUNKS, prepare, 0)
        sum_table.fill(items, codes.at[1], weights.at[pl.ds(SETS, SETS)], hot)

        def query_side(i, _):
            cols = span(i * CHUNK, CHUNK)
            inner = span(i * CHUNK + EDGE, CHUNK)
            weights[:SETS, cols] = hash_weight(qkv[:HEAD, cols], codes[0, :, cols], planes[...])
            v_ext[:, inner] = by_item(qkv[2 * HEAD :, cols] + v_bias, jnp.zeros((1, CHUNK), F32), masks[:, inner])
            return 0

        lax.fori_loop(0, CHUNKS, query_side, 0)
        sum_table.add()
        v_halo.finish()
        none = jnp.zeros((1, EDGE), F32)
        v_ext[:, :EDGE] = by_item(v_came[0].astype(F32) + v_bias, none, masks[:, :EDGE])
        v_ext[:, EDGE + BLOCK :] = by_item(v_came[1].astype(F32) + v_bias, none, masks[:, EDGE + BLOCK :])
        lower, upper = circulant(tap_row(conv_w, head, True))

        def convolve(i, _):
            at = i * 256
            mixed = nn(v_ext[:, span(at, 256)], lower) + nn(v_ext[:, span(at + 256, 256)], upper)
            conv[:, span(at, 256)] = pick_item(mixed, masks[:, span(at + EDGE, 256)])[:HEAD] + v_bias
            return 0

        lax.fori_loop(0, BLOCK // 256, convolve, 0)
        sum_table.finish()

        def read(i, _):
            cols = span(i * CHUNK, CHUNK)
            own = masks[:, span(i * CHUNK + EDGE, CHUNK)]
            for s in range(SETS):
                big_hot[s * SLOTS : (s + 1) * SLOTS, :] = one_hot(codes[0, s : s + 1, cols], weights[s : s + 1, cols])
            found = pick_item(nn(table[...], big_hot[...]), own)
            recip = 1.0 / (found[HEAD : HEAD + 1] + 1.0)
            est = (found[:HEAD] - v_bias) * recip
            estimate[:, cols] = est
            scale[:, cols] = recip
            rows = jnp.transpose(est + conv[:, cols])
            for u in range(PER_CHUNK):
                p = i * PER_CHUNK + u
                att_out[p] = pack(rows[u * OWN : (u + 1) * OWN])
                att_rows.start(p)
            return 0

        lax.fori_loop(0, CHUNKS, read, 0)

    def feed_forward(w_out_v, w_in_v, w_back_v, slope_v):
        loads = [
            pltpu.make_async_copy(a, b, local.at[5 + k])
            for k, (a, b) in enumerate([(w_out, w_out_v), (w_in, w_in_v), (w_back, w_back_v)])
        ]
        for load in loads:
            load.start()
        att_rows.finish()
        gain1, gain2 = ln1_gain[...][None, :], ln2_gain[...][None, :]
        attended = unpack_heads(lambda h: att[h])
        flip_in(attended, att_t, 0)
        acts[2].start()
        loads[0].wait()
        branch = nn(attended, w_out_v[...]) + b_out[...][None, :]
        hat1, recip1 = norm_forward(tokens[span(mine * OWN, OWN, 16), :].astype(F32) + branch)
        hidden = hat1 * gain1 + ln1_bias[...][None, :]
        hidden_low = hidden.astype(BF)
        flip_in(hidden, hidden_t, 0)
        acts[0].start()
        loads[1].wait()
        outer = b_back[...][None, :]
        for k in range(FF // D):
            cols = slice(k * D, (k + 1) * D)
            inner = nn(hidden_low, w_in_v[:, cols]) + b_in[pl.ds(k * D, D)][None, :]
            phi = 0.5 * (1.0 + lax.erf(inner * (2.0**-0.5)))
            slope_v[:, cols] = phi + inner * (jnp.exp(-0.5 * inner * inner) * 0.3989422804014327)
            act = (inner * phi).astype(BF)
            flip_in(act, act_t, k * D)
            if k == 0:
                loads[2].wait()
            outer = outer + nn(act, w_back_v[cols, :])
        acts[1].start()
        hat2, recip2 = norm_forward(hidden + outer)
        output[...] = hat2 * gain2 + ln2_bias[...][None, :]
        got = cot[...]
        sum_grad = norm_backward(got, hat2, recip2, gain2)
        outer_grad = sum_grad.astype(BF)
        outer_g[...] = outer_grad
        acts[4].start()
        hidden_grad = sum_grad
        sums = [column_sums(outer_grad.astype(F32)), column_sums(got * hat2), column_sums(got)]
        bias_rows = []
        for k in range(FF // D):
            cols = slice(k * D, (k + 1) * D)
            act_grad = nt(outer_grad, w_back_v[cols, :])
            inner_grad = (act_grad * slope_v[:, cols]).astype(BF)
            inner_g[:, cols] = inner_grad
            bias_rows.append(column_sums(inner_grad.astype(F32)))
            hidden_grad = hidden_grad + nt(inner_grad, w_in_v[:, cols])
        acts[3].start()
        grad1 = norm_backward(hidden_grad, hat1, recip1, gain1)
        resid[...] = grad1
        branch_grad = grad1.astype(BF)
        branch_g[...] = branch_grad
        att_grad = nt(branch_grad, w_out_v[...])
        for h in range(HEADS):
            grad_out[h] = pack(att_grad[:, h * HEAD : (h + 1) * HEAD])
        give_grad.start()
        acts[5].start()
        rows = [column_sums(branch_grad.astype(F32)), column_sums(hidden_grad * hat1), column_sums(hidden_grad)]
        vector.value = jnp.concatenate(rows + sums + bias_rows + [jnp.zeros((6, D), F32)], axis=0)
        vector.start(0)

    def backward(w_all, grad, den, items, hot, ext, rows_ref, g_all, mix, *accs):
        per = len(big_refs) // 2
        mats = [
            Matrix(*MATRICES[t], refs=(result, accs[t], *big_refs[t * per : (t + 1) * per]))
            for t, result in enumerate((sum_a, sum_b))
        ]
        sums = BigSum(spot, slots, local.at[pl.ds(10, 6)], mats)
        loads = [
            pltpu.make_async_copy(w, w_all.at[k], local.at[16 + k]) for k, w in enumerate((w_query, w_key, w_value))
        ]
        for load in loads:
            load.start()
        every_part = range(PARTS)

        def weight_part(a):
            mat_a, mat_b = mats
            rows = span(core * mat_a.half, mat_a.half, 16)
            start, stop = a * mat_a.part, min((a + 1) * mat_a.part, FF)
            into = nn(hidden_t[rows, :], inner_g[:, start:stop]) + nn(hidden_s[...], inner_s[:, start:stop])
            mat_a.acc[:, start:stop] = into.astype(BF)
            if stop == FF:
                into = nn(att_t[rows, :], branch_g[...]) + nn(att_s[...], branch_s[...])
                mat_a.acc[:, FF:] = into.astype(BF)
            lanes = slice(a * mat_b.part, (a + 1) * mat_b.part)
            rows = span(core * mat_b.half, mat_b.half, 16)
            into = nn(act_t[rows, :], outer_g[:, lanes]) + nn(act_s[...], outer_s[:, lanes])
            mat_b.acc[:, lanes] = into.astype(BF)

        for copy in acts:
            copy.wait()
        for a in every_part:
            weight_part(a)
            sums.begin(a)

        give_grad.finish()
        for p in range(MEMBERS):
            both = chunks_in[p].astype(F32)
            rows_ref[p * OWN : p * OWN + SIDE] = both[:, :HEAD]
            rows_ref[p * OWN + SIDE : (p + 1) * OWN] = both[:, HEAD:]

        def prepare(i, _):
            cols = span(i * CHUNK, CHUNK)
            own = masks[:, span(i * CHUNK + EDGE, CHUNK)]
            this = jnp.transpose(rows_ref[span(i * CHUNK, CHUNK), :])
            grad[:, cols] = this
            numer = this * scale[:, cols]
            mass = -jnp.sum(numer * estimate[:, cols], axis=0, keepdims=True)
            den[:, cols] = mass
            items[:, cols] = by_item(numer, mass, own)
            ext[:, span(i * CHUNK + EDGE, CHUNK)] = by_item(this, jnp.zeros((1, CHUNK), F32), own)
            return 0

        lax.fori_loop(0, CHUNKS, prepare, 0)
        g_edges[0] = grad[:, :EDGE].astype(BF)
        g_edges[1] = grad[:, BLOCK - EDGE :].astype(BF)
        g_halo.start()
        sum_grads.fill(items, codes.at[0], weights.at[pl.ds(0, SETS)], hot)

        def query_back(i, _):
            cols = span(i * CHUNK, CHUNK)
            own = masks[:, span(i * CHUNK + EDGE, CHUNK)]
            q_codes = codes[0, :, cols]
            numer = grad[:, cols] * scale[:, cols]
            mass = den[:, cols]
            found_all = []
            for s in range(SETS):
                one = one_hot(q_codes[s : s + 1], 1.0)
                found = pick_item(nn(table[:, s * SLOTS : (s + 1) * SLOTS], one), own)
                found_all.append(
                    jnp.sum(found[:HEAD] * numer, axis=0, keepdims=True) + found[HEAD : HEAD + 1] * mass
                )
            z_grad = jnp.concatenate(found_all, axis=0) * weights[:SETS, cols]
            g_all[:HEAD, cols] = hash_back(z_grad, qkv[:HEAD, cols], q_codes, planes[...]).astype(BF)
            return 0

        sum_grads.add()
        vector.finish(0)
        vector.start(1)
        lax.fori_loop(0, 1, query_back, 0)
        for a in every_part:
            sums.relay(a)
        lax.fori_loop(1, 3, query_back, 0)

        g_halo.finish()
        none = jnp.zeros((1, EDGE), F32)
        ext[:, :EDGE] = by_item(g_came[0].astype(F32), none, masks[:, :EDGE])
        ext[:, EDGE + BLOCK :] = by_item(g_came[1].astype(F32), none, masks[:, EDGE + BLOCK :])
        lower, upper = circulant(tap_row(conv_w, head, False))

        def conv_back(i, carry):
            at = i * 256
            mixed = nn(ext[:, span(at, 256)], lower) + nn(ext[:, span(at + 256, 256)], upper)
            mix[:, span(at, 256)] = pick_item(mixed, masks[:, span(at + EDGE, 256)])[:HEAD]
            this = ext[:, span(at + EDGE, 256)]
            return carry[0] + tn(v_ext[:, span(at, 256)], this), carry[1] + tn(v_ext[:, span(at + 256, 256)], this)

        zeros = jnp.zeros((256, 256), F32)
        c_low, c_high = lax.fori_loop(0, BLOCK // 256, conv_back, (zeros, zeros))
        row, col = iota((256, 256), 0), iota((256, 256), 1)
        skew = jnp.where(col < row, c_low, c_high)
        for b in range(8):
            skew = jnp.where(jnp.bitwise_and(row, 1 << b) != 0, pltpu.roll(skew, 256 - (1 << b), 1), skew)
        taps_grad = jnp.sum(skew, axis=0, keepdims=True)
        vector.finish(1)
        vector.start(2)
        for a in every_part:
            sums.second(a)
        lax.fori_loop(3, CHUNKS, query_back, 0)
        sum_grads.finish()

        def key_back(i, _):
            cols = span(i * CHUNK, CHUNK)
            own = masks[:, span(i * CHUNK + EDGE, CHUNK)]
            k_codes = codes[1, :, cols]
            k_w = weights[SETS:, cols]
            val = qkv[2 * HEAD :, cols]
            found_all = []
            v_grad = mix[:, cols]
            for s in range(SETS):
                one = one_hot(k_codes[s : s + 1], 1.0)
                found = pick_item(nn(gtable[:, s * SLOTS : (s + 1) * SLOTS], one), own)
                found_all.append(
                    jnp.sum(found[:HEAD] * val, axis=0, keepdims=True) + found[HEAD : HEAD + 1]
                )
                v_grad = v_grad + found[:HEAD] * k_w[s : s + 1]
            z_grad = jnp.concatenate(found_all, axis=0) * k_w
            k_grad = hash_back(z_grad, qkv[HEAD : 2 * HEAD, cols], k_codes, planes[...])
            g_all[HEAD : 2 * HEAD, cols] = k_grad.astype(BF)
            g_all[2 * HEAD : 3 * HEAD, cols] = v_grad.astype(BF)
            for k in range(3):
                rows = jnp.transpose(g_all[k * HEAD : (k + 1) * HEAD, cols].astype(F32))
                for u in range(PER_CHUNK):
                    g_chunks[i * PER_CHUNK + u, k] = pack(rows[u * OWN : (u + 1) * OWN])
            for u in range(PER_CHUNK):
                grad_rows.start(i * PER_CHUNK + u)
            return 0

        lax.fori_loop(0, 1, key_back, 0)
        for a in every_part:
            sums.third(a)
        lax.fori_loop(1, 2, key_back, 0)
        vector.finish(2)
        vector.start(3)
        lax.fori_loop(2, 3, key_back, 0)
        for a in every_part:
            sums.back(a)
        lax.fori_loop(3, CHUNKS, key_back, 0)

        g_all[3 * HEAD :, :] = jnp.zeros((HEAD, BLOCK), BF)
        own_part = g_all[: 3 * HEAD, span(core * ROWS, ROWS)]
        away = g_all[: 3 * HEAD, span((1 - core) * ROWS, ROWS)]
        w_grad = jnp.transpose(nn(own_part, tokens[...]) + nn(away, other_tok[...]))
        head_w[:D] = w_grad[:, : 2 * HEAD].astype(BF)
        head_w[D:] = jnp.concatenate([w_grad[: D // 2, 2 * HEAD :], w_grad[D // 2 :, 2 * HEAD :]], axis=1).astype(BF)
        heads.start_sum()
        for a in every_part:
            sums.ring(a)
        biases = nt(jnp.ones((8, BLOCK), BF), g_all[...])[0:1]
        mine = (iota((16, SMALL), 0) == head) & owner
        small.value = jnp.where(mine, jnp.concatenate([biases, taps_grad], axis=1), 0.0)
        small.start(0)
        vector.finish(3)
        vec_out[...] = vector.value
        heads.finish_sum()
        for p in every_part:
            heads.start(p, 0)
        small.finish(0)
        small.start(1)
        grad_rows.finish()
        total = resid[...]
        for k in range(3):
            loads[k].wait()
            total = total + nt(unpack_heads(lambda h, k=k: g_in[h, k]), w_all[k])
        grad_tokens[...] = total
        for p in every_part:
            heads.finish(p, 0)
            heads.start(p, 1)
        small.finish(1)
        small.start(2)
        for p in every_part:
            heads.finish(p, 1)
            heads.start(p, 2)
        for a in every_part:
            sums.pass_on(a)
        small.finish(2)
        small.start(3)
        for p in every_part:
            heads.finish(p, 2)
            heads.start(p, 3)
        for a in every_part:
            sums.core(a)
        small.finish(3)
        small_out[...] = small.value
        for p in every_part:
            heads.finish(p, 3)
        for a in every_part:
            sums.finish(a)

    pl.run_scoped(
        front, vmem(3, D, D), vmem(3 * HEAD, D), vmem(STACK, BLOCK), vmem(2, SLOTS, BLOCK), vmem(TABLE, CHUNK),
        vmem(HEAD, BLOCK, kind=F32), vmem(HEADS, 2, ROWS, kind=I32),
    )
    pl.run_scoped(feed_forward, vmem(D, D), vmem(D, FF), vmem(FF, D), vmem(OWN, FF, kind=F32))
    pl.run_scoped(
        backward, vmem(3, D, D), vmem(HEAD, BLOCK, kind=F32), vmem(1, BLOCK, kind=F32), vmem(STACK, BLOCK),
        vmem(2, SLOTS, BLOCK), vmem(STACK, EXT), vmem(BLOCK, HEAD, kind=F32), vmem(4 * HEAD, BLOCK),
        vmem(HEAD, BLOCK, kind=F32), *[Matrix(*m).whole() for m in MATRICES],
    )


PIECES = 8


def last_kernel(
    sum_a, sum_b, even, odd, vec, small, layer_out, tok_grad,
    output, grad_tokens, g_wq, g_bq, g_wk, g_bk, g_wv, g_bv, g_conv, g_wo, g_bo, g_l1g, g_l1b, g_wi, g_bi, g_wb, g_bb, g_l2g,
    g_l2b,
    a_in, b_in, a_out, b_out, qkv_out, in_sems, out_sems,
):
    a_rows, b_rows = D // PIECES, FF // PIECES
    loads = []
    for k in range(PIECES):
        rows = pl.ds(k * a_rows, a_rows)
        loads.append(pltpu.make_async_copy(sum_a.at[rows], a_in.at[rows], in_sems.at[2 * k]))
        rows = pl.ds(k * b_rows, b_rows)
        loads.append(pltpu.make_async_copy(sum_b.at[rows], b_in.at[rows], in_sems.at[2 * k + 1]))
    for load in loads:
        load.start()
    writes = []

    def write(source, dest):
        copy = pltpu.make_async_copy(source, dest, out_sems.at[len(writes)])
        copy.start()
        writes.append(copy)

    left = iota((SHARE, 128), 1) < HEAD

    def pieces(pair, j):
        zh, x = j // 4, j % 4
        if pair < 4:
            return even[zh, 0, x, pair].astype(F32), even[zh, 1, x, pair].astype(F32)
        return odd[zh, x, 0, pair - 4].astype(F32), odd[zh, x, 1, pair - 4].astype(F32)

    for pair in range(HEADS // 2):
        lanes = pl.ds(pair * 128, 128)
        for j in range(BLOCKS):
            a, b = pieces(pair, j)
            first = jnp.where(left, a, pltpu.roll(b, HEAD, 1))
            second = jnp.where(left, pltpu.roll(a, HEAD, 1), b)
            low, high = j * SHARE, (j + 1) * SHARE
            cut = min(max(D - low, 0), SHARE)
            if cut > 0:
                qkv_out[0, low : low + cut, lanes] = first[:cut]
                qkv_out[1, low : low + cut, lanes] = second[:cut]
            if cut < SHARE:
                start, stop = low + cut - D, high - D
                qkv_out[2, start:stop, lanes] = first[cut:]
                qkv_out[2, D // 2 + start : D // 2 + stop, lanes] = second[cut:]
    for k, dest in enumerate((g_wq, g_wk, g_wv)):
        write(qkv_out.at[k], dest)
    for k in range(PIECES):
        rows = pl.ds(k * a_rows, a_rows)
        loads[2 * k].wait()
        a_out[rows, :] = a_in[rows, :].astype(F32)
        write(a_out.at[rows, pl.ds(0, FF)], g_wi.at[rows])
        write(a_out.at[rows, pl.ds(FF, D)], g_wo.at[rows])
        rows = pl.ds(k * b_rows, b_rows)
        loads[2 * k + 1].wait()
        b_out[rows, :] = b_in[rows, :].astype(F32)
        write(b_out.at[rows], g_wb.at[rows])
    output[...] = layer_out[...]
    grad_tokens[...] = tok_grad[...]
    for k, dest in enumerate((g_bo, g_l1g, g_l1b, g_bb, g_l2g, g_l2b)):
        dest[...] = vec[k, :]
    for k in range(FF // D):
        g_bi[pl.ds(k * D, D)] = vec[6 + k, :]
    for k, dest in enumerate((g_bq, g_bk, g_bv)):
        for pair in range(HEADS // 2):
            lanes = slice(k * HEAD, (k + 1) * HEAD)
            dest[pl.ds(pair * 128, 128)] = jnp.concatenate(
                [small[2 * pair : 2 * pair + 1, lanes], small[2 * pair + 1 : 2 * pair + 2, lanes]], axis=1
            )[0]
    row, col = iota((256, 128), 0), iota((256, 128), 1)
    flip = jnp.where(row == 160 - col, 1.0, 0.0)
    g_conv[...] = nn(small[:, 256:], flip, precision=HIGHEST)[:HEADS, :65]
    for copy in writes:
        copy.wait()


VMEM_SPEC = pl.BlockSpec(memory_space=pltpu.VMEM)
ANY_SPEC = pl.BlockSpec(memory_space=pl.ANY)
SMEM_SPEC = pl.BlockSpec(memory_space=pltpu.SMEM)


def call(kernel, outs, scratch, *args, ident=None, far=(), far_outs=(), scalars=()):
    params = {} if ident is None else {"collective_id": ident, "has_side_effects": True}
    specs = [ANY_SPEC if k in far else SMEM_SPEC if k in scalars else VMEM_SPEC for k in range(len(args))]
    return pl.pallas_call(
        kernel,
        out_shape=[jax.ShapeDtypeStruct(shape, kind) for shape, kind in outs],
        in_specs=specs,
        out_specs=[ANY_SPEC if k in far_outs else VMEM_SPEC for k in range(len(outs))],
        scratch_shapes=scratch,
        compiler_params=pltpu.CompilerParams(vmem_limit_bytes=VMEM_LIMIT, **params),
    )(*args)


def per_device(
    tokens, item_cuts, q_codes, k_codes, hyperplanes, w_query, b_query, w_key, b_key,
    w_value, b_value, conv_weight, w_out, b_out, ln1_gain, ln1_bias, w_in, b_in, w_back,
    b_back, ln2_gain, ln2_bias, cotangent,
):
    chunk = (SIDE, 128)
    layer_out, tok_grad, sum_a, sum_b, vec_sum, small_sum, even, odd = call(
        layer_kernel,
        [
            ((OWN, D), F32), ((OWN, D), F32), ((D, WIDE), BF), ((FF, D), BF), ((16, D), F32), ((16, SMALL), F32),
            ((2, 2, 4, 4, SHARE, 128), BF), ((2, 4, 2, 2, SHARE, 128), BF),
        ],
        [
            vmem(ROWS, D), vmem(3 * HEAD, BLOCK, kind=F32), vmem(2 * SETS, BLOCK, kind=F32),
            vmem(2, SETS, BLOCK, kind=I32), vmem(BITS * SETS, HEAD, kind=F32), vmem(8, EXT, kind=F32),
            vmem(STACK, TABLE), vmem(HEAD, BLOCK, kind=F32), vmem(1, BLOCK, kind=F32), vmem(STACK, EXT),
            vmem(MEMBERS, 2, ROWS, kind=I32), vmem(SETS, BITS, HEAD, kind=F32), vmem(BLOCKS - 1, ITEM, SLOTS),
            vmem(BLOCKS - 1, ITEM, SLOTS), vmem(2, HEAD, EDGE), vmem(2, HEAD, EDGE), vmem(MEMBERS, *chunk),
            vmem(HEADS, *chunk),
            vmem(HEADS, *chunk), vmem(MEMBERS, *chunk), vmem(2, HEAD, EDGE), vmem(2, HEAD, EDGE),
            vmem(BLOCKS - 1, ITEM, SLOTS), vmem(BLOCKS - 1, ITEM, SLOTS), vmem(STACK, TABLE),
            vmem(MEMBERS, 3, *chunk), vmem(HEADS, 3, *chunk), vmem(HEAD_ROWS, 128), vmem(BLOCKS - 1, SHARE, 128),
            vmem(4, 4, 16, D, kind=F32), vmem(4, 4, 16, SMALL, kind=F32),
            vmem(OWN, D, kind=F32), vmem(D, OWN), vmem(D, OWN), vmem(FF, OWN), vmem(OWN, FF), vmem(OWN, D),
            vmem(OWN, D), vmem(D // 2, OWN), vmem(D // 2, OWN), vmem(FF // 2, OWN), vmem(OWN, FF), vmem(OWN, D),
            vmem(OWN, D), dma(19), dma(LAYER_SEMS), dma(LAYER_SEMS),
        ]
        + Matrix(*MATRICES[0]).scratch()
        + Matrix(*MATRICES[1]).scratch(),
        tokens, q_codes.transpose(1, 0, 2), k_codes.transpose(1, 0, 2), hyperplanes.transpose(0, 2, 1), item_cuts,
        b_query, b_key, b_value, conv_weight, b_out, ln1_gain, ln1_bias, b_in, b_back, ln2_gain, ln2_bias, cotangent,
        w_query, w_key, w_value, w_out, w_in, w_back,
        ident=0, far=(17, 18, 19, 20, 21, 22), far_outs=(2, 3), scalars=(4,),
    )
    square, line = ((D, D), F32), ((D,), F32)
    return call(
        last_kernel,
        [
            ((OWN, D), F32), ((OWN, D), F32), square, line, square, line, square, line, ((HEADS, 65), F32), square, line, line, line,
            ((D, FF), F32), ((FF,), F32), ((FF, D), F32), line, line, line,
        ],
        [
            vmem(D, WIDE), vmem(FF, D), vmem(D, WIDE, kind=F32), vmem(FF, D, kind=F32), vmem(3, D, D, kind=F32),
            dma(2 * PIECES), dma(3 + 3 * PIECES),
        ],
        sum_a, sum_b, even, odd, vec_sum, small_sum, layer_out, tok_grad,
        far=(0, 1), far_outs=(2, 4, 6, 9, 13, 15),
    )


def solution(mesh):
    grid = Mesh(mesh.devices.reshape(2, 4, 2, 4, 2), ALL_AXES)
    rows = ("zh", "x", "c")
    sets = ("y", "zl")
    placed = (
        P(rows, None), P(), P(sets, None, rows), P(sets, None, rows), P(sets, None, None),
    ) + (P(),) * 17 + (P(ALL_AXES, None),)
    return jax.shard_map(
        per_device,
        mesh=grid,
        in_specs=placed,
        out_specs=(P(ALL_AXES, None), P(ALL_AXES, None)) + (P(),) * 17,
        check_vma=False,
    )
```

```python
import jax
import jax.numpy as jnp
from jax import lax
from jax.experimental import pallas as pl
from jax.experimental.pallas import tpu as pltpu
from jax.sharding import Mesh, PartitionSpec as P

BF = jnp.bfloat16
F32 = jnp.float32
I32 = jnp.int32
HIGHEST = lax.Precision.HIGHEST
MESH = pl.DeviceIdType.MESH
EPS_NORM = 1e-05
EPS_UNIT = 1e-06

D = 768
HEADS = 12
HEAD = 64
SETS = 8
BITS = 8
SLOTS = 256
TABLE = SETS * SLOTS
FF = 3072
ROWS = 1280
BLOCK = 2560
BLOCKS = 8
OWN = 160
SIDE = OWN // 2
MEMBERS = 16
EDGE = 128
EXT = BLOCK + 2 * EDGE
TOTAL = 20480
CHUNK = 640
CHUNKS = BLOCK // CHUNK
PER_CHUNK = CHUNK // OWN
ITEM = 80
CLASSES = 3
STACK = ITEM * CLASSES
SHARE = 144
HEAD_ROWS = D + D // 2
SMALL = 512
WIDE = FF + D
VMEM_LIMIT = 61 * 1024 * 1024

BLOCK_AXES = ("zh", "x")
ALL_AXES = ("zh", "x", "c", "y", "zl")


def nt(left, right, **kw):
    return lax.dot_general(left, right, (((1,), (1,)), ((), ())), preferred_element_type=F32, **kw)


def nn(left, right, **kw):
    return lax.dot_general(left, right, (((1,), (0,)), ((), ())), preferred_element_type=F32, **kw)


def tn(left, right, **kw):
    return lax.dot_general(left, right, (((0,), (0,)), ((), ())), preferred_element_type=F32, **kw)


def unit_of(proj):
    scale = lax.rsqrt(jnp.sum(proj * proj, axis=0, keepdims=True) + EPS_UNIT)
    return proj * scale, scale


def bits_of(codes):
    return [(jnp.bitwise_and(codes, 1 << b) != 0) for b in range(BITS)]


def hash_weight(proj, codes, planes):
    unit, _ = unit_of(proj)
    lifted = nn(planes, unit, precision=HIGHEST)
    total = None
    for b, bit in enumerate(bits_of(codes)):
        part = lifted[b * SETS : (b + 1) * SETS]
        part = jnp.where(bit, part, -part)
        total = part if total is None else total + part
    return jnp.exp(total)


def hash_back(z_grad, proj, codes, planes):
    unit, scale = unit_of(proj)
    lifted_grad = jnp.concatenate([jnp.where(bit, z_grad, -z_grad) for bit in bits_of(codes)], axis=0)
    unit_grad = tn(planes, lifted_grad, precision=HIGHEST)
    return scale * (unit_grad - unit * jnp.sum(unit * unit_grad, axis=0, keepdims=True))


def one_hot(codes_row, weight_row):
    width = codes_row.shape[1]
    slots = lax.broadcasted_iota(jnp.int32, (SLOTS, width), 0)
    return jnp.where(slots == codes_row, weight_row, 0.0).astype(BF)


def by_item(sums, mass, masks):
    width = sums.shape[1]
    lead = lax.broadcasted_iota(jnp.int32, (ITEM - HEAD, width), 0) == 0
    tail = jnp.where(lead, mass, 0.0)
    whole = jnp.concatenate([sums, tail], axis=0)
    return jnp.concatenate([whole * masks[w : w + 1] for w in range(CLASSES)], axis=0).astype(BF)


def pick_item(stacked, masks):
    total = None
    for w in range(CLASSES):
        part = stacked[w * ITEM : (w + 1) * ITEM] * masks[w : w + 1]
        total = part if total is None else total + part
    return total


def circulant(base):
    grid = jnp.broadcast_to(base, (256, 256))
    grid = pltpu.roll(grid, 0, 1, stride=1, stride_axis=0)
    row = lax.broadcasted_iota(jnp.int32, (256, 256), 0)
    col = lax.broadcasted_iota(jnp.int32, (256, 256), 1)
    return (
        jnp.where(col < row, grid, 0.0).astype(BF),
        jnp.where(col >= row, grid, 0.0).astype(BF),
    )


def member_id(member):
    return {"c": member // 8, "y": (member % 8) // 2, "zl": member % 2}


def block_id(block):
    return {"zh": block // 4, "x": block % 4}


def owns(member):
    return (member < 8) | (member % 2 == ((member % 8) // 2) % 2)


def head_at(member):
    return jnp.where(member < 8, member, 8 + (member % 8) // 2)


def owner_of(head):
    return head if head < 8 else 8 + (head - 8) * 2 + (head - 8) % 2


def my_member():
    return lax.axis_index("c") * 8 + lax.axis_index("y") * 2 + lax.axis_index("zl")


def my_block():
    return lax.axis_index("zh") * 4 + lax.axis_index("x")


def send(src, dst, send_sem, recv_sem, device):
    return pltpu.make_async_remote_copy(
        src_ref=src, dst_ref=dst, send_sem=send_sem, recv_sem=recv_sem,
        device_id=device, device_id_type=MESH,
    )


def on_axis(axis, k):
    return {"zh": k // 2, "zl": k % 2} if axis == "z" else {axis: k}


def here():
    spot = {a: lax.axis_index(a) for a in ALL_AXES}
    spot["z"] = spot["zh"] * 2 + spot["zl"]
    return spot


class Slots:
    def __init__(self, send_sem, recv_sem):
        self.send_sem, self.recv_sem, self.used = send_sem, recv_sem, 0

    def take(self):
        k = self.used
        self.used += 1
        return self.send_sem.at[k], self.recv_sem.at[k]


AXES = ("c", "x", "y", "z")
ORDERS = (("x", "y", "z"), ("y", "z", "x"), ("z", "x", "y"))
PARTS = 3
VEC_SLOTS = 1 + 3 * 3


class VectorSum:
    def __init__(self, spot, slots, value, buffer):
        self.spot, self.value, self.buffer, self.copies = spot, value, buffer, {}
        for stage, axis in enumerate(AXES):
            size = 2 if axis == "c" else 4
            self.copies[stage] = []
            for d in range(1, size):
                k = spot[axis]
                here_ref = buffer.at[stage, k]
                copy = send(here_ref, here_ref, *slots.take(), on_axis(axis, (k + d) % size))
                self.copies[stage].append(copy)

    def start(self, stage):
        self.buffer[stage, self.spot[AXES[stage]]] = self.value
        for copy in self.copies[stage]:
            copy.start()

    def finish(self, stage):
        for copy in self.copies[stage]:
            copy.wait()
        total = self.buffer[stage, 0] + self.buffer[stage, 1]
        if stage > 0:
            total = total + (self.buffer[stage, 2] + self.buffer[stage, 3])
        self.value = total


def dma(count):
    return pltpu.SemaphoreType.DMA((count,))


def vmem(*shape, kind=BF):
    return pltpu.VMEM(shape, kind)


def hello(ids):
    barrier = pltpu.get_barrier_semaphore()
    for one in ids:
        pl.semaphore_signal(barrier, inc=1, device_id=one, device_id_type=MESH)


def all_here(count):
    pl.semaphore_wait(pltpu.get_barrier_semaphore(), count)


def every(count, step, body):
    def one(i, _):
        body(pl.multiple_of(i * step, 16))
        return 0

    lax.fori_loop(0, count // step, one, 0)


def span(start, size, unit=128):
    return pl.ds(pl.multiple_of(start, unit), size)


class Matrix:
    def __init__(self, shape, row_cut, refs=None):
        self.rows, self.cols = shape
        self.half = self.rows // 2
        self.part = self.cols // PARTS
        self.quarter = self.half // 4
        self.eighth = self.quarter // 2
        self.row_cut = row_cut
        self.col_cut = 4 // row_cut
        self.small = (self.quarter // row_cut, self.part // self.col_cut)
        self.step = 16 if self.part > 512 else 96
        if refs is not None:
            (
                self.result, self.acc, self.relay, self.mixed, self.first, self.first_sum, self.second, self.third,
                self.own,
            ) = refs

    def whole(self):
        return pltpu.VMEM((self.half, self.cols), BF)

    def scratch(self):
        quarter, eighth = (self.quarter, self.part), (self.eighth, self.part)
        shapes = [
            (PARTS, 2, *eighth), (PARTS, 2, *eighth), (PARTS, 2, *quarter), (PARTS, *quarter),
            (PARTS, 3, *self.small), (PARTS, 4, *self.small), (PARTS, *self.small),
        ]
        return [pltpu.VMEM(shape, BF) for shape in shapes]

    def lanes(self, a):
        return pl.ds(a * self.part, self.part)

    def spot16(self, j):
        return (j // self.col_cut) * self.small[0], (j % self.col_cut) * self.small[1]

    def part_of(self, q, a, side=None, base=0):
        start = base + q * self.quarter
        if side is None:
            return span(start, self.quarter, 16), self.lanes(a)
        return span(start + side * self.eighth, self.eighth, 16), self.lanes(a)


MATRICES = (((D, WIDE), 2), ((FF, D), 4))
BIG_SLOTS = 2 * PARTS * (6 + 3 * 3 + 4 + 4)


class BigSum:
    def __init__(self, spot, slots, local, mats):
        self.spot, self.mats, self.local = spot, mats, local
        c = spot["c"]
        sibling = on_axis("c", 1 - c)
        self.copies = {}
        self.keeps = {}
        for t, m in enumerate(mats):
            base = c * m.half
            for a in range(PARTS):
                one, two, three = ORDERS[a]
                i, j, k = spot[one], spot[two], spot[three]
                up, down, across = (i + 1) % 4, (i + 3) % 4, (i + 2) % 4
                to_up, to_down = on_axis(one, up), on_axis(one, down)

                def put(name, src, dst, device):
                    self.copies.setdefault((name, a), []).append(send(src, dst, *slots.take(), device))

                put("far", m.acc.at[m.part_of(across, a, 0)], m.relay.at[a, 0], to_up)
                put("far", m.acc.at[m.part_of(across, a, 1)], m.relay.at[a, 1], to_down)
                upper, lower = pl.ds(0, m.eighth), pl.ds(m.eighth, m.eighth)
                put("near", m.acc.at[m.part_of(up, a, 1)], m.first.at[a, 0, lower], to_up)
                put("near", m.acc.at[m.part_of(down, a, 0)], m.first.at[a, 1, upper], to_down)
                put("mixed", m.mixed.at[a, 0], m.first.at[a, 0, upper], to_up)
                put("mixed", m.mixed.at[a, 1], m.first.at[a, 1, lower], to_down)
                row, lane = m.spot16(j)
                at = (
                    span(base + i * m.quarter + row, m.small[0], 16),
                    span(a * m.part + lane, m.small[1]),
                )
                self.keeps[t, a] = pltpu.make_async_copy(m.own.at[a], m.result.at[at], local.at[t * PARTS + a])
                for d in range(1, 4):
                    to = (j + d) % 4
                    row, lane = m.spot16(to)
                    piece = m.first_sum.at[a, span(row, m.small[0], 16), span(lane, m.small[1])]
                    put("second", piece, m.second.at[a, d - 1], on_axis(two, to))
                    piece = m.third.at[a, k]
                    put("third", piece, piece, on_axis(three, (k + d) % 4))
                    put("back", m.own.at[a], m.result.at[at], on_axis(two, (j + d) % 4))
                mine = m.result.at[m.part_of(i, a, None, base)]
                put("ring", mine, mine, to_up)
                put("ring", mine, mine, to_down)
                piece = m.result.at[m.part_of(down, a, 0, base)]
                put("pass", piece, piece, to_up)
                piece = m.result.at[m.part_of(up, a, 1, base)]
                put("pass", piece, piece, to_down)
                for q in (i, up, down, across):
                    piece = m.result.at[m.part_of(q, a, None, base)]
                    put("core", piece, piece, sibling)

    def start(self, name, a):
        for copy in self.copies[name, a]:
            copy.start()

    def wait(self, name, a):
        for copy in self.copies[name, a]:
            copy.wait()

    def start_core(self, a, which):
        for t in range(len(self.mats)):
            for q in which:
                self.copies["core", a][4 * t + q].start()

    def begin(self, a):
        self.start("far", a)

    def near(self, a):
        self.start("near", a)

    def relay(self, a):
        self.wait("far", a)
        i = self.spot[ORDERS[a][0]]
        for m in self.mats:
            for side, q in ((0, (i + 1) % 4), (1, (i + 3) % 4)):

                def add(r, m=m, side=side, q=q):
                    rows = pl.ds(r, m.step)
                    start = q * m.quarter + side * m.eighth
                    mine = m.acc[span(start + r, m.step, 16), m.lanes(a)].astype(F32)
                    m.mixed[a, side, rows] = (mine + m.relay[a, side, rows].astype(F32)).astype(BF)

                every(m.eighth, m.step, add)
        self.start("mixed", a)

    def second(self, a):
        self.wait("near", a)
        self.wait("mixed", a)
        i = self.spot[ORDERS[a][0]]
        for m in self.mats:

            def add(r, m=m):
                rows = pl.ds(r, m.step)
                total = m.acc[span(i * m.quarter + r, m.step, 16), m.lanes(a)].astype(F32)
                total = total + m.first[a, 0, rows].astype(F32) + m.first[a, 1, rows].astype(F32)
                m.first_sum[a, rows] = total.astype(BF)

            every(m.quarter, m.step, add)
        self.start("second", a)

    def third(self, a):
        self.wait("second", a)
        _, two, three = ORDERS[a]
        j, k = self.spot[two], self.spot[three]
        for m in self.mats:
            row, lane = m.spot16(j)
            total = m.first_sum[a, span(row, m.small[0], 16), span(lane, m.small[1])].astype(F32)
            for d in range(3):
                total = total + m.second[a, d].astype(F32)
            m.third[a, k] = total.astype(BF)
        self.start("third", a)

    def back(self, a):
        self.wait("third", a)
        for t, m in enumerate(self.mats):
            low = m.third[a, 0].astype(F32) + m.third[a, 1].astype(F32)
            high = m.third[a, 2].astype(F32) + m.third[a, 3].astype(F32)
            m.own[a] = (low + high).astype(BF)
            self.keeps[t, a].start()
        self.start("back", a)

    def ring(self, a):
        self.wait("back", a)
        for t in range(len(self.mats)):
            self.keeps[t, a].wait()
        self.start("ring", a)
        self.start_core(a, (0,))

    def pass_on(self, a):
        self.wait("ring", a)
        self.start("pass", a)
        self.start_core(a, (1, 2))

    def core(self, a):
        self.wait("pass", a)
        self.start_core(a, (3,))

    def finish(self, a):
        self.wait("core", a)


class HeadSum:
    def __init__(self, spot, slots, source, got, even, odd):
        self.spot, self.source, self.got, self.even, self.odd = spot, source, got, even, odd
        c, x, y, zh, zl = (spot[a] for a in ("c", "x", "y", "zh", "zl"))
        self.block = zh * 4 + x
        self.is_even, self.is_odd = c == 0, c == 1
        self.active = (c == 0) | (zl == y % 2)
        self.pieces = []
        for d in range(1, BLOCKS):
            to = (self.block + d) % BLOCKS
            piece = source.at[pl.ds(pl.multiple_of(to * SHARE, 16), SHARE)]
            self.pieces.append(send(piece, got.at[d - 1], *slots.take(), block_id(to)))
        self.copies = {}
        whole = slice(None)
        for p in range(PARTS):
            rows = pl.ds(p * SHARE // PARTS, SHARE // PARTS)
            for stage in range(4):
                done = ORDERS[p][:stage]
                in_x = whole if "x" in done else x
                in_zh = whole if "z" in done else zh
                even_at = (in_zh, whole if "z" in done else zl, in_x, whole if "y" in done else y, rows)
                if "y" not in done:
                    in_y = (y % 2, y // 2)
                else:
                    in_y = (whole if "z" in done else zl, whole)
                odd_at = (in_zh, in_x, *in_y, rows)
                for side, piece in enumerate((even.at[even_at], odd.at[odd_at])):
                    if stage == 3:
                        self.copies[p, stage, side] = [send(piece, piece, *slots.take(), on_axis("c", 1 - c))]
                        continue
                    axis = ORDERS[p][stage]
                    self.copies[p, stage, side] = [
                        send(piece, piece, *slots.take(), on_axis(axis, (spot[axis] + d) % 4)) for d in range(1, 4)
                    ]

    def start_sum(self):
        for copy in self.pieces:
            pl.when(self.active)(copy.start)

    def finish_sum(self):
        spot = self.spot

        def body():
            for copy in self.pieces:
                copy.wait()
            total = self.source[pl.ds(pl.multiple_of(self.block * SHARE, 16), SHARE)].astype(F32)
            for d in range(BLOCKS - 1):
                total = total + self.got[d].astype(F32)
            total = total.astype(BF)

            def keep_even():
                self.even[spot["zh"], spot["zl"], spot["x"], spot["y"]] = total

            def keep_odd():
                self.odd[spot["zh"], spot["x"], spot["y"] % 2, spot["y"] // 2] = total

            pl.when(self.is_even)(keep_even)
            pl.when(self.is_odd)(keep_odd)

        pl.when(self.active)(body)

    def sends(self, p, stage):
        return self.is_odd if stage > 0 and ORDERS[p][:stage] != ("x",) else self.is_odd & self.active

    def start(self, p, stage):
        def go(side):
            for copy in self.copies[p, stage, side]:
                copy.start()

        pl.when(self.is_even)(lambda: go(0))
        pl.when(self.sends(p, stage) if stage < 3 else self.is_odd)(lambda: go(1))

    def finish(self, p, stage):
        if stage == 3:
            for side, mine in enumerate((self.is_even, self.is_odd)):
                copy = self.copies[p, stage, side][0]
                pl.when(mine)(copy.wait_send)
                pl.when(jnp.logical_not(mine))(copy.wait_recv)
            return

        def even():
            for copy in self.copies[p, stage, 0]:
                copy.wait()

        def odd_sent():
            for copy in self.copies[p, stage, 1]:
                copy.wait_send()

        pl.when(self.is_even)(even)
        pl.when(self.sends(p, stage))(odd_sent)
        axis = ORDERS[p][stage]
        early = stage == 0 or ORDERS[p][:stage] == ("x",)
        for d in range(1, 4):
            came = (self.spot[axis] + 4 - d) % 4
            sent = self.is_odd
            if early and axis == "x":
                sent = sent & self.active
            if early and axis == "y":
                sent = sent & (self.spot["zl"] == came % 2)
            if early and axis == "z":
                sent = sent & (came % 2 == self.spot["y"] % 2)
            pl.when(sent)(self.copies[p, stage, 1][d - 1].wait_recv)


HEAD_SLOTS = 7 + 2 * PARTS * (3 * 3 + 1)


class TableSum:
    def __init__(self, slots, table, parts, got):
        self.me = my_block()
        self.owner = owns(my_member())
        self.table, self.parts, self.got = table, parts, got
        self.shares, self.spread = [], []
        for d in range(1, BLOCKS):
            to = (self.me + d) % BLOCKS
            self.shares.append(send(parts.at[d - 1], got.at[d - 1], *slots.take(), block_id(to)))
        mine = table.at[pl.ds(0, ITEM), span(self.me * SLOTS, SLOTS)]
        for d in range(1, BLOCKS):
            to = (self.me + d) % BLOCKS
            self.spread.append(send(mine, mine, *slots.take(), block_id(to)))

    def fill(self, items, codes_ref, weights_ref, hot):
        for t in range(1, BLOCKS + 1):
            s = (self.me + t) % BLOCKS
            slot = t % 2
            for i in range(CHUNKS):
                cols = pl.ds(i * CHUNK, CHUNK)
                hot[slot, :, cols] = one_hot(codes_ref[pl.ds(s, 1), cols], weights_ref[pl.ds(s, 1), cols])
            got = nt(items[...], hot[slot])
            self.table[pl.ds(ITEM, STACK - ITEM), span(s * SLOTS, SLOTS)] = got[ITEM:].astype(BF)
            if t < BLOCKS:
                self.parts[t - 1] = got[:ITEM].astype(BF)
                pl.when(self.owner)(self.shares[t - 1].start)
            else:
                self.own = got[:ITEM]

    def add(self):
        total = self.own
        for d in range(1, BLOCKS):
            pl.when(self.owner)(self.shares[d - 1].wait)
            total = total + self.got[d - 1].astype(F32)
        self.table[pl.ds(0, ITEM), span(self.me * SLOTS, SLOTS)] = total.astype(BF)
        for copy in self.spread:
            pl.when(self.owner)(copy.start)

    def finish(self):
        for copy in self.spread:
            pl.when(self.owner)(copy.wait)


TABLE_SLOTS = 2 * (BLOCKS - 1)


class Halo:
    def __init__(self, slots, edges, came):
        me = my_block()
        down, up = block_id((me + BLOCKS - 1) % BLOCKS), block_id((me + 1) % BLOCKS)
        self.copies = [
            send(edges.at[0], came.at[1], *slots.take(), down),
            send(edges.at[1], came.at[0], *slots.take(), up),
        ]

    def start(self):
        for copy in self.copies:
            copy.start()

    def finish(self):
        for copy in self.copies:
            copy.wait()


HALO_SLOTS = 2


class Scatter:
    def __init__(self, slots_send, slots_recv, local, chunks, out):
        self.me = my_member()
        self.owner, self.head = owns(self.me), head_at(self.me)
        self.send_sem, self.recv_sem, self.local = slots_send, slots_recv, local
        self.chunks, self.out = chunks, out

    def copy(self, p):
        return send(
            self.chunks.at[p], self.out.at[self.head], self.send_sem.at[p], self.recv_sem.at[self.head], member_id(p)
        )

    def keep(self, p):
        return pltpu.make_async_copy(self.chunks.at[p], self.out.at[self.head], self.local)

    def start(self, p):
        pl.when(self.owner & (self.me != p))(lambda: self.copy(p).start())
        pl.when(self.owner & (self.me == p))(lambda: self.keep(p).start())

    def finish(self):
        for h in range(HEADS):
            at = owner_of(h)
            got = send(self.chunks.at[0], self.out.at[h], self.send_sem.at[0], self.recv_sem.at[h], member_id(at))
            pl.when(self.me != at)(got.wait_recv)
        for p in range(MEMBERS):
            pl.when(self.owner & (self.me != p))(self.copy(p).wait_send)
        pl.when(self.owner)(self.keep(self.me).wait)


class Gather:
    def __init__(self, slots_send, slots_recv, local, chunks, out):
        self.me = my_member()
        self.owner, self.head = owns(self.me), head_at(self.me)
        self.chunks, self.out, self.send_sem, self.recv_sem = chunks, out, slots_send, slots_recv
        self.keep = pltpu.make_async_copy(chunks.at[self.head], out.at[self.me], local)
        self.copies = []
        for d in range(1, MEMBERS):
            to = (self.me + d) % MEMBERS
            copy = send(chunks.at[head_at(to)], out.at[self.me], slots_send.at[d], slots_recv.at[self.me], member_id(to))
            self.copies.append((owns(to), copy))

    def start(self):
        for wanted, copy in self.copies:
            pl.when(wanted)(copy.start)
        self.keep.start()

    def finish(self):
        self.keep.wait()
        for d in range(1, MEMBERS):
            came = (self.me + d) % MEMBERS
            got = send(self.chunks.at[0], self.out.at[came], self.send_sem.at[0], self.recv_sem.at[came], member_id(came))
            pl.when(self.owner)(got.wait_recv)
        for wanted, copy in self.copies:
            pl.when(wanted)(copy.wait_send)


def block_peers():
    me = my_block()
    return [block_id((me + d) % BLOCKS) for d in range(1, BLOCKS)]


def member_peers():
    me = my_member()
    return [member_id((me + d) % MEMBERS) for d in range(1, MEMBERS)]


def iota(shape, dim):
    return lax.broadcasted_iota(I32, shape, dim)


def tap_row(conv_w, head, flip):
    mine = jnp.where(iota((HEADS, 65), 0) == head, conv_w[...], 0.0)
    row, col = iota((65, 256), 0), iota((65, 256), 1)
    place = jnp.where(col == (160 - row if flip else row + 96), 1.0, 0.0)
    return jnp.sum(nn(mine, place, precision=HIGHEST), axis=0, keepdims=True)


def head_column(vector, head):
    rows = jnp.broadcast_to(vector[...][None, :], (128, D))
    pick = jnp.where(iota((HEAD, D), 1) == iota((HEAD, D), 0) + head * HEAD, 1.0, 0.0)
    return nt(pick, rows, precision=HIGHEST)[:, 0:1]


def item_masks(cuts, block):
    start = block * BLOCK - EDGE
    pos = start + iota((1, EXT), 1)
    item = jnp.zeros((1, EXT), I32)
    for k in range(1, 4):
        item = item + jnp.where(pos >= cuts[k], 1, 0)
    longest = jnp.where(cuts[2] - cuts[1] > 1024, 1, 2)
    outer = jnp.where(block < 4, 0, 3)
    inner = jnp.where(block < 4, 1, 2)
    valid = jnp.where((pos >= 0) & (pos < TOTAL), 1.0, 0.0)
    is_long = jnp.where(item == longest, valid, 0.0)
    is_outer = jnp.where(item == outer, valid, 0.0)
    is_inner = jnp.where(item == inner, valid, 0.0) - jnp.where(inner == longest, is_long, 0.0)
    return jnp.concatenate([is_long, is_outer, is_inner, jnp.zeros((5, EXT), F32)], axis=0)


def pack(rows):
    return jnp.concatenate([rows[:SIDE], rows[SIDE:]], axis=1).astype(BF)


def unpack_heads(chunk):
    pairs = []
    for i in range(HEADS // 2):
        a, b = chunk(2 * i), chunk(2 * i + 1)
        top = jnp.concatenate([a[:, :HEAD], b[:, :HEAD]], axis=1)
        low = jnp.concatenate([a[:, HEAD:], b[:, HEAD:]], axis=1)
        pairs.append(jnp.concatenate([top, low], axis=0))
    return jnp.concatenate(pairs, axis=1)


def norm_forward(values):
    centred = values - jnp.mean(values, axis=-1, keepdims=True)
    recip = lax.rsqrt(jnp.mean(centred * centred, axis=-1, keepdims=True) + EPS_NORM)
    return centred * recip, recip


def norm_backward(grad, hat, recip, gain):
    scaled = grad * gain
    mean = jnp.mean(scaled, axis=-1, keepdims=True)
    along = jnp.mean(scaled * hat, axis=-1, keepdims=True)
    return recip * (scaled - mean - hat * along)


def column_sums(values):
    return jnp.sum(values, axis=0, keepdims=True)


LAYER_SEMS = (
    4 * MEMBERS + 1 + 7 + 6 + 2 * TABLE_SLOTS + 2 * HALO_SLOTS + BIG_SLOTS + HEAD_SLOTS + 2 * VEC_SLOTS
)


def flip_in(values, dest, start):
    dest[start : start + values.shape[1], :] = jnp.transpose(values.astype(F32)).astype(BF)


def layer_kernel(
    q_codes, k_codes, hyper, cuts, b_query, b_key, b_value, conv_w, b_out, ln1_gain, ln1_bias, b_in, b_back, ln2_gain,
    ln2_bias, all_tokens, all_cot, w_query, w_key, w_value, w_out, w_in, w_back,
    output, grad_tokens, sum_a, sum_b, vec_out, small_out, even, odd,
    tokens, cot, other_tok, qkv, weights, codes, planes, masks, table, estimate, scale, v_ext,
    codes_in, planes_in, parts, got, v_edges, v_came, att_out, att,
    grad_out, chunks_in, g_edges, g_came, g_parts, g_got, gtable, g_chunks, g_in, head_w, head_got, vec_buf, small_buf,
    resid, att_t, hidden_t, act_t, inner_g, outer_g, branch_g, att_s, hidden_s, act_s, inner_s, outer_s, branch_s,
    local, send_sem, recv_sem, *big_refs,
):
    spot = here()
    me, block, core = my_member(), my_block(), spot["c"]
    head, owner, mine = head_at(me), owns(me), me % 8
    far = {"zh": 1 - spot["zh"], "zl": 1 - spot["zl"]}
    hello(member_peers() + block_peers() + [far])

    def sixteen(k):
        at = pl.ds(k * MEMBERS, MEMBERS)
        return send_sem.at[at], recv_sem.at[at]

    slots = Slots(send_sem, recv_sem)
    slots.used = 4 * MEMBERS
    sibling = on_axis("c", 1 - core)
    swap = send(all_tokens, other_tok, *slots.take(), sibling)
    token_load = pltpu.make_async_copy(all_tokens, tokens, local.at[19])
    cot_load = pltpu.make_async_copy(all_cot, cot, local.at[20])
    token_load.start()
    cot_load.start()
    spread = []
    for d in range(1, 8):
        piece = planes_in.at[mine]
        spread.append(send(piece, piece, *slots.take(), member_id(core * 8 + (mine + d) % 8)))
    acts = []
    for source, dest in ((hidden_t, hidden_s), (act_t, act_s), (att_t, att_s)):
        half = source.shape[0] // 2
        acts.append(send(source.at[span((1 - core) * half, half, 16)], dest, *slots.take(), sibling))
    for source, dest in ((inner_g, inner_s), (outer_g, outer_s), (branch_g, branch_s)):
        acts.append(send(source, dest, *slots.take(), sibling))
    sum_table = TableSum(slots, table, parts, got)
    sum_grads = TableSum(slots, gtable, g_parts, g_got)
    v_halo = Halo(slots, v_edges, v_came)
    g_halo = Halo(slots, g_edges, g_came)
    att_rows = Scatter(*sixteen(1), local.at[4], att_out, att)
    give_grad = Gather(*sixteen(2), local.at[8], grad_out, chunks_in)
    grad_rows = Scatter(*sixteen(3), local.at[9], g_chunks, g_in)
    heads = HeadSum(spot, slots, head_w, head_got, even, odd)
    vector = VectorSum(spot, slots, None, vec_buf)
    small = VectorSum(spot, slots, None, small_buf)
    v_bias = head_column(b_value, head)

    def front(w_all, w_t, items, hot, big_hot, conv, codes_out):
        loads = [
            pltpu.make_async_copy(w, w_all.at[k], local.at[k]) for k, w in enumerate((w_query, w_key, w_value))
        ]
        for load in loads:
            load.start()
        for h in range(HEADS):
            codes_out[h, 0:1, :] = q_codes[h]
            codes_out[h, 1:2, :] = k_codes[h]
        planes_in[mine] = hyper[0]
        masks[...] = item_masks(cuts, block)
        give = Gather(*sixteen(0), local.at[3], codes_out, codes_in)
        all_here(MEMBERS - 1 + BLOCKS - 1 + 1)

        give.start()
        swap.start()
        for copy in spread:
            copy.start()

        pick = jnp.where(iota((HEAD, D), 1) == iota((HEAD, D), 0) + head * HEAD, 1.0, 0.0).astype(BF)
        bias = jnp.concatenate([head_column(b_query, head), head_column(b_key, head), jnp.zeros((HEAD, 1), F32)], axis=0)
        for k, load in enumerate(loads):
            load.wait()
            w_t[k * HEAD : (k + 1) * HEAD, :] = nt(pick, w_all[k]).astype(BF)

        def project(source, start):
            def step(i, _):
                rows = span(i * CHUNK, CHUNK)
                qkv[:, span(start + i * CHUNK, CHUNK)] = nt(w_t[...], source[rows, :]) + bias
                return 0

            lax.fori_loop(0, ROWS // CHUNK, step, 0)

        token_load.wait()
        project(tokens, core * ROWS)
        swap.wait()
        project(other_tok, (1 - core) * ROWS)
        v_edges[0] = qkv[2 * HEAD :, :EDGE].astype(BF)
        v_edges[1] = qkv[2 * HEAD :, BLOCK - EDGE :].astype(BF)
        v_halo.start()

        give.finish()
        for copy in spread:
            copy.wait()
        for b in range(BITS):
            planes[b * SETS : (b + 1) * SETS, :] = planes_in[:, b, :]
        for side in range(2):
            for s in range(SETS):
                for k in range(2):
                    codes[side, s : s + 1, k * ROWS : (k + 1) * ROWS] = codes_in[k * 8 + s, side : side + 1, :]

        def prepare(i, _):
            cols = span(i * CHUNK, CHUNK)
            inner = span(i * CHUNK + EDGE, CHUNK)
            weights[SETS:, cols] = hash_weight(qkv[HEAD : 2 * HEAD, cols], codes[1, :, cols], planes[...])
            items[:, cols] = by_item(qkv[2 * HEAD :, cols], jnp.ones((1, CHUNK), F32), masks[:, inner])
            return 0

        lax.fori_loop(0, CHUNKS, prepare, 0)
        sum_table.fill(items, codes.at[1], weights.at[pl.ds(SETS, SETS)], hot)

        def query_side(i, _):
            cols = span(i * CHUNK, CHUNK)
            inner = span(i * CHUNK + EDGE, CHUNK)
            weights[:SETS, cols] = hash_weight(qkv[:HEAD, cols], codes[0, :, cols], planes[...])
            v_ext[:, inner] = by_item(qkv[2 * HEAD :, cols] + v_bias, jnp.zeros((1, CHUNK), F32), masks[:, inner])
            return 0

        lax.fori_loop(0, CHUNKS, query_side, 0)
        sum_table.add()
        v_halo.finish()
        none = jnp.zeros((1, EDGE), F32)
        v_ext[:, :EDGE] = by_item(v_came[0].astype(F32) + v_bias, none, masks[:, :EDGE])
        v_ext[:, EDGE + BLOCK :] = by_item(v_came[1].astype(F32) + v_bias, none, masks[:, EDGE + BLOCK :])
        lower, upper = circulant(tap_row(conv_w, head, True))

        def convolve(i, _):
            at = i * 256
            mixed = nn(v_ext[:, span(at, 256)], lower) + nn(v_ext[:, span(at + 256, 256)], upper)
            conv[:, span(at, 256)] = pick_item(mixed, masks[:, span(at + EDGE, 256)])[:HEAD] + v_bias
            return 0

        lax.fori_loop(0, BLOCK // 256, convolve, 0)
        sum_table.finish()

        def read(i, _):
            i = (i + me) % CHUNKS
            cols = span(i * CHUNK, CHUNK)
            own = masks[:, span(i * CHUNK + EDGE, CHUNK)]
            for s in range(SETS):
                big_hot[s * SLOTS : (s + 1) * SLOTS, :] = one_hot(codes[0, s : s + 1, cols], weights[s : s + 1, cols])
            found = pick_item(nn(table[...], big_hot[...]), own)
            recip = 1.0 / (found[HEAD : HEAD + 1] + 1.0)
            est = (found[:HEAD] - v_bias) * recip
            estimate[:, cols] = est
            scale[:, cols] = recip
            rows = jnp.transpose(est + conv[:, cols])
            for u in range(PER_CHUNK):
                p = i * PER_CHUNK + u
                att_out[p] = pack(rows[u * OWN : (u + 1) * OWN])
                att_rows.start(p)
            return 0

        lax.fori_loop(0, CHUNKS, read, 0)

    def feed_forward(w_out_v, w_in_v, w_back_v, slope_v):
        loads = [
            pltpu.make_async_copy(a, b, local.at[5 + k])
            for k, (a, b) in enumerate([(w_out, w_out_v), (w_in, w_in_v), (w_back, w_back_v)])
        ]
        for load in loads:
            load.start()
        att_rows.finish()
        gain1, gain2 = ln1_gain[...][None, :], ln2_gain[...][None, :]
        attended = unpack_heads(lambda h: att[h])
        flip_in(attended, att_t, 0)
        acts[2].start()
        loads[0].wait()
        branch = nn(attended, w_out_v[...]) + b_out[...][None, :]
        hat1, recip1 = norm_forward(tokens[span(mine * OWN, OWN, 16), :].astype(F32) + branch)
        hidden = hat1 * gain1 + ln1_bias[...][None, :]
        hidden_low = hidden.astype(BF)
        flip_in(hidden, hidden_t, 0)
        acts[0].start()
        loads[1].wait()
        outer = b_back[...][None, :]
        for k in range(FF // D):
            cols = slice(k * D, (k + 1) * D)
            inner = nn(hidden_low, w_in_v[:, cols]) + b_in[pl.ds(k * D, D)][None, :]
            phi = 0.5 * (1.0 + lax.erf(inner * (2.0**-0.5)))
            slope_v[:, cols] = phi + inner * (jnp.exp(-0.5 * inner * inner) * 0.3989422804014327)
            act = (inner * phi).astype(BF)
            flip_in(act, act_t, k * D)
            if k == 0:
                loads[2].wait()
            outer = outer + nn(act, w_back_v[cols, :])
        acts[1].start()
        hat2, recip2 = norm_forward(hidden + outer)
        output[...] = hat2 * gain2 + ln2_bias[...][None, :]
        cot_load.wait()
        got = cot[...]
        sum_grad = norm_backward(got, hat2, recip2, gain2)
        outer_grad = sum_grad.astype(BF)
        outer_g[...] = outer_grad
        acts[4].start()
        hidden_grad = sum_grad
        sums = [column_sums(outer_grad.astype(F32)), column_sums(got * hat2), column_sums(got)]
        bias_rows = []
        for k in range(FF // D):
            cols = slice(k * D, (k + 1) * D)
            act_grad = nt(outer_grad, w_back_v[cols, :])
            inner_grad = (act_grad * slope_v[:, cols]).astype(BF)
            inner_g[:, cols] = inner_grad
            bias_rows.append(column_sums(inner_grad.astype(F32)))
            hidden_grad = hidden_grad + nt(inner_grad, w_in_v[:, cols])
        acts[3].start()
        grad1 = norm_backward(hidden_grad, hat1, recip1, gain1)
        resid[...] = grad1
        branch_grad = grad1.astype(BF)
        branch_g[...] = branch_grad
        att_grad = nt(branch_grad, w_out_v[...])
        for h in range(HEADS):
            grad_out[h] = pack(att_grad[:, h * HEAD : (h + 1) * HEAD])
        give_grad.start()
        acts[5].start()
        rows = [column_sums(branch_grad.astype(F32)), column_sums(hidden_grad * hat1), column_sums(hidden_grad)]
        vector.value = jnp.concatenate(rows + sums + bias_rows + [jnp.zeros((6, D), F32)], axis=0)
        vector.start(0)

    def backward(w_all, grad, den, items, hot, ext, rows_ref, g_all, mix, *accs):
        per = len(big_refs) // 2
        mats = [
            Matrix(*MATRICES[t], refs=(result, accs[t], *big_refs[t * per : (t + 1) * per]))
            for t, result in enumerate((sum_a, sum_b))
        ]
        into = BigSum(spot, slots, local.at[pl.ds(10, 3)], mats[:1])
        outof = BigSum(spot, slots, local.at[pl.ds(13, 3)], mats[1:])
        loads = [
            pltpu.make_async_copy(w, w_all.at[k], local.at[16 + k]) for k, w in enumerate((w_query, w_key, w_value))
        ]
        for load in loads:
            load.start()
        every_part = range(PARTS)

        def weight_into(a):
            m = mats[0]
            rows = span(core * m.half, m.half, 16)
            start, stop = a * m.part, min((a + 1) * m.part, FF)
            total = nn(hidden_t[rows, :], inner_g[:, start:stop]) + nn(hidden_s[...], inner_s[:, start:stop])
            m.acc[:, start:stop] = total.astype(BF)
            if stop == FF:
                total = nn(att_t[rows, :], branch_g[...]) + nn(att_s[...], branch_s[...])
                m.acc[:, FF:] = total.astype(BF)

        def weight_outof(a):
            m = mats[1]
            lanes = slice(a * m.part, (a + 1) * m.part)
            rows = span(core * m.half, m.half, 16)
            total = nn(act_t[rows, :], outer_g[:, lanes]) + nn(act_s[...], outer_s[:, lanes])
            m.acc[:, lanes] = total.astype(BF)

        def step(sums, name):
            for a in every_part:
                getattr(sums, name)(a)

        for copy in acts:
            copy.wait()
        for a in every_part:
            weight_outof(a)
            outof.begin(a)
        for a in every_part:
            weight_into(a)
            into.begin(a)

        give_grad.finish()
        for p in range(MEMBERS):
            both = chunks_in[p].astype(F32)
            rows_ref[p * OWN : p * OWN + SIDE] = both[:, :HEAD]
            rows_ref[p * OWN + SIDE : (p + 1) * OWN] = both[:, HEAD:]

        def prepare(i, _):
            cols = span(i * CHUNK, CHUNK)
            own = masks[:, span(i * CHUNK + EDGE, CHUNK)]
            this = jnp.transpose(rows_ref[span(i * CHUNK, CHUNK), :])
            grad[:, cols] = this
            numer = this * scale[:, cols]
            mass = -jnp.sum(numer * estimate[:, cols], axis=0, keepdims=True)
            den[:, cols] = mass
            items[:, cols] = by_item(numer, mass, own)
            ext[:, span(i * CHUNK + EDGE, CHUNK)] = by_item(this, jnp.zeros((1, CHUNK), F32), own)
            return 0

        lax.fori_loop(0, CHUNKS, prepare, 0)
        g_edges[0] = grad[:, :EDGE].astype(BF)
        g_edges[1] = grad[:, BLOCK - EDGE :].astype(BF)
        g_halo.start()
        sum_grads.fill(items, codes.at[0], weights.at[pl.ds(0, SETS)], hot)
        step(outof, "near")
        step(into, "near")

        def query_back(i, _):
            cols = span(i * CHUNK, CHUNK)
            own = masks[:, span(i * CHUNK + EDGE, CHUNK)]
            q_codes = codes[0, :, cols]
            numer = grad[:, cols] * scale[:, cols]
            mass = den[:, cols]
            found_all = []
            for s in range(SETS):
                one = one_hot(q_codes[s : s + 1], 1.0)
                found = pick_item(nn(table[:, s * SLOTS : (s + 1) * SLOTS], one), own)
                found_all.append(
                    jnp.sum(found[:HEAD] * numer, axis=0, keepdims=True) + found[HEAD : HEAD + 1] * mass
                )
            z_grad = jnp.concatenate(found_all, axis=0) * weights[:SETS, cols]
            g_all[:HEAD, cols] = hash_back(z_grad, qkv[:HEAD, cols], q_codes, planes[...]).astype(BF)
            return 0

        lax.fori_loop(0, 2, query_back, 0)
        sum_grads.add()
        step(outof, "relay")
        step(into, "relay")
        vector.finish(0)
        vector.start(1)
        lax.fori_loop(2, CHUNKS, query_back, 0)

        g_halo.finish()
        none = jnp.zeros((1, EDGE), F32)
        ext[:, :EDGE] = by_item(g_came[0].astype(F32), none, masks[:, :EDGE])
        ext[:, EDGE + BLOCK :] = by_item(g_came[1].astype(F32), none, masks[:, EDGE + BLOCK :])
        lower, upper = circulant(tap_row(conv_w, head, False))

        def conv_back(i, carry):
            at = i * 256
            mixed = nn(ext[:, span(at, 256)], lower) + nn(ext[:, span(at + 256, 256)], upper)
            mix[:, span(at, 256)] = pick_item(mixed, masks[:, span(at + EDGE, 256)])[:HEAD]
            this = ext[:, span(at + EDGE, 256)]
            return carry[0] + tn(v_ext[:, span(at, 256)], this), carry[1] + tn(v_ext[:, span(at + 256, 256)], this)

        zeros = jnp.zeros((256, 256), F32)
        c_low, c_high = lax.fori_loop(0, BLOCK // 256, conv_back, (zeros, zeros))
        row, col = iota((256, 256), 0), iota((256, 256), 1)
        skew = jnp.where(col < row, c_low, c_high)
        for b in range(8):
            skew = jnp.where(jnp.bitwise_and(row, 1 << b) != 0, pltpu.roll(skew, 256 - (1 << b), 1), skew)
        taps_grad = jnp.sum(skew, axis=0, keepdims=True)
        step(outof, "second")
        step(into, "second")
        vector.finish(1)
        vector.start(2)
        sum_grads.finish()

        def key_back(i, _):
            i = (i + me) % CHUNKS
            cols = span(i * CHUNK, CHUNK)
            own = masks[:, span(i * CHUNK + EDGE, CHUNK)]
            k_codes = codes[1, :, cols]
            k_w = weights[SETS:, cols]
            val = qkv[2 * HEAD :, cols]
            found_all = []
            v_grad = mix[:, cols]
            for s in range(SETS):
                one = one_hot(k_codes[s : s + 1], 1.0)
                found = pick_item(nn(gtable[:, s * SLOTS : (s + 1) * SLOTS], one), own)
                found_all.append(
                    jnp.sum(found[:HEAD] * val, axis=0, keepdims=True) + found[HEAD : HEAD + 1]
                )
                v_grad = v_grad + found[:HEAD] * k_w[s : s + 1]
            z_grad = jnp.concatenate(found_all, axis=0) * k_w
            k_grad = hash_back(z_grad, qkv[HEAD : 2 * HEAD, cols], k_codes, planes[...])
            g_all[HEAD : 2 * HEAD, cols] = k_grad.astype(BF)
            g_all[2 * HEAD : 3 * HEAD, cols] = v_grad.astype(BF)
            for k in range(3):
                rows = jnp.transpose(g_all[k * HEAD : (k + 1) * HEAD, cols].astype(F32))
                for u in range(PER_CHUNK):
                    g_chunks[i * PER_CHUNK + u, k] = pack(rows[u * OWN : (u + 1) * OWN])
            for u in range(PER_CHUNK):
                grad_rows.start(i * PER_CHUNK + u)
            return 0

        lax.fori_loop(0, 1, key_back, 0)
        lax.fori_loop(1, 3, key_back, 0)
        step(outof, "third")
        step(into, "third")
        vector.finish(2)
        vector.start(3)
        lax.fori_loop(3, CHUNKS, key_back, 0)

        g_all[3 * HEAD :, :] = jnp.zeros((HEAD, BLOCK), BF)
        own_part = g_all[: 3 * HEAD, span(core * ROWS, ROWS)]
        away = g_all[: 3 * HEAD, span((1 - core) * ROWS, ROWS)]
        w_grad = jnp.transpose(nn(own_part, tokens[...]) + nn(away, other_tok[...]))
        head_w[:D] = w_grad[:, : 2 * HEAD].astype(BF)
        head_w[D:] = jnp.concatenate([w_grad[: D // 2, 2 * HEAD :], w_grad[D // 2 :, 2 * HEAD :]], axis=1).astype(BF)
        heads.start_sum()
        biases = nt(jnp.ones((8, BLOCK), BF), g_all[...])[0:1]
        own_row = (iota((16, SMALL), 0) == head) & owner
        small.value = jnp.where(own_row, jnp.concatenate([biases, taps_grad], axis=1), 0.0)
        small.start(0)
        vector.finish(3)
        vec_out[...] = vector.value
        step(outof, "back")
        step(into, "back")
        small.finish(0)
        small.start(1)
        heads.finish_sum()
        for p in every_part:
            heads.start(p, 0)
        step(outof, "ring")
        step(into, "ring")
        grad_rows.finish()
        total = resid[...]
        for k in range(3):
            loads[k].wait()
            total = total + nt(unpack_heads(lambda h, k=k: g_in[h, k]), w_all[k])
        grad_tokens[...] = total
        for p in every_part:
            heads.finish(p, 0)
            heads.start(p, 1)
        small.finish(1)
        small.start(2)
        step(outof, "pass_on")
        for p in every_part:
            heads.finish(p, 1)
            heads.start(p, 2)
        step(into, "pass_on")
        small.finish(2)
        small.start(3)
        step(outof, "core")
        for p in every_part:
            heads.finish(p, 2)
            heads.start(p, 3)
        step(into, "core")
        small.finish(3)
        small_out[...] = small.value
        for p in every_part:
            heads.finish(p, 3)
        step(outof, "finish")
        step(into, "finish")

    pl.run_scoped(
        front, vmem(3, D, D), vmem(3 * HEAD, D), vmem(STACK, BLOCK), vmem(2, SLOTS, BLOCK), vmem(TABLE, CHUNK),
        vmem(HEAD, BLOCK, kind=F32), vmem(HEADS, 2, ROWS, kind=I32),
    )
    pl.run_scoped(feed_forward, vmem(D, D), vmem(D, FF), vmem(FF, D), vmem(OWN, FF, kind=F32))
    pl.run_scoped(
        backward, vmem(3, D, D), vmem(HEAD, BLOCK, kind=F32), vmem(1, BLOCK, kind=F32), vmem(STACK, BLOCK),
        vmem(2, SLOTS, BLOCK), vmem(STACK, EXT), vmem(BLOCK, HEAD, kind=F32), vmem(4 * HEAD, BLOCK),
        vmem(HEAD, BLOCK, kind=F32), *[Matrix(*m).whole() for m in MATRICES],
    )


PIECES = 8


def last_kernel(
    sum_a, sum_b, even, odd, vec, small, layer_out, tok_grad,
    output, grad_tokens, g_wq, g_bq, g_wk, g_bk, g_wv, g_bv, g_conv, g_wo, g_bo, g_l1g, g_l1b, g_wi, g_bi, g_wb, g_bb, g_l2g,
    g_l2b,
    a_in, b_in, a_out, b_out, qkv_out, in_sems, out_sems,
):
    a_rows, b_rows = D // PIECES, FF // PIECES
    loads = []
    for k in range(PIECES):
        rows = pl.ds(k * a_rows, a_rows)
        loads.append(pltpu.make_async_copy(sum_a.at[rows], a_in.at[rows], in_sems.at[2 * k]))
        rows = pl.ds(k * b_rows, b_rows)
        loads.append(pltpu.make_async_copy(sum_b.at[rows], b_in.at[rows], in_sems.at[2 * k + 1]))
    for load in loads:
        load.start()
    writes = []

    def write(source, dest):
        copy = pltpu.make_async_copy(source, dest, out_sems.at[len(writes)])
        copy.start()
        writes.append(copy)

    left = iota((SHARE, 128), 1) < HEAD

    def pieces(pair, j):
        zh, x = j // 4, j % 4
        if pair < 4:
            return even[zh, 0, x, pair].astype(F32), even[zh, 1, x, pair].astype(F32)
        return odd[zh, x, 0, pair - 4].astype(F32), odd[zh, x, 1, pair - 4].astype(F32)

    for pair in range(HEADS // 2):
        lanes = pl.ds(pair * 128, 128)
        for j in range(BLOCKS):
            a, b = pieces(pair, j)
            first = jnp.where(left, a, pltpu.roll(b, HEAD, 1))
            second = jnp.where(left, pltpu.roll(a, HEAD, 1), b)
            low, high = j * SHARE, (j + 1) * SHARE
            cut = min(max(D - low, 0), SHARE)
            if cut > 0:
                qkv_out[0, low : low + cut, lanes] = first[:cut]
                qkv_out[1, low : low + cut, lanes] = second[:cut]
            if cut < SHARE:
                start, stop = low + cut - D, high - D
                qkv_out[2, start:stop, lanes] = first[cut:]
                qkv_out[2, D // 2 + start : D // 2 + stop, lanes] = second[cut:]
    for k, dest in enumerate((g_wq, g_wk, g_wv)):
        write(qkv_out.at[k], dest)
    for k in range(PIECES):
        rows = pl.ds(k * a_rows, a_rows)
        loads[2 * k].wait()
        a_out[rows, :] = a_in[rows, :].astype(F32)
        write(a_out.at[rows, pl.ds(0, FF)], g_wi.at[rows])
        write(a_out.at[rows, pl.ds(FF, D)], g_wo.at[rows])
        rows = pl.ds(k * b_rows, b_rows)
        loads[2 * k + 1].wait()
        b_out[rows, :] = b_in[rows, :].astype(F32)
        write(b_out.at[rows], g_wb.at[rows])
    output[...] = layer_out[...]
    grad_tokens[...] = tok_grad[...]
    for k, dest in enumerate((g_bo, g_l1g, g_l1b, g_bb, g_l2g, g_l2b)):
        dest[...] = vec[k, :]
    for k in range(FF // D):
        g_bi[pl.ds(k * D, D)] = vec[6 + k, :]
    for k, dest in enumerate((g_bq, g_bk, g_bv)):
        for pair in range(HEADS // 2):
            lanes = slice(k * HEAD, (k + 1) * HEAD)
            dest[pl.ds(pair * 128, 128)] = jnp.concatenate(
                [small[2 * pair : 2 * pair + 1, lanes], small[2 * pair + 1 : 2 * pair + 2, lanes]], axis=1
            )[0]
    row, col = iota((256, 128), 0), iota((256, 128), 1)
    flip = jnp.where(row == 160 - col, 1.0, 0.0)
    g_conv[...] = nn(small[:, 256:], flip, precision=HIGHEST)[:HEADS, :65]
    for copy in writes:
        copy.wait()


VMEM_SPEC = pl.BlockSpec(memory_space=pltpu.VMEM)
ANY_SPEC = pl.BlockSpec(memory_space=pl.ANY)
SMEM_SPEC = pl.BlockSpec(memory_space=pltpu.SMEM)


def call(kernel, outs, scratch, *args, ident=None, far=(), far_outs=(), scalars=()):
    params = {} if ident is None else {"collective_id": ident, "has_side_effects": True}
    specs = [ANY_SPEC if k in far else SMEM_SPEC if k in scalars else VMEM_SPEC for k in range(len(args))]
    return pl.pallas_call(
        kernel,
        out_shape=[jax.ShapeDtypeStruct(shape, kind) for shape, kind in outs],
        in_specs=specs,
        out_specs=[ANY_SPEC if k in far_outs else VMEM_SPEC for k in range(len(outs))],
        scratch_shapes=scratch,
        compiler_params=pltpu.CompilerParams(vmem_limit_bytes=VMEM_LIMIT, **params),
    )(*args)


def per_device(
    tokens, item_cuts, q_codes, k_codes, hyperplanes, w_query, b_query, w_key, b_key,
    w_value, b_value, conv_weight, w_out, b_out, ln1_gain, ln1_bias, w_in, b_in, w_back,
    b_back, ln2_gain, ln2_bias, cotangent,
):
    chunk = (SIDE, 128)
    layer_out, tok_grad, sum_a, sum_b, vec_sum, small_sum, even, odd = call(
        layer_kernel,
        [
            ((OWN, D), F32), ((OWN, D), F32), ((D, WIDE), BF), ((FF, D), BF), ((16, D), F32), ((16, SMALL), F32),
            ((2, 2, 4, 4, SHARE, 128), BF), ((2, 4, 2, 2, SHARE, 128), BF),
        ],
        [
            vmem(ROWS, D), vmem(OWN, D, kind=F32), vmem(ROWS, D), vmem(3 * HEAD, BLOCK, kind=F32), vmem(2 * SETS, BLOCK, kind=F32),
            vmem(2, SETS, BLOCK, kind=I32), vmem(BITS * SETS, HEAD, kind=F32), vmem(8, EXT, kind=F32),
            vmem(STACK, TABLE), vmem(HEAD, BLOCK, kind=F32), vmem(1, BLOCK, kind=F32), vmem(STACK, EXT),
            vmem(MEMBERS, 2, ROWS, kind=I32), vmem(SETS, BITS, HEAD, kind=F32), vmem(BLOCKS - 1, ITEM, SLOTS),
            vmem(BLOCKS - 1, ITEM, SLOTS), vmem(2, HEAD, EDGE), vmem(2, HEAD, EDGE), vmem(MEMBERS, *chunk),
            vmem(HEADS, *chunk),
            vmem(HEADS, *chunk), vmem(MEMBERS, *chunk), vmem(2, HEAD, EDGE), vmem(2, HEAD, EDGE),
            vmem(BLOCKS - 1, ITEM, SLOTS), vmem(BLOCKS - 1, ITEM, SLOTS), vmem(STACK, TABLE),
            vmem(MEMBERS, 3, *chunk), vmem(HEADS, 3, *chunk), vmem(HEAD_ROWS, 128), vmem(BLOCKS - 1, SHARE, 128),
            vmem(4, 4, 16, D, kind=F32), vmem(4, 4, 16, SMALL, kind=F32),
            vmem(OWN, D, kind=F32), vmem(D, OWN), vmem(D, OWN), vmem(FF, OWN), vmem(OWN, FF), vmem(OWN, D),
            vmem(OWN, D), vmem(D // 2, OWN), vmem(D // 2, OWN), vmem(FF // 2, OWN), vmem(OWN, FF), vmem(OWN, D),
            vmem(OWN, D), dma(21), dma(LAYER_SEMS), dma(LAYER_SEMS),
        ]
        + Matrix(*MATRICES[0]).scratch()
        + Matrix(*MATRICES[1]).scratch(),
        q_codes.transpose(1, 0, 2), k_codes.transpose(1, 0, 2), hyperplanes.transpose(0, 2, 1), item_cuts, b_query,
        b_key, b_value, conv_weight, b_out, ln1_gain, ln1_bias, b_in, b_back, ln2_gain, ln2_bias, tokens, cotangent,
        w_query, w_key, w_value, w_out, w_in, w_back,
        ident=0, far=(15, 16, 17, 18, 19, 20, 21, 22), far_outs=(2, 3), scalars=(3,),
    )
    square, line = ((D, D), F32), ((D,), F32)
    return call(
        last_kernel,
        [
            ((OWN, D), F32), ((OWN, D), F32), square, line, square, line, square, line, ((HEADS, 65), F32), square, line, line, line,
            ((D, FF), F32), ((FF,), F32), ((FF, D), F32), line, line, line,
        ],
        [
            vmem(D, WIDE), vmem(FF, D), vmem(D, WIDE, kind=F32), vmem(FF, D, kind=F32), vmem(3, D, D, kind=F32),
            dma(2 * PIECES), dma(3 + 3 * PIECES),
        ],
        sum_a, sum_b, even, odd, vec_sum, small_sum, layer_out, tok_grad,
        far=(0, 1), far_outs=(2, 4, 6, 9, 13, 15),
    )


def solution(mesh):
    grid = Mesh(mesh.devices.reshape(2, 4, 2, 4, 2), ALL_AXES)
    rows = ("zh", "x", "c")
    sets = ("y", "zl")
    placed = (
        P(rows, None), P(), P(sets, None, rows), P(sets, None, rows), P(sets, None, None),
    ) + (P(),) * 17 + (P(ALL_AXES, None),)
    return jax.shard_map(
        per_device,
        mesh=grid,
        in_specs=placed,
        out_specs=(P(ALL_AXES, None), P(ALL_AXES, None)) + (P(),) * 17,
        check_vma=False,
    )
```

```python
import jax
import jax.numpy as jnp
from jax import lax
from jax.experimental import pallas as pl
from jax.experimental.pallas import tpu as pltpu
from jax.sharding import Mesh, PartitionSpec as P

BF = jnp.bfloat16
F32 = jnp.float32
I32 = jnp.int32
HIGHEST = lax.Precision.HIGHEST
MESH = pl.DeviceIdType.MESH
EPS_NORM = 1e-05
EPS_UNIT = 1e-06

D = 768
HEADS = 12
HEAD = 64
SETS = 8
BITS = 8
SLOTS = 256
TABLE = SETS * SLOTS
FF = 3072
ROWS = 1280
BLOCK = 2560
BLOCKS = 8
OWN = 160
SIDE = OWN // 2
MEMBERS = 16
EDGE = 128
EXT = BLOCK + 2 * EDGE
TOTAL = 20480
CHUNK = 640
CHUNKS = BLOCK // CHUNK
PER_CHUNK = CHUNK // OWN
ITEM = 80
CLASSES = 3
STACK = ITEM * CLASSES
SHARE = 144
HEAD_ROWS = D + D // 2
SMALL = 512
WIDE = FF + D
VMEM_LIMIT = 61 * 1024 * 1024

BLOCK_AXES = ("zh", "x")
ALL_AXES = ("zh", "x", "c", "y", "zl")


def nt(left, right, **kw):
    return lax.dot_general(left, right, (((1,), (1,)), ((), ())), preferred_element_type=F32, **kw)


def nn(left, right, **kw):
    return lax.dot_general(left, right, (((1,), (0,)), ((), ())), preferred_element_type=F32, **kw)


def tn(left, right, **kw):
    return lax.dot_general(left, right, (((0,), (0,)), ((), ())), preferred_element_type=F32, **kw)


def unit_of(proj):
    scale = lax.rsqrt(jnp.sum(proj * proj, axis=0, keepdims=True) + EPS_UNIT)
    return proj * scale, scale


def bits_of(codes):
    return [(jnp.bitwise_and(codes, 1 << b) != 0) for b in range(BITS)]


def hash_weight(proj, codes, planes):
    unit, _ = unit_of(proj)
    lifted = nn(planes, unit, precision=HIGHEST)
    total = None
    for b, bit in enumerate(bits_of(codes)):
        part = lifted[b * SETS : (b + 1) * SETS]
        part = jnp.where(bit, part, -part)
        total = part if total is None else total + part
    return jnp.exp(total)


def hash_back(z_grad, proj, codes, planes):
    unit, scale = unit_of(proj)
    lifted_grad = jnp.concatenate([jnp.where(bit, z_grad, -z_grad) for bit in bits_of(codes)], axis=0)
    unit_grad = tn(planes, lifted_grad, precision=HIGHEST)
    return scale * (unit_grad - unit * jnp.sum(unit * unit_grad, axis=0, keepdims=True))


def one_hot(codes_row, weight_row):
    width = codes_row.shape[1]
    slots = lax.broadcasted_iota(jnp.int32, (SLOTS, width), 0)
    return jnp.where(slots == codes_row, weight_row, 0.0).astype(BF)


def by_item(sums, mass, masks):
    width = sums.shape[1]
    lead = lax.broadcasted_iota(jnp.int32, (ITEM - HEAD, width), 0) == 0
    tail = jnp.where(lead, mass, 0.0)
    whole = jnp.concatenate([sums, tail], axis=0)
    return jnp.concatenate([whole * masks[w : w + 1] for w in range(CLASSES)], axis=0).astype(BF)


def pick_item(stacked, masks):
    total = None
    for w in range(CLASSES):
        part = stacked[w * ITEM : (w + 1) * ITEM] * masks[w : w + 1]
        total = part if total is None else total + part
    return total


def circulant(base):
    grid = jnp.broadcast_to(base, (256, 256))
    grid = pltpu.roll(grid, 0, 1, stride=1, stride_axis=0)
    row = lax.broadcasted_iota(jnp.int32, (256, 256), 0)
    col = lax.broadcasted_iota(jnp.int32, (256, 256), 1)
    return (
        jnp.where(col < row, grid, 0.0).astype(BF),
        jnp.where(col >= row, grid, 0.0).astype(BF),
    )


def member_id(member):
    return {"c": member // 8, "y": (member % 8) // 2, "zl": member % 2}


def block_id(block):
    return {"zh": block // 4, "x": block % 4}


def owns(member):
    return (member < 8) | (member % 2 == ((member % 8) // 2) % 2)


def head_at(member):
    return jnp.where(member < 8, member, 8 + (member % 8) // 2)


def owner_of(head):
    return head if head < 8 else 8 + (head - 8) * 2 + (head - 8) % 2


def my_member():
    return lax.axis_index("c") * 8 + lax.axis_index("y") * 2 + lax.axis_index("zl")


def my_block():
    return lax.axis_index("zh") * 4 + lax.axis_index("x")


def send(src, dst, send_sem, recv_sem, device):
    return pltpu.make_async_remote_copy(
        src_ref=src, dst_ref=dst, send_sem=send_sem, recv_sem=recv_sem,
        device_id=device, device_id_type=MESH,
    )


def on_axis(axis, k):
    return {"zh": k // 2, "zl": k % 2} if axis == "z" else {axis: k}


def here():
    spot = {a: lax.axis_index(a) for a in ALL_AXES}
    spot["z"] = spot["zh"] * 2 + spot["zl"]
    return spot


class Slots:
    def __init__(self, send_sem, recv_sem):
        self.send_sem, self.recv_sem, self.used = send_sem, recv_sem, 0

    def take(self):
        k = self.used
        self.used += 1
        return self.send_sem.at[k], self.recv_sem.at[k]


AXES = ("c", "x", "y", "z", "c")
ORDERS = (("x", "y", "z"), ("y", "z", "x"), ("z", "x", "y"))
PARTS = 3
VEC_SLOTS = 1 + 3 * 3 + 1


class VectorSum:
    def __init__(self, spot, slots, value, buffer):
        self.spot, self.value, self.buffer, self.copies = spot, value, buffer, {}
        for stage, axis in enumerate(AXES):
            size = 2 if axis == "c" else 4
            self.copies[stage] = []
            for d in range(1, size):
                k = spot[axis]
                dest = buffer.at[stage, k]
                source = buffer.at[0, 2] if stage == 0 else dest
                self.copies[stage].append(send(source, dest, *slots.take(), on_axis(axis, (k + d) % size)))

    def start(self, stage):
        c = self.spot["c"]
        if stage == 0:
            upper, lower = self.value[:8], self.value[8:]
            self.buffer[0, 2] = jnp.where(c == 0, lower, upper)
            self.value = jnp.where(c == 0, upper, lower)
        self.buffer[stage, self.spot[AXES[stage]]] = self.value
        for copy in self.copies[stage]:
            copy.start()

    def finish(self, stage):
        for copy in self.copies[stage]:
            copy.wait()
        if stage == 4:
            self.value = jnp.concatenate([self.buffer[4, 0], self.buffer[4, 1]], axis=0)
            return
        total = self.buffer[stage, 0] + self.buffer[stage, 1]
        if stage > 0:
            total = total + (self.buffer[stage, 2] + self.buffer[stage, 3])
        self.value = total


def dma(count):
    return pltpu.SemaphoreType.DMA((count,))


def vmem(*shape, kind=BF):
    return pltpu.VMEM(shape, kind)


def hello(ids):
    barrier = pltpu.get_barrier_semaphore()
    for one in ids:
        pl.semaphore_signal(barrier, inc=1, device_id=one, device_id_type=MESH)


def all_here(count):
    pl.semaphore_wait(pltpu.get_barrier_semaphore(), count)


def every(count, step, body):
    def one(i, _):
        body(pl.multiple_of(i * step, 16))
        return 0

    lax.fori_loop(0, count // step, one, 0)


def span(start, size, unit=128):
    return pl.ds(pl.multiple_of(start, unit), size)


class Matrix:
    def __init__(self, shape, row_cut, refs=None):
        self.rows, self.cols = shape
        self.half = self.rows // 2
        self.part = self.cols // PARTS
        self.quarter = self.half // 4
        self.eighth = self.quarter // 2
        self.row_cut = row_cut
        self.col_cut = 4 // row_cut
        self.small = (self.quarter // row_cut, self.part // self.col_cut)
        self.step = 16 if self.part > 512 else 96
        if refs is not None:
            (
                self.result, self.acc, self.relay, self.mixed, self.first, self.first_sum, self.second, self.third,
                self.own,
            ) = refs

    def whole(self):
        return pltpu.VMEM((self.half, self.cols), BF)

    def scratch(self):
        quarter, eighth = (self.quarter, self.part), (self.eighth, self.part)
        shapes = [
            (PARTS, 2, *eighth), (PARTS, 2, *eighth), (PARTS, 2, *quarter), (PARTS, *quarter),
            (PARTS, 3, *self.small), (PARTS, 4, *self.small), (PARTS, *self.small),
        ]
        return [pltpu.VMEM(shape, BF) for shape in shapes]

    def lanes(self, a):
        return pl.ds(a * self.part, self.part)

    def spot16(self, j):
        return (j // self.col_cut) * self.small[0], (j % self.col_cut) * self.small[1]

    def part_of(self, q, a, side=None, base=0):
        start = base + q * self.quarter
        if side is None:
            return span(start, self.quarter, 16), self.lanes(a)
        return span(start + side * self.eighth, self.eighth, 16), self.lanes(a)


MATRICES = (((D, WIDE), 2), ((FF, D), 4))
BIG_SLOTS = 2 * PARTS * (6 + 3 * 3 + 4 + 4)


class BigSum:
    def __init__(self, spot, slots, local, mats):
        self.spot, self.mats, self.local = spot, mats, local
        c = spot["c"]
        sibling = on_axis("c", 1 - c)
        self.copies = {}
        self.keeps = {}
        for t, m in enumerate(mats):
            base = c * m.half
            for a in range(PARTS):
                one, two, three = ORDERS[a]
                i, j, k = spot[one], spot[two], spot[three]
                up, down, across = (i + 1) % 4, (i + 3) % 4, (i + 2) % 4
                to_up, to_down = on_axis(one, up), on_axis(one, down)

                def put(name, src, dst, device):
                    self.copies.setdefault((name, a), []).append(send(src, dst, *slots.take(), device))

                put("far", m.acc.at[m.part_of(across, a, 0)], m.relay.at[a, 0], to_up)
                put("far", m.acc.at[m.part_of(across, a, 1)], m.relay.at[a, 1], to_down)
                upper, lower = pl.ds(0, m.eighth), pl.ds(m.eighth, m.eighth)
                put("near", m.acc.at[m.part_of(up, a, 1)], m.first.at[a, 0, lower], to_up)
                put("near", m.acc.at[m.part_of(down, a, 0)], m.first.at[a, 1, upper], to_down)
                put("mixed", m.mixed.at[a, 0], m.first.at[a, 0, upper], to_up)
                put("mixed", m.mixed.at[a, 1], m.first.at[a, 1, lower], to_down)
                row, lane = m.spot16(j)
                at = (
                    span(base + i * m.quarter + row, m.small[0], 16),
                    span(a * m.part + lane, m.small[1]),
                )
                self.keeps[t, a] = pltpu.make_async_copy(m.own.at[a], m.result.at[at], local.at[t * PARTS + a])
                for d in range(1, 4):
                    to = (j + d) % 4
                    row, lane = m.spot16(to)
                    piece = m.first_sum.at[a, span(row, m.small[0], 16), span(lane, m.small[1])]
                    put("second", piece, m.second.at[a, d - 1], on_axis(two, to))
                    piece = m.third.at[a, k]
                    put("third", piece, piece, on_axis(three, (k + d) % 4))
                    put("back", m.own.at[a], m.result.at[at], on_axis(two, (j + d) % 4))
                mine = m.result.at[m.part_of(i, a, None, base)]
                put("ring", mine, mine, to_up)
                put("ring", mine, mine, to_down)
                piece = m.result.at[m.part_of(down, a, 0, base)]
                put("pass", piece, piece, to_up)
                piece = m.result.at[m.part_of(up, a, 1, base)]
                put("pass", piece, piece, to_down)
                for q in (i, up, down, across):
                    piece = m.result.at[m.part_of(q, a, None, base)]
                    put("core", piece, piece, sibling)

    def start(self, name, a):
        for copy in self.copies[name, a]:
            copy.start()

    def wait(self, name, a):
        for copy in self.copies[name, a]:
            copy.wait()

    def start_core(self, a, which):
        for t in range(len(self.mats)):
            for q in which:
                self.copies["core", a][4 * t + q].start()

    def begin(self, a):
        self.start("far", a)

    def near(self, a):
        self.start("near", a)

    def relay(self, a):
        self.wait("far", a)
        i = self.spot[ORDERS[a][0]]
        for m in self.mats:
            for side, q in ((0, (i + 1) % 4), (1, (i + 3) % 4)):

                def add(r, m=m, side=side, q=q):
                    rows = pl.ds(r, m.step)
                    start = q * m.quarter + side * m.eighth
                    mine = m.acc[span(start + r, m.step, 16), m.lanes(a)].astype(F32)
                    m.mixed[a, side, rows] = (mine + m.relay[a, side, rows].astype(F32)).astype(BF)

                every(m.eighth, m.step, add)
        self.start("mixed", a)

    def second(self, a):
        self.wait("near", a)
        self.wait("mixed", a)
        i = self.spot[ORDERS[a][0]]
        for m in self.mats:

            def add(r, m=m):
                rows = pl.ds(r, m.step)
                total = m.acc[span(i * m.quarter + r, m.step, 16), m.lanes(a)].astype(F32)
                total = total + m.first[a, 0, rows].astype(F32) + m.first[a, 1, rows].astype(F32)
                m.first_sum[a, rows] = total.astype(BF)

            every(m.quarter, m.step, add)
        self.start("second", a)

    def third(self, a):
        self.wait("second", a)
        _, two, three = ORDERS[a]
        j, k = self.spot[two], self.spot[three]
        for m in self.mats:
            row, lane = m.spot16(j)
            total = m.first_sum[a, span(row, m.small[0], 16), span(lane, m.small[1])].astype(F32)
            for d in range(3):
                total = total + m.second[a, d].astype(F32)
            m.third[a, k] = total.astype(BF)
        self.start("third", a)

    def back(self, a):
        self.wait("third", a)
        for t, m in enumerate(self.mats):
            low = m.third[a, 0].astype(F32) + m.third[a, 1].astype(F32)
            high = m.third[a, 2].astype(F32) + m.third[a, 3].astype(F32)
            m.own[a] = (low + high).astype(BF)
            self.keeps[t, a].start()
        self.start("back", a)

    def ring(self, a):
        self.wait("back", a)
        for t in range(len(self.mats)):
            self.keeps[t, a].wait()
        self.start("ring", a)
        self.start_core(a, (0,))

    def pass_on(self, a):
        self.wait("ring", a)
        self.start("pass", a)
        self.start_core(a, (1, 2))

    def core(self, a):
        self.wait("pass", a)
        self.start_core(a, (3,))

    def finish(self, a):
        self.wait("core", a)


class HeadSum:
    def __init__(self, spot, slots, source, got, even, odd):
        self.spot, self.source, self.got, self.even, self.odd = spot, source, got, even, odd
        c, x, y, zh, zl = (spot[a] for a in ("c", "x", "y", "zh", "zl"))
        self.block = zh * 4 + x
        self.is_even, self.is_odd = c == 0, c == 1
        self.active = (c == 0) | (zl == y % 2)
        self.pieces = []
        for d in range(1, BLOCKS):
            to = (self.block + d) % BLOCKS
            piece = source.at[pl.ds(pl.multiple_of(to * SHARE, 16), SHARE)]
            self.pieces.append(send(piece, got.at[d - 1], *slots.take(), block_id(to)))
        self.copies = {}
        whole = slice(None)
        for p in range(PARTS):
            rows = pl.ds(p * SHARE // PARTS, SHARE // PARTS)
            for stage in range(4):
                done = ORDERS[p][:stage]
                in_x = whole if "x" in done else x
                in_zh = whole if "z" in done else zh
                even_at = (in_zh, whole if "z" in done else zl, in_x, whole if "y" in done else y, rows)
                if "y" not in done:
                    in_y = (y % 2, y // 2)
                else:
                    in_y = (whole if "z" in done else zl, whole)
                odd_at = (in_zh, in_x, *in_y, rows)
                for side, piece in enumerate((even.at[even_at], odd.at[odd_at])):
                    if stage == 3:
                        self.copies[p, stage, side] = [send(piece, piece, *slots.take(), on_axis("c", 1 - c))]
                        continue
                    axis = ORDERS[p][stage]
                    self.copies[p, stage, side] = [
                        send(piece, piece, *slots.take(), on_axis(axis, (spot[axis] + d) % 4)) for d in range(1, 4)
                    ]

    def start_sum(self):
        for copy in self.pieces:
            pl.when(self.active)(copy.start)

    def finish_sum(self):
        spot = self.spot

        def body():
            for copy in self.pieces:
                copy.wait()
            total = self.source[pl.ds(pl.multiple_of(self.block * SHARE, 16), SHARE)].astype(F32)
            for d in range(BLOCKS - 1):
                total = total + self.got[d].astype(F32)
            total = total.astype(BF)

            def keep_even():
                self.even[spot["zh"], spot["zl"], spot["x"], spot["y"]] = total

            def keep_odd():
                self.odd[spot["zh"], spot["x"], spot["y"] % 2, spot["y"] // 2] = total

            pl.when(self.is_even)(keep_even)
            pl.when(self.is_odd)(keep_odd)

        pl.when(self.active)(body)

    def sends(self, p, stage):
        return self.is_odd if stage > 0 and ORDERS[p][:stage] != ("x",) else self.is_odd & self.active

    def start(self, p, stage):
        def go(side):
            for copy in self.copies[p, stage, side]:
                copy.start()

        pl.when(self.is_even)(lambda: go(0))
        pl.when(self.sends(p, stage) if stage < 3 else self.is_odd)(lambda: go(1))

    def finish(self, p, stage):
        if stage == 3:
            for side, mine in enumerate((self.is_even, self.is_odd)):
                copy = self.copies[p, stage, side][0]
                pl.when(mine)(copy.wait_send)
                pl.when(jnp.logical_not(mine))(copy.wait_recv)
            return

        def even():
            for copy in self.copies[p, stage, 0]:
                copy.wait()

        def odd_sent():
            for copy in self.copies[p, stage, 1]:
                copy.wait_send()

        pl.when(self.is_even)(even)
        pl.when(self.sends(p, stage))(odd_sent)
        axis = ORDERS[p][stage]
        early = stage == 0 or ORDERS[p][:stage] == ("x",)
        for d in range(1, 4):
            came = (self.spot[axis] + 4 - d) % 4
            sent = self.is_odd
            if early and axis == "x":
                sent = sent & self.active
            if early and axis == "y":
                sent = sent & (self.spot["zl"] == came % 2)
            if early and axis == "z":
                sent = sent & (came % 2 == self.spot["y"] % 2)
            pl.when(sent)(self.copies[p, stage, 1][d - 1].wait_recv)


HEAD_SLOTS = 7 + 2 * PARTS * (3 * 3 + 1)


class TableSum:
    def __init__(self, slots, table, parts, got):
        self.me = my_block()
        self.owner = owns(my_member())
        self.table, self.parts, self.got = table, parts, got
        self.shares, self.spread = [], []
        for d in range(1, BLOCKS):
            to = (self.me + d) % BLOCKS
            self.shares.append(send(parts.at[d - 1], got.at[d - 1], *slots.take(), block_id(to)))
        mine = table.at[pl.ds(0, ITEM), span(self.me * SLOTS, SLOTS)]
        for d in range(1, BLOCKS):
            to = (self.me + d) % BLOCKS
            self.spread.append(send(mine, mine, *slots.take(), block_id(to)))

    def fill(self, items, codes_ref, weights_ref, hot):
        for t in range(1, BLOCKS + 1):
            s = (self.me + t) % BLOCKS
            slot = t % 2
            for i in range(CHUNKS):
                cols = pl.ds(i * CHUNK, CHUNK)
                hot[slot, :, cols] = one_hot(codes_ref[pl.ds(s, 1), cols], weights_ref[pl.ds(s, 1), cols])
            got = nt(items[...], hot[slot])
            self.table[pl.ds(ITEM, STACK - ITEM), span(s * SLOTS, SLOTS)] = got[ITEM:].astype(BF)
            if t < BLOCKS:
                self.parts[t - 1] = got[:ITEM].astype(BF)
                pl.when(self.owner)(self.shares[t - 1].start)
            else:
                self.own = got[:ITEM]

    def add(self):
        total = self.own
        for d in range(1, BLOCKS):
            pl.when(self.owner)(self.shares[d - 1].wait)
            total = total + self.got[d - 1].astype(F32)
        self.table[pl.ds(0, ITEM), span(self.me * SLOTS, SLOTS)] = total.astype(BF)
        for copy in self.spread:
            pl.when(self.owner)(copy.start)

    def finish(self):
        for copy in self.spread:
            pl.when(self.owner)(copy.wait)


TABLE_SLOTS = 2 * (BLOCKS - 1)


class Halo:
    def __init__(self, slots, edges, came):
        me = my_block()
        down, up = block_id((me + BLOCKS - 1) % BLOCKS), block_id((me + 1) % BLOCKS)
        self.copies = [
            send(edges.at[0], came.at[1], *slots.take(), down),
            send(edges.at[1], came.at[0], *slots.take(), up),
        ]

    def start(self):
        for copy in self.copies:
            copy.start()

    def finish(self):
        for copy in self.copies:
            copy.wait()


HALO_SLOTS = 2


class Scatter:
    def __init__(self, slots_send, slots_recv, local, chunks, out):
        self.me = my_member()
        self.owner, self.head = owns(self.me), head_at(self.me)
        self.send_sem, self.recv_sem, self.local = slots_send, slots_recv, local
        self.chunks, self.out = chunks, out

    def copy(self, p):
        return send(
            self.chunks.at[p], self.out.at[self.head], self.send_sem.at[p], self.recv_sem.at[self.head], member_id(p)
        )

    def keep(self, p):
        return pltpu.make_async_copy(self.chunks.at[p], self.out.at[self.head], self.local)

    def start(self, p):
        pl.when(self.owner & (self.me != p))(lambda: self.copy(p).start())
        pl.when(self.owner & (self.me == p))(lambda: self.keep(p).start())

    def finish(self):
        for h in range(HEADS):
            at = owner_of(h)
            got = send(self.chunks.at[0], self.out.at[h], self.send_sem.at[0], self.recv_sem.at[h], member_id(at))
            pl.when(self.me != at)(got.wait_recv)
        for p in range(MEMBERS):
            pl.when(self.owner & (self.me != p))(self.copy(p).wait_send)
        pl.when(self.owner)(self.keep(self.me).wait)


class Gather:
    def __init__(self, slots_send, slots_recv, local, chunks, out):
        self.me = my_member()
        self.owner, self.head = owns(self.me), head_at(self.me)
        self.chunks, self.out, self.send_sem, self.recv_sem = chunks, out, slots_send, slots_recv
        self.keep = pltpu.make_async_copy(chunks.at[self.head], out.at[self.me], local)
        self.copies = []
        for d in range(1, MEMBERS):
            to = (self.me + d) % MEMBERS
            copy = send(chunks.at[head_at(to)], out.at[self.me], slots_send.at[d], slots_recv.at[self.me], member_id(to))
            self.copies.append((owns(to), copy))

    def start(self):
        for wanted, copy in self.copies:
            pl.when(wanted)(copy.start)
        self.keep.start()

    def finish(self):
        self.keep.wait()
        for d in range(1, MEMBERS):
            came = (self.me + d) % MEMBERS
            got = send(self.chunks.at[0], self.out.at[came], self.send_sem.at[0], self.recv_sem.at[came], member_id(came))
            pl.when(self.owner)(got.wait_recv)
        for wanted, copy in self.copies:
            pl.when(wanted)(copy.wait_send)


def block_peers():
    me = my_block()
    return [block_id((me + d) % BLOCKS) for d in range(1, BLOCKS)]


def member_peers():
    me = my_member()
    return [member_id((me + d) % MEMBERS) for d in range(1, MEMBERS)]


def iota(shape, dim):
    return lax.broadcasted_iota(I32, shape, dim)


def tap_row(conv_w, head, flip):
    mine = jnp.where(iota((HEADS, 65), 0) == head, conv_w[...], 0.0)
    row, col = iota((65, 256), 0), iota((65, 256), 1)
    place = jnp.where(col == (160 - row if flip else row + 96), 1.0, 0.0)
    return jnp.sum(nn(mine, place, precision=HIGHEST), axis=0, keepdims=True)


def head_column(vector, head):
    rows = jnp.broadcast_to(vector[...][None, :], (128, D))
    pick = jnp.where(iota((HEAD, D), 1) == iota((HEAD, D), 0) + head * HEAD, 1.0, 0.0)
    return nt(pick, rows, precision=HIGHEST)[:, 0:1]


def item_masks(cuts, block):
    start = block * BLOCK - EDGE
    pos = start + iota((1, EXT), 1)
    item = jnp.zeros((1, EXT), I32)
    for k in range(1, 4):
        item = item + jnp.where(pos >= cuts[k], 1, 0)
    longest = jnp.where(cuts[2] - cuts[1] > 1024, 1, 2)
    outer = jnp.where(block < 4, 0, 3)
    inner = jnp.where(block < 4, 1, 2)
    valid = jnp.where((pos >= 0) & (pos < TOTAL), 1.0, 0.0)
    is_long = jnp.where(item == longest, valid, 0.0)
    is_outer = jnp.where(item == outer, valid, 0.0)
    is_inner = jnp.where(item == inner, valid, 0.0) - jnp.where(inner == longest, is_long, 0.0)
    return jnp.concatenate([is_long, is_outer, is_inner, jnp.zeros((5, EXT), F32)], axis=0)


def pack(rows):
    return jnp.concatenate([rows[:SIDE], rows[SIDE:]], axis=1).astype(BF)


def unpack_heads(chunk):
    pairs = []
    for i in range(HEADS // 2):
        a, b = chunk(2 * i), chunk(2 * i + 1)
        top = jnp.concatenate([a[:, :HEAD], b[:, :HEAD]], axis=1)
        low = jnp.concatenate([a[:, HEAD:], b[:, HEAD:]], axis=1)
        pairs.append(jnp.concatenate([top, low], axis=0))
    return jnp.concatenate(pairs, axis=1)


def norm_forward(values):
    centred = values - jnp.mean(values, axis=-1, keepdims=True)
    recip = lax.rsqrt(jnp.mean(centred * centred, axis=-1, keepdims=True) + EPS_NORM)
    return centred * recip, recip


def norm_backward(grad, hat, recip, gain):
    scaled = grad * gain
    mean = jnp.mean(scaled, axis=-1, keepdims=True)
    along = jnp.mean(scaled * hat, axis=-1, keepdims=True)
    return recip * (scaled - mean - hat * along)


def column_sums(values):
    return jnp.sum(values, axis=0, keepdims=True)


LAYER_SEMS = (
    4 * MEMBERS + 1 + 7 + 6 + 2 * TABLE_SLOTS + 2 * HALO_SLOTS + BIG_SLOTS + HEAD_SLOTS + 2 * VEC_SLOTS
)


def flip_in(values, dest, start):
    dest[start : start + values.shape[1], :] = jnp.transpose(values.astype(F32)).astype(BF)


def layer_kernel(
    q_codes, k_codes, hyper, cuts, b_query, b_key, b_value, conv_w, b_out, ln1_gain, ln1_bias, b_in, b_back, ln2_gain,
    ln2_bias, all_tokens, all_cot, w_query, w_key, w_value, w_out, w_in, w_back,
    output, grad_tokens, sum_a, sum_b, vec_out, small_out, even, odd,
    tokens, cot, other_tok, qkv, weights, codes, planes, masks, table, estimate, scale, v_ext,
    codes_in, planes_in, parts, got, v_edges, v_came, att_out, att,
    grad_out, chunks_in, g_edges, g_came, g_parts, g_got, gtable, g_chunks, g_in, head_w, head_got, vec_buf, small_buf,
    resid, att_t, hidden_t, act_t, inner_g, outer_g, branch_g, att_s, hidden_s, act_s, inner_s, outer_s, branch_s,
    local, send_sem, recv_sem, *big_refs,
):
    spot = here()
    me, block, core = my_member(), my_block(), spot["c"]
    head, owner, mine = head_at(me), owns(me), me % 8
    far = {"zh": 1 - spot["zh"], "zl": 1 - spot["zl"]}
    hello(member_peers() + block_peers() + [far])

    def sixteen(k):
        at = pl.ds(k * MEMBERS, MEMBERS)
        return send_sem.at[at], recv_sem.at[at]

    slots = Slots(send_sem, recv_sem)
    slots.used = 4 * MEMBERS
    sibling = on_axis("c", 1 - core)
    swap = send(all_tokens, other_tok, *slots.take(), sibling)
    token_load = pltpu.make_async_copy(all_tokens, tokens, local.at[19])
    cot_load = pltpu.make_async_copy(all_cot, cot, local.at[20])
    token_load.start()
    cot_load.start()
    spread = []
    for d in range(1, 8):
        piece = planes_in.at[mine]
        spread.append(send(piece, piece, *slots.take(), member_id(core * 8 + (mine + d) % 8)))
    acts = []
    for source, dest in ((hidden_t, hidden_s), (act_t, act_s), (att_t, att_s)):
        half = source.shape[0] // 2
        acts.append(send(source.at[span((1 - core) * half, half, 16)], dest, *slots.take(), sibling))
    for source, dest in ((inner_g, inner_s), (outer_g, outer_s), (branch_g, branch_s)):
        acts.append(send(source, dest, *slots.take(), sibling))
    sum_table = TableSum(slots, table, parts, got)
    sum_grads = TableSum(slots, gtable, g_parts, g_got)
    v_halo = Halo(slots, v_edges, v_came)
    g_halo = Halo(slots, g_edges, g_came)
    att_rows = Scatter(*sixteen(1), local.at[4], att_out, att)
    give_grad = Gather(*sixteen(2), local.at[8], grad_out, chunks_in)
    grad_rows = Scatter(*sixteen(3), local.at[9], g_chunks, g_in)
    heads = HeadSum(spot, slots, head_w, head_got, even, odd)
    vector = VectorSum(spot, slots, None, vec_buf)
    small = VectorSum(spot, slots, None, small_buf)
    v_bias = head_column(b_value, head)

    def front(w_all, w_t, items, hot, big_hot, conv, codes_out):
        loads = [
            pltpu.make_async_copy(w, w_all.at[k], local.at[k]) for k, w in enumerate((w_query, w_key, w_value))
        ]
        for load in loads:
            load.start()
        for h in range(HEADS):
            codes_out[h, 0:1, :] = q_codes[h]
            codes_out[h, 1:2, :] = k_codes[h]
        planes_in[mine] = hyper[0]
        masks[...] = item_masks(cuts, block)
        give = Gather(*sixteen(0), local.at[3], codes_out, codes_in)
        all_here(MEMBERS - 1 + BLOCKS - 1 + 1)

        give.start()
        swap.start()
        for copy in spread:
            copy.start()

        pick = jnp.where(iota((HEAD, D), 1) == iota((HEAD, D), 0) + head * HEAD, 1.0, 0.0).astype(BF)
        bias = jnp.concatenate([head_column(b_query, head), head_column(b_key, head), jnp.zeros((HEAD, 1), F32)], axis=0)
        for k, load in enumerate(loads):
            load.wait()
            w_t[k * HEAD : (k + 1) * HEAD, :] = nt(pick, w_all[k]).astype(BF)

        def project(source, start):
            def step(i, _):
                rows = span(i * CHUNK, CHUNK)
                qkv[:, span(start + i * CHUNK, CHUNK)] = nt(w_t[...], source[rows, :]) + bias
                return 0

            lax.fori_loop(0, ROWS // CHUNK, step, 0)

        token_load.wait()
        project(tokens, core * ROWS)
        swap.wait()
        project(other_tok, (1 - core) * ROWS)
        v_edges[0] = qkv[2 * HEAD :, :EDGE].astype(BF)
        v_edges[1] = qkv[2 * HEAD :, BLOCK - EDGE :].astype(BF)
        v_halo.start()

        give.finish()
        for copy in spread:
            copy.wait()
        for b in range(BITS):
            planes[b * SETS : (b + 1) * SETS, :] = planes_in[:, b, :]
        for side in range(2):
            for s in range(SETS):
                for k in range(2):
                    codes[side, s : s + 1, k * ROWS : (k + 1) * ROWS] = codes_in[k * 8 + s, side : side + 1, :]

        def prepare(i, _):
            cols = span(i * CHUNK, CHUNK)
            inner = span(i * CHUNK + EDGE, CHUNK)
            weights[SETS:, cols] = hash_weight(qkv[HEAD : 2 * HEAD, cols], codes[1, :, cols], planes[...])
            items[:, cols] = by_item(qkv[2 * HEAD :, cols], jnp.ones((1, CHUNK), F32), masks[:, inner])
            return 0

        lax.fori_loop(0, CHUNKS, prepare, 0)
        sum_table.fill(items, codes.at[1], weights.at[pl.ds(SETS, SETS)], hot)

        def query_side(i, _):
            cols = span(i * CHUNK, CHUNK)
            inner = span(i * CHUNK + EDGE, CHUNK)
            weights[:SETS, cols] = hash_weight(qkv[:HEAD, cols], codes[0, :, cols], planes[...])
            v_ext[:, inner] = by_item(qkv[2 * HEAD :, cols] + v_bias, jnp.zeros((1, CHUNK), F32), masks[:, inner])
            return 0

        lax.fori_loop(0, CHUNKS, query_side, 0)
        sum_table.add()
        v_halo.finish()
        none = jnp.zeros((1, EDGE), F32)
        v_ext[:, :EDGE] = by_item(v_came[0].astype(F32) + v_bias, none, masks[:, :EDGE])
        v_ext[:, EDGE + BLOCK :] = by_item(v_came[1].astype(F32) + v_bias, none, masks[:, EDGE + BLOCK :])
        lower, upper = circulant(tap_row(conv_w, head, True))

        def convolve(i, _):
            at = i * 256
            mixed = nn(v_ext[:, span(at, 256)], lower) + nn(v_ext[:, span(at + 256, 256)], upper)
            conv[:, span(at, 256)] = pick_item(mixed, masks[:, span(at + EDGE, 256)])[:HEAD] + v_bias
            return 0

        lax.fori_loop(0, BLOCK // 256, convolve, 0)
        sum_table.finish()

        def read(i, _):
            i = (i + me) % CHUNKS
            cols = span(i * CHUNK, CHUNK)
            own = masks[:, span(i * CHUNK + EDGE, CHUNK)]
            for s in range(SETS):
                big_hot[s * SLOTS : (s + 1) * SLOTS, :] = one_hot(codes[0, s : s + 1, cols], weights[s : s + 1, cols])
            found = pick_item(nn(table[...], big_hot[...]), own)
            recip = 1.0 / (found[HEAD : HEAD + 1] + 1.0)
            est = (found[:HEAD] - v_bias) * recip
            estimate[:, cols] = est
            scale[:, cols] = recip
            rows = jnp.transpose(est + conv[:, cols])
            for u in range(PER_CHUNK):
                p = i * PER_CHUNK + u
                att_out[p] = pack(rows[u * OWN : (u + 1) * OWN])
                att_rows.start(p)
            return 0

        lax.fori_loop(0, CHUNKS, read, 0)

    def feed_forward(w_out_v, w_in_v, w_back_v, slope_v):
        loads = [
            pltpu.make_async_copy(a, b, local.at[5 + k])
            for k, (a, b) in enumerate([(w_out, w_out_v), (w_in, w_in_v), (w_back, w_back_v)])
        ]
        for load in loads:
            load.start()
        att_rows.finish()
        gain1, gain2 = ln1_gain[...][None, :], ln2_gain[...][None, :]
        attended = unpack_heads(lambda h: att[h])
        flip_in(attended, att_t, 0)
        acts[2].start()
        loads[0].wait()
        branch = nn(attended, w_out_v[...]) + b_out[...][None, :]
        hat1, recip1 = norm_forward(tokens[span(mine * OWN, OWN, 16), :].astype(F32) + branch)
        hidden = hat1 * gain1 + ln1_bias[...][None, :]
        hidden_low = hidden.astype(BF)
        flip_in(hidden, hidden_t, 0)
        acts[0].start()
        loads[1].wait()
        outer = b_back[...][None, :]
        for k in range(FF // D):
            cols = slice(k * D, (k + 1) * D)
            inner = nn(hidden_low, w_in_v[:, cols]) + b_in[pl.ds(k * D, D)][None, :]
            phi = 0.5 * (1.0 + lax.erf(inner * (2.0**-0.5)))
            slope_v[:, cols] = phi + inner * (jnp.exp(-0.5 * inner * inner) * 0.3989422804014327)
            act = (inner * phi).astype(BF)
            flip_in(act, act_t, k * D)
            if k == 0:
                loads[2].wait()
            outer = outer + nn(act, w_back_v[cols, :])
        acts[1].start()
        hat2, recip2 = norm_forward(hidden + outer)
        output[...] = hat2 * gain2 + ln2_bias[...][None, :]
        cot_load.wait()
        got = cot[...]
        sum_grad = norm_backward(got, hat2, recip2, gain2)
        outer_grad = sum_grad.astype(BF)
        outer_g[...] = outer_grad
        acts[4].start()
        hidden_grad = sum_grad
        sums = [column_sums(outer_grad.astype(F32)), column_sums(got * hat2), column_sums(got)]
        bias_rows = []
        for k in range(FF // D):
            cols = slice(k * D, (k + 1) * D)
            act_grad = nt(outer_grad, w_back_v[cols, :])
            inner_grad = (act_grad * slope_v[:, cols]).astype(BF)
            inner_g[:, cols] = inner_grad
            bias_rows.append(column_sums(inner_grad.astype(F32)))
            hidden_grad = hidden_grad + nt(inner_grad, w_in_v[:, cols])
        acts[3].start()
        grad1 = norm_backward(hidden_grad, hat1, recip1, gain1)
        resid[...] = grad1
        branch_grad = grad1.astype(BF)
        branch_g[...] = branch_grad
        att_grad = nt(branch_grad, w_out_v[...])
        for h in range(HEADS):
            grad_out[h] = pack(att_grad[:, h * HEAD : (h + 1) * HEAD])
        give_grad.start()
        acts[5].start()
        rows = [column_sums(branch_grad.astype(F32)), column_sums(hidden_grad * hat1), column_sums(hidden_grad)]
        vector.value = jnp.concatenate(rows + sums + bias_rows + [jnp.zeros((6, D), F32)], axis=0)
        vector.start(0)

    def backward(w_all, grad, den, items, hot, ext, rows_ref, g_all, mix, *accs):
        per = len(big_refs) // 2
        mats = [
            Matrix(*MATRICES[t], refs=(result, accs[t], *big_refs[t * per : (t + 1) * per]))
            for t, result in enumerate((sum_a, sum_b))
        ]
        into = BigSum(spot, slots, local.at[pl.ds(10, 3)], mats[:1])
        outof = BigSum(spot, slots, local.at[pl.ds(13, 3)], mats[1:])
        loads = [
            pltpu.make_async_copy(w, w_all.at[k], local.at[16 + k]) for k, w in enumerate((w_query, w_key, w_value))
        ]
        for load in loads:
            load.start()
        every_part = range(PARTS)

        def weight_into(a):
            m = mats[0]
            rows = span(core * m.half, m.half, 16)
            start, stop = a * m.part, min((a + 1) * m.part, FF)
            total = nn(hidden_t[rows, :], inner_g[:, start:stop]) + nn(hidden_s[...], inner_s[:, start:stop])
            m.acc[:, start:stop] = total.astype(BF)
            if stop == FF:
                total = nn(att_t[rows, :], branch_g[...]) + nn(att_s[...], branch_s[...])
                m.acc[:, FF:] = total.astype(BF)

        def weight_outof(a):
            m = mats[1]
            lanes = slice(a * m.part, (a + 1) * m.part)
            rows = span(core * m.half, m.half, 16)
            total = nn(act_t[rows, :], outer_g[:, lanes]) + nn(act_s[...], outer_s[:, lanes])
            m.acc[:, lanes] = total.astype(BF)

        def step(sums, name):
            for a in every_part:
                getattr(sums, name)(a)

        for copy in acts:
            copy.wait()
        for a in every_part:
            weight_outof(a)
            outof.begin(a)
        for a in every_part:
            weight_into(a)
            into.begin(a)

        give_grad.finish()
        for p in range(MEMBERS):
            both = chunks_in[p].astype(F32)
            rows_ref[p * OWN : p * OWN + SIDE] = both[:, :HEAD]
            rows_ref[p * OWN + SIDE : (p + 1) * OWN] = both[:, HEAD:]

        def prepare(i, _):
            cols = span(i * CHUNK, CHUNK)
            own = masks[:, span(i * CHUNK + EDGE, CHUNK)]
            this = jnp.transpose(rows_ref[span(i * CHUNK, CHUNK), :])
            grad[:, cols] = this
            numer = this * scale[:, cols]
            mass = -jnp.sum(numer * estimate[:, cols], axis=0, keepdims=True)
            den[:, cols] = mass
            items[:, cols] = by_item(numer, mass, own)
            ext[:, span(i * CHUNK + EDGE, CHUNK)] = by_item(this, jnp.zeros((1, CHUNK), F32), own)
            return 0

        lax.fori_loop(0, CHUNKS, prepare, 0)
        g_edges[0] = grad[:, :EDGE].astype(BF)
        g_edges[1] = grad[:, BLOCK - EDGE :].astype(BF)
        g_halo.start()
        sum_grads.fill(items, codes.at[0], weights.at[pl.ds(0, SETS)], hot)
        step(outof, "near")
        step(into, "near")

        def query_back(i, _):
            cols = span(i * CHUNK, CHUNK)
            own = masks[:, span(i * CHUNK + EDGE, CHUNK)]
            q_codes = codes[0, :, cols]
            numer = grad[:, cols] * scale[:, cols]
            mass = den[:, cols]
            found_all = []
            for s in range(SETS):
                one = one_hot(q_codes[s : s + 1], 1.0)
                found = pick_item(nn(table[:, s * SLOTS : (s + 1) * SLOTS], one), own)
                found_all.append(
                    jnp.sum(found[:HEAD] * numer, axis=0, keepdims=True) + found[HEAD : HEAD + 1] * mass
                )
            z_grad = jnp.concatenate(found_all, axis=0) * weights[:SETS, cols]
            g_all[:HEAD, cols] = hash_back(z_grad, qkv[:HEAD, cols], q_codes, planes[...]).astype(BF)
            return 0

        lax.fori_loop(0, 2, query_back, 0)
        sum_grads.add()
        step(outof, "relay")
        step(into, "relay")
        vector.finish(0)
        vector.start(1)
        lax.fori_loop(2, CHUNKS, query_back, 0)

        g_halo.finish()
        none = jnp.zeros((1, EDGE), F32)
        ext[:, :EDGE] = by_item(g_came[0].astype(F32), none, masks[:, :EDGE])
        ext[:, EDGE + BLOCK :] = by_item(g_came[1].astype(F32), none, masks[:, EDGE + BLOCK :])
        lower, upper = circulant(tap_row(conv_w, head, False))

        def conv_back(i, carry):
            at = i * 256
            mixed = nn(ext[:, span(at, 256)], lower) + nn(ext[:, span(at + 256, 256)], upper)
            mix[:, span(at, 256)] = pick_item(mixed, masks[:, span(at + EDGE, 256)])[:HEAD]
            this = ext[:, span(at + EDGE, 256)]
            return carry[0] + tn(v_ext[:, span(at, 256)], this), carry[1] + tn(v_ext[:, span(at + 256, 256)], this)

        zeros = jnp.zeros((256, 256), F32)
        c_low, c_high = lax.fori_loop(0, BLOCK // 256, conv_back, (zeros, zeros))
        row, col = iota((256, 256), 0), iota((256, 256), 1)
        skew = jnp.where(col < row, c_low, c_high)
        for b in range(8):
            skew = jnp.where(jnp.bitwise_and(row, 1 << b) != 0, pltpu.roll(skew, 256 - (1 << b), 1), skew)
        taps_grad = jnp.sum(skew, axis=0, keepdims=True)
        step(outof, "second")
        step(into, "second")
        vector.finish(1)
        vector.start(2)
        sum_grads.finish()

        def key_back(i, _):
            i = (i + me) % CHUNKS
            cols = span(i * CHUNK, CHUNK)
            own = masks[:, span(i * CHUNK + EDGE, CHUNK)]
            k_codes = codes[1, :, cols]
            k_w = weights[SETS:, cols]
            val = qkv[2 * HEAD :, cols]
            found_all = []
            v_grad = mix[:, cols]
            for s in range(SETS):
                one = one_hot(k_codes[s : s + 1], 1.0)
                found = pick_item(nn(gtable[:, s * SLOTS : (s + 1) * SLOTS], one), own)
                found_all.append(
                    jnp.sum(found[:HEAD] * val, axis=0, keepdims=True) + found[HEAD : HEAD + 1]
                )
                v_grad = v_grad + found[:HEAD] * k_w[s : s + 1]
            z_grad = jnp.concatenate(found_all, axis=0) * k_w
            k_grad = hash_back(z_grad, qkv[HEAD : 2 * HEAD, cols], k_codes, planes[...])
            g_all[HEAD : 2 * HEAD, cols] = k_grad.astype(BF)
            g_all[2 * HEAD : 3 * HEAD, cols] = v_grad.astype(BF)
            for k in range(3):
                rows = jnp.transpose(g_all[k * HEAD : (k + 1) * HEAD, cols].astype(F32))
                for u in range(PER_CHUNK):
                    g_chunks[i * PER_CHUNK + u, k] = pack(rows[u * OWN : (u + 1) * OWN])
            for u in range(PER_CHUNK):
                grad_rows.start(i * PER_CHUNK + u)
            return 0

        lax.fori_loop(0, 1, key_back, 0)
        lax.fori_loop(1, 3, key_back, 0)
        step(outof, "third")
        step(into, "third")
        vector.finish(2)
        vector.start(3)
        lax.fori_loop(3, CHUNKS, key_back, 0)

        g_all[3 * HEAD :, :] = jnp.zeros((HEAD, BLOCK), BF)
        own_part = g_all[: 3 * HEAD, span(core * ROWS, ROWS)]
        away = g_all[: 3 * HEAD, span((1 - core) * ROWS, ROWS)]
        w_grad = jnp.transpose(nn(own_part, tokens[...]) + nn(away, other_tok[...]))
        head_w[:D] = w_grad[:, : 2 * HEAD].astype(BF)
        head_w[D:] = jnp.concatenate([w_grad[: D // 2, 2 * HEAD :], w_grad[D // 2 :, 2 * HEAD :]], axis=1).astype(BF)
        heads.start_sum()
        biases = nt(jnp.ones((8, BLOCK), BF), g_all[...])[0:1]
        own_row = (iota((16, SMALL), 0) == head) & owner
        small.value = jnp.where(own_row, jnp.concatenate([biases, taps_grad], axis=1), 0.0)
        small.start(0)
        vector.finish(3)
        vector.start(4)
        step(outof, "back")
        step(into, "back")
        small.finish(0)
        small.start(1)
        heads.finish_sum()
        for p in every_part:
            heads.start(p, 0)
        step(outof, "ring")
        step(into, "ring")
        grad_rows.finish()
        total = resid[...]
        for k in range(3):
            loads[k].wait()
            total = total + nt(unpack_heads(lambda h, k=k: g_in[h, k]), w_all[k])
        grad_tokens[...] = total
        for p in every_part:
            heads.finish(p, 0)
            heads.start(p, 1)
        small.finish(1)
        small.start(2)
        step(outof, "pass_on")
        for p in every_part:
            heads.finish(p, 1)
            heads.start(p, 2)
        step(into, "pass_on")
        small.finish(2)
        small.start(3)
        step(outof, "core")
        for p in every_part:
            heads.finish(p, 2)
            heads.start(p, 3)
        step(into, "core")
        small.finish(3)
        small.start(4)
        vector.finish(4)
        vec_out[...] = vector.value
        for p in every_part:
            heads.finish(p, 3)
        small.finish(4)
        small_out[...] = small.value
        step(outof, "finish")
        step(into, "finish")

    pl.run_scoped(
        front, vmem(3, D, D), vmem(3 * HEAD, D), vmem(STACK, BLOCK), vmem(2, SLOTS, BLOCK), vmem(TABLE, CHUNK),
        vmem(HEAD, BLOCK, kind=F32), vmem(HEADS, 2, ROWS, kind=I32),
    )
    pl.run_scoped(feed_forward, vmem(D, D), vmem(D, FF), vmem(FF, D), vmem(OWN, FF, kind=F32))
    pl.run_scoped(
        backward, vmem(3, D, D), vmem(HEAD, BLOCK, kind=F32), vmem(1, BLOCK, kind=F32), vmem(STACK, BLOCK),
        vmem(2, SLOTS, BLOCK), vmem(STACK, EXT), vmem(BLOCK, HEAD, kind=F32), vmem(4 * HEAD, BLOCK),
        vmem(HEAD, BLOCK, kind=F32), *[Matrix(*m).whole() for m in MATRICES],
    )


PIECES = 8


def last_kernel(
    sum_a, sum_b, even, odd, vec, small, layer_out, tok_grad,
    output, grad_tokens, g_wq, g_bq, g_wk, g_bk, g_wv, g_bv, g_conv, g_wo, g_bo, g_l1g, g_l1b, g_wi, g_bi, g_wb, g_bb, g_l2g,
    g_l2b,
    a_in, b_in, a_out, b_out, qkv_out, in_sems, out_sems,
):
    a_rows, b_rows = D // PIECES, FF // PIECES
    loads = []
    for k in range(PIECES):
        rows = pl.ds(k * a_rows, a_rows)
        loads.append(pltpu.make_async_copy(sum_a.at[rows], a_in.at[rows], in_sems.at[2 * k]))
        rows = pl.ds(k * b_rows, b_rows)
        loads.append(pltpu.make_async_copy(sum_b.at[rows], b_in.at[rows], in_sems.at[2 * k + 1]))
    for load in loads:
        load.start()
    writes = []

    def write(source, dest):
        copy = pltpu.make_async_copy(source, dest, out_sems.at[len(writes)])
        copy.start()
        writes.append(copy)

    left = iota((SHARE, 128), 1) < HEAD

    def pieces(pair, j):
        zh, x = j // 4, j % 4
        if pair < 4:
            return even[zh, 0, x, pair].astype(F32), even[zh, 1, x, pair].astype(F32)
        return odd[zh, x, 0, pair - 4].astype(F32), odd[zh, x, 1, pair - 4].astype(F32)

    for pair in range(HEADS // 2):
        lanes = pl.ds(pair * 128, 128)
        for j in range(BLOCKS):
            a, b = pieces(pair, j)
            first = jnp.where(left, a, pltpu.roll(b, HEAD, 1))
            second = jnp.where(left, pltpu.roll(a, HEAD, 1), b)
            low, high = j * SHARE, (j + 1) * SHARE
            cut = min(max(D - low, 0), SHARE)
            if cut > 0:
                qkv_out[0, low : low + cut, lanes] = first[:cut]
                qkv_out[1, low : low + cut, lanes] = second[:cut]
            if cut < SHARE:
                start, stop = low + cut - D, high - D
                qkv_out[2, start:stop, lanes] = first[cut:]
                qkv_out[2, D // 2 + start : D // 2 + stop, lanes] = second[cut:]
    for k, dest in enumerate((g_wq, g_wk, g_wv)):
        write(qkv_out.at[k], dest)
    for k in range(PIECES):
        rows = pl.ds(k * a_rows, a_rows)
        loads[2 * k].wait()
        a_out[rows, :] = a_in[rows, :].astype(F32)
        write(a_out.at[rows, pl.ds(0, FF)], g_wi.at[rows])
        write(a_out.at[rows, pl.ds(FF, D)], g_wo.at[rows])
        rows = pl.ds(k * b_rows, b_rows)
        loads[2 * k + 1].wait()
        b_out[rows, :] = b_in[rows, :].astype(F32)
        write(b_out.at[rows], g_wb.at[rows])
    output[...] = layer_out[...]
    grad_tokens[...] = tok_grad[...]
    for k, dest in enumerate((g_bo, g_l1g, g_l1b, g_bb, g_l2g, g_l2b)):
        dest[...] = vec[k, :]
    for k in range(FF // D):
        g_bi[pl.ds(k * D, D)] = vec[6 + k, :]
    for k, dest in enumerate((g_bq, g_bk, g_bv)):
        for pair in range(HEADS // 2):
            lanes = slice(k * HEAD, (k + 1) * HEAD)
            dest[pl.ds(pair * 128, 128)] = jnp.concatenate(
                [small[2 * pair : 2 * pair + 1, lanes], small[2 * pair + 1 : 2 * pair + 2, lanes]], axis=1
            )[0]
    row, col = iota((256, 128), 0), iota((256, 128), 1)
    flip = jnp.where(row == 160 - col, 1.0, 0.0)
    g_conv[...] = nn(small[:, 256:], flip, precision=HIGHEST)[:HEADS, :65]
    for copy in writes:
        copy.wait()


VMEM_SPEC = pl.BlockSpec(memory_space=pltpu.VMEM)
ANY_SPEC = pl.BlockSpec(memory_space=pl.ANY)
SMEM_SPEC = pl.BlockSpec(memory_space=pltpu.SMEM)


def call(kernel, outs, scratch, *args, ident=None, far=(), far_outs=(), scalars=()):
    params = {} if ident is None else {"collective_id": ident, "has_side_effects": True}
    specs = [ANY_SPEC if k in far else SMEM_SPEC if k in scalars else VMEM_SPEC for k in range(len(args))]
    return pl.pallas_call(
        kernel,
        out_shape=[jax.ShapeDtypeStruct(shape, kind) for shape, kind in outs],
        in_specs=specs,
        out_specs=[ANY_SPEC if k in far_outs else VMEM_SPEC for k in range(len(outs))],
        scratch_shapes=scratch,
        compiler_params=pltpu.CompilerParams(vmem_limit_bytes=VMEM_LIMIT, **params),
    )(*args)


def per_device(
    tokens, item_cuts, q_codes, k_codes, hyperplanes, w_query, b_query, w_key, b_key,
    w_value, b_value, conv_weight, w_out, b_out, ln1_gain, ln1_bias, w_in, b_in, w_back,
    b_back, ln2_gain, ln2_bias, cotangent,
):
    chunk = (SIDE, 128)
    layer_out, tok_grad, sum_a, sum_b, vec_sum, small_sum, even, odd = call(
        layer_kernel,
        [
            ((OWN, D), F32), ((OWN, D), F32), ((D, WIDE), BF), ((FF, D), BF), ((16, D), F32), ((16, SMALL), F32),
            ((2, 2, 4, 4, SHARE, 128), BF), ((2, 4, 2, 2, SHARE, 128), BF),
        ],
        [
            vmem(ROWS, D), vmem(OWN, D, kind=F32), vmem(ROWS, D), vmem(3 * HEAD, BLOCK, kind=F32), vmem(2 * SETS, BLOCK, kind=F32),
            vmem(2, SETS, BLOCK, kind=I32), vmem(BITS * SETS, HEAD, kind=F32), vmem(8, EXT, kind=F32),
            vmem(STACK, TABLE), vmem(HEAD, BLOCK, kind=F32), vmem(1, BLOCK, kind=F32), vmem(STACK, EXT),
            vmem(MEMBERS, 2, ROWS, kind=I32), vmem(SETS, BITS, HEAD, kind=F32), vmem(BLOCKS - 1, ITEM, SLOTS),
            vmem(BLOCKS - 1, ITEM, SLOTS), vmem(2, HEAD, EDGE), vmem(2, HEAD, EDGE), vmem(MEMBERS, *chunk),
            vmem(HEADS, *chunk),
            vmem(HEADS, *chunk), vmem(MEMBERS, *chunk), vmem(2, HEAD, EDGE), vmem(2, HEAD, EDGE),
            vmem(BLOCKS - 1, ITEM, SLOTS), vmem(BLOCKS - 1, ITEM, SLOTS), vmem(STACK, TABLE),
            vmem(MEMBERS, 3, *chunk), vmem(HEADS, 3, *chunk), vmem(HEAD_ROWS, 128), vmem(BLOCKS - 1, SHARE, 128),
            vmem(5, 4, 8, D, kind=F32), vmem(5, 4, 8, SMALL, kind=F32),
            vmem(OWN, D, kind=F32), vmem(D, OWN), vmem(D, OWN), vmem(FF, OWN), vmem(OWN, FF), vmem(OWN, D),
            vmem(OWN, D), vmem(D // 2, OWN), vmem(D // 2, OWN), vmem(FF // 2, OWN), vmem(OWN, FF), vmem(OWN, D),
            vmem(OWN, D), dma(21), dma(LAYER_SEMS), dma(LAYER_SEMS),
        ]
        + Matrix(*MATRICES[0]).scratch()
        + Matrix(*MATRICES[1]).scratch(),
        q_codes.transpose(1, 0, 2), k_codes.transpose(1, 0, 2), hyperplanes.transpose(0, 2, 1), item_cuts, b_query,
        b_key, b_value, conv_weight, b_out, ln1_gain, ln1_bias, b_in, b_back, ln2_gain, ln2_bias, tokens, cotangent,
        w_query, w_key, w_value, w_out, w_in, w_back,
        ident=0, far=(15, 16, 17, 18, 19, 20, 21, 22), far_outs=(2, 3), scalars=(3,),
    )
    square, line = ((D, D), F32), ((D,), F32)
    return call(
        last_kernel,
        [
            ((OWN, D), F32), ((OWN, D), F32), square, line, square, line, square, line, ((HEADS, 65), F32), square, line, line, line,
            ((D, FF), F32), ((FF,), F32), ((FF, D), F32), line, line, line,
        ],
        [
            vmem(D, WIDE), vmem(FF, D), vmem(D, WIDE, kind=F32), vmem(FF, D, kind=F32), vmem(3, D, D, kind=F32),
            dma(2 * PIECES), dma(3 + 3 * PIECES),
        ],
        sum_a, sum_b, even, odd, vec_sum, small_sum, layer_out, tok_grad,
        far=(0, 1), far_outs=(2, 4, 6, 9, 13, 15),
    )


def solution(mesh):
    grid = Mesh(mesh.devices.reshape(2, 4, 2, 4, 2), ALL_AXES)
    rows = ("zh", "x", "c")
    sets = ("y", "zl")
    placed = (
        P(rows, None), P(), P(sets, None, rows), P(sets, None, rows), P(sets, None, None),
    ) + (P(),) * 17 + (P(ALL_AXES, None),)
    return jax.shard_map(
        per_device,
        mesh=grid,
        in_specs=placed,
        out_specs=(P(ALL_AXES, None), P(ALL_AXES, None)) + (P(),) * 17,
        check_vma=False,
    )
```
